256 devices in a mesh: dp: 16 (over z_lo, x, core), ctx: 16 (over z_hi, y).
Axes of the slice: x: 4, y: 4, z: 8 (z_hi: 4, z_lo: 2; z = z_hi * 2 + z_lo), core: 2. Of those that a mesh axis runs over, the one named last changes fastest.
Arguments:
- hidden_rows: bfloat16 [32768, 4096], P(('dp', 'ctx')), may hold values from -6 to 6
- query_rows: bfloat16 [32768, 2048], P(('dp', 'ctx')), may hold values from -17 to 17
- out_grad: bfloat16 [32768, 2048], P(('dp', 'ctx')), may hold values from -6 to 6
- projection: bfloat16 [1024, 4096], replicated, may hold values from -0.09375 to 0.09375
- packing_plan: int32 [256, 128], P(('dp', 'ctx')), may hold values from 0 to 127, each once within a row
- document_ids: int32 [16, 2048], P('dp'), may hold values from 0 to 7, never falling along the last dimension, each value on 1 to 1536 neighbouring positions
Outputs:
- attended: bfloat16 [32768, 2048], P(('dp', 'ctx'))
- query_grad: bfloat16 [32768, 2048], P(('dp', 'ctx'))
- hidden_grad: bfloat16 [32768, 4096], P(('dp', 'ctx'))
- weight_grad: float32 [1024, 4096], P('dp', 'ctx')
The draws below stay inside these ranges and needn't reach their ends.
Inputs may be any that keep to these rules, and one draw needn't show every extreme that they name: `packing_plan`: each row holds every value once, so each device sends exactly 8 rows to each packed sequence. `document_ids`: never falling along a sequence; a document spans at most 1536 positions, and some document exactly that many.
All inputs are finite; a program needn't handle non-finite values.
Results may differ from the reference program's by a relative error of at most 0.017.
The reference program's roundings to bfloat16 on the way (of `rounded`, `grad_score` and `projected_grad`) count: a program that leaves them out, or rounds other values in their place, can miss the bound.
Values may be sent and summed in bfloat16 or wider, within the bound.
A program may use at most 64 MiB of HBM per device.

```python
import math
import jax
import jax.numpy as jnp
import numpy as np
from jax import lax

D = 4096
HEADS = 16
KV_HEADS = 4
HEAD_DIM = 128
S_DEV = 128
DOCS = 8
SEQS = 16
SPLIT = 16
SEQ_LEN = 2048
TOKENS = 32768
SEND = 8
KV_WIDTH = 1024


def draw_query_rows(key, part):
    array_shape = (TOKENS, HEADS * HEAD_DIM)
    normal = jax.random.normal(jax.random.fold_in(key, 23), array_shape, jnp.float32)
    return (jnp.clip(normal, -6.0, 6.0) * 2.0).astype(jnp.bfloat16)


def block_levels(own_key, extent, cuts, low, top_value):
    loudness, own = 1.0, jax.random.fold_in(own_key, 6)
    for position, shards_of in cuts:
        steps = jnp.exp(jax.random.uniform(jax.random.fold_in(own, position), (shards_of,), jnp.float32, low / len(cuts), top_value / len(cuts)))
        loudness = loudness * jnp.repeat(steps, extent[position] // shards_of).reshape([-1 if axis == position else 1 for axis in range(len(extent))])
    return loudness


def profile(count, total, limit, lean):
    weights = [(1 << 20) // math.isqrt(standing ** lean) + 1 for standing in range(2, count + 1)]
    rest, counts = total - limit - (count - 1), [1] * (count - 1)
    while rest > 0:
        free = [i for i in range(count - 1) if counts[i] < limit]
        mass, budget = sum([weights[i] for i in free]), rest
        for i in free:
            addition = min(limit - counts[i], max(1, budget * weights[i] // mass), rest)
            counts[i] = counts[i] + addition
            rest = rest - addition
    return np.array([limit] + counts)


def ragged(key, number_of, total, most, slope):
    if number_of == 2:
        one = jax.random.randint(key, (), max(1, total - most), min(most, total - 1) + 1)
        return jnp.stack([one, total - one])
    tallies = jnp.asarray(profile(number_of, total, most, slope), jnp.int32)
    twos = (number_of - 1) // 2
    giver, sink = tallies[1:1 + 2 * twos:2], tallies[2:2 + 2 * twos:2]
    slack = jnp.minimum(giver - 1, most - sink)
    passed = jax.random.randint(jax.random.fold_in(key, 1), (twos,), 0, 1 << 20) % (slack + 1)
    tallies = tallies.at[1:1 + 2 * twos:2].set(giver - passed).at[2:2 + 2 * twos:2].set(sink + passed)
    return tallies[jax.random.permutation(jax.random.fold_in(key, 2), number_of)]


def scatter_about(stream_key, shape, scale, reach, split=(), held_as=jnp.bfloat16):
    array = scale * jax.random.normal(stream_key, shape, jnp.float32)
    if split:
        array = array * block_levels(stream_key, shape, split, -0.22, 0.18)
    return jnp.clip(array, -reach, reach).astype(held_as)


def setup_inputs(seed: int = 0) -> dict:
    keys = jax.random.split(jax.random.key(seed), 7)
    hidden_rows = scatter_about(keys[0], (TOKENS, D), 1.0, 6.0, ((0, 256),))
    query_rows = draw_query_rows(jax.random.fold_in(keys[6], 71), 0)
    out_grad = scatter_about(keys[2], (TOKENS, HEADS * HEAD_DIM), 1.0, 6.0, ((0, 256),))
    projection = scatter_about(keys[3], (KV_WIDTH, D), D ** -0.5, 0.09375)
    packing_plan = jax.vmap(lambda own: jax.random.permutation(own, S_DEV))(jax.random.split(keys[4], (SEQS * SPLIT))).reshape((SEQS * SPLIT, S_DEV)).astype(jnp.int32)
    document_ids = jax.vmap(lambda own: jnp.searchsorted(jnp.cumsum(ragged(own, DOCS, SEQ_LEN, SEQ_LEN * 3 // 4, 2)), jnp.arange(SEQ_LEN), side="right"))(jax.random.split(keys[5], SEQS)).reshape((SEQS, SEQ_LEN)).astype(jnp.int32)
    return dict(hidden_rows=hidden_rows, query_rows=query_rows, out_grad=out_grad, projection=projection, packing_plan=packing_plan, document_ids=document_ids)


ROPE_BASE = 500000.0
MASK_VALUE = -1e30


def rotary_tables(positions, head_width):
    half_width = head_width // 2
    exponent = jnp.arange(half_width, dtype=jnp.float32) * (-2.0 * math.log(ROPE_BASE) / head_width)
    angles = positions.astype(jnp.float32)[:, None] * jnp.exp(exponent)[None, :]
    return jnp.cos(angles), jnp.sin(angles)


def rotate_forward(head_rows, cosine_table, sine_table):
    half_width = head_rows.shape[-1] // 2
    first_half = head_rows[..., :half_width]
    second_half = head_rows[..., half_width:]
    cosine_part = cosine_table[:, None, :]
    sine_part = sine_table[:, None, :]
    return jnp.concatenate([first_half * cosine_part - second_half * sine_part, second_half * cosine_part + first_half * sine_part], axis=-1)


def rotate_adjoint(head_grads, cosine_table, sine_table):
    half_width = head_grads.shape[-1] // 2
    first_half = head_grads[..., :half_width]
    second_half = head_grads[..., half_width:]
    cosine_part = cosine_table[:, None, :]
    sine_part = sine_table[:, None, :]
    return jnp.concatenate([first_half * cosine_part + second_half * sine_part, second_half * cosine_part - first_half * sine_part], axis=-1)


def inner_rows(left_side, right_side):
    return lax.dot_general(left_side, right_side, (((1,), (1,)), ((), ())), preferred_element_type=jnp.float32)


def outer_rows(left_side, right_side):
    return lax.dot_general(left_side, right_side, (((0,), (0,)), ((), ())), preferred_element_type=jnp.float32)


def block_terms(query_block, grad_block, key_rows, value_rows, query_index, query_document, key_document):
    score_scale = key_rows.shape[1] ** -0.5
    scores = inner_rows(query_block, key_rows) * score_scale
    key_index = jnp.arange(key_rows.shape[0], dtype=jnp.int32)
    allowed = (key_index[None, :] <= query_index[:, None]) & (key_document[None, :] == query_document[:, None])
    scores = jnp.where(allowed, scores, MASK_VALUE)
    row_max = jnp.max(scores, axis=1, keepdims=True)
    exponent = jnp.exp(scores - row_max)
    probability = exponent / jnp.sum(exponent, axis=1, keepdims=True)
    rounded = probability.astype(jnp.bfloat16)
    attended = jnp.dot(rounded, value_rows, preferred_element_type=jnp.float32).astype(jnp.bfloat16)
    grad_prob = inner_rows(grad_block, value_rows)
    delta_sum = jnp.sum(probability * grad_prob, axis=1, keepdims=True)
    grad_score = (probability * (grad_prob - delta_sum)).astype(jnp.bfloat16)
    query_grad = (jnp.dot(grad_score, key_rows, preferred_element_type=jnp.float32) * score_scale).astype(jnp.bfloat16)
    key_part = outer_rows(grad_score, query_block) * score_scale
    value_part = outer_rows(rounded, grad_block)
    return attended, query_grad, key_part, value_part


def reference(hidden_rows, query_rows, out_grad, projection, packing_plan, document_ids):
    block_ids = jnp.arange(SEQS * SPLIT, dtype=jnp.int32)
    sequence_of = (block_ids // SPLIT)[:, None]
    part_of = (block_ids % SPLIT)[:, None]
    targets = (packing_plan // SEND) * SEQ_LEN + part_of * S_DEV + sequence_of * SEND + packing_plan % SEND
    targets = targets.reshape(-1).astype(jnp.int32)
    packed_hidden = jnp.zeros_like(hidden_rows).at[targets].set(hidden_rows)
    packed_query = jnp.zeros_like(query_rows).at[targets].set(query_rows)
    projected = inner_rows(packed_hidden, projection)
    positions = jnp.arange(TOKENS, dtype=jnp.int32) % SEQ_LEN
    cosine_table, sine_table = rotary_tables(positions, HEAD_DIM)
    key_width = KV_HEADS * HEAD_DIM
    key_heads = rotate_forward(projected[:, :key_width].reshape(TOKENS, KV_HEADS, HEAD_DIM), cosine_table, sine_table).astype(jnp.bfloat16)
    values = projected[:, key_width:].reshape(TOKENS, KV_HEADS, HEAD_DIM).astype(jnp.bfloat16)
    query_heads = packed_query.reshape(SEQS, SEQ_LEN, HEADS, HEAD_DIM).transpose(0, 2, 1, 3).reshape(SEQS * HEADS, SEQ_LEN, HEAD_DIM)
    grad_heads = out_grad.reshape(SEQS, SEQ_LEN, HEADS, HEAD_DIM).transpose(0, 2, 1, 3).reshape(SEQS * HEADS, SEQ_LEN, HEAD_DIM)
    key_major = key_heads.reshape(SEQS, SEQ_LEN, KV_HEADS, HEAD_DIM).transpose(0, 2, 1, 3)
    value_major = values.reshape(SEQS, SEQ_LEN, KV_HEADS, HEAD_DIM).transpose(0, 2, 1, 3)
    group_size = HEADS // KV_HEADS
    query_index = jnp.arange(SEQ_LEN, dtype=jnp.int32)

    def one_head(pair_index):
        sequence = pair_index // HEADS
        group_index = (pair_index % HEADS) // group_size
        documents = document_ids[sequence]
        return block_terms(query_heads[pair_index], grad_heads[pair_index], key_major[sequence, group_index], value_major[sequence, group_index], query_index, documents, documents)

    attended_heads, query_grad_heads, key_parts, value_parts = lax.map(one_head, jnp.arange(SEQS * HEADS, dtype=jnp.int32))

    def to_rows(head_major):
        return head_major.reshape(SEQS, HEADS, SEQ_LEN, HEAD_DIM).transpose(0, 2, 1, 3).reshape(TOKENS, HEADS * HEAD_DIM)

    attended = to_rows(attended_heads)
    query_grad = to_rows(query_grad_heads)
    key_grad = key_parts.reshape(SEQS, KV_HEADS, group_size, SEQ_LEN, HEAD_DIM).sum(axis=2).astype(jnp.bfloat16)
    value_grad = value_parts.reshape(SEQS, KV_HEADS, group_size, SEQ_LEN, HEAD_DIM).sum(axis=2).astype(jnp.bfloat16)
    key_grad = key_grad.transpose(0, 2, 1, 3).reshape(TOKENS, KV_HEADS, HEAD_DIM)
    value_grad = value_grad.transpose(0, 2, 1, 3).reshape(TOKENS, key_width)
    key_back = rotate_adjoint(key_grad.astype(jnp.float32), cosine_table, sine_table).reshape(TOKENS, key_width)
    projected_grad = jnp.concatenate([key_back, value_grad.astype(jnp.float32)], axis=1).astype(jnp.bfloat16)
    hidden_grad = jnp.dot(projected_grad, projection, preferred_element_type=jnp.float32).astype(jnp.bfloat16)
    block_count = SEQS * SPLIT
    grad_blocks = projected_grad.reshape(block_count, S_DEV, KV_WIDTH)
    hidden_blocks = packed_hidden.reshape(block_count, S_DEV, D)

    def add_block(running_sum, block_pair):
        block_term = outer_rows(block_pair[0], block_pair[1]).astype(jnp.bfloat16)
        block_term = lax.optimization_barrier(block_term)
        return running_sum + block_term.astype(jnp.float32), None

    running_sum, unused = lax.scan(add_block, jnp.zeros((KV_WIDTH, D), jnp.float32), (grad_blocks, hidden_blocks))
    weight_grad = running_sum / SEQS
    return attended, query_grad, hidden_grad, weight_grad
```

```python
import functools
import math

import jax
import jax.numpy as jnp
from jax import lax
from jax.experimental import pallas as pl
from jax.experimental.pallas import tpu as pltpu
from jax.sharding import PartitionSpec as P

ROPE_BASE = 500000.0
MASK_VALUE = -1e30
HD = 128
SCALE = HD ** (-0.5)
BF = jnp.bfloat16
F32 = jnp.float32
MESH = pl.DeviceIdType.MESH
KB = 256
MIB = 1024 * 1024


def vm():
    return pl.BlockSpec(memory_space=pltpu.VMEM)


def rows_dot(a, b):
    return lax.dot_general(a, b, (((1,), (1,)), ((), ())), preferred_element_type=F32)


def cols_dot(a, b):
    return lax.dot_general(a, b, (((0,), (0,)), ((), ())), preferred_element_type=F32)


def angle_tables(positions):
    half = HD // 2
    exponent = jnp.arange(half, dtype=F32) * (-2.0 * math.log(ROPE_BASE) / HD)
    angles = positions.astype(F32)[:, None] * jnp.exp(exponent)[None, :]
    cosine, sine = jnp.cos(angles), jnp.sin(angles)
    return jnp.concatenate([cosine, cosine], 1), jnp.concatenate([-sine, sine], 1)


def project_kernel(plan, x, q, og, w, cos, sin, kv, qs, gs, hs, xp, acc):
    step = pl.program_id(0)

    @pl.when(step == 0)
    def _():
        pick = (lax.broadcasted_iota(jnp.int32, (128, 128), 0) == plan[...]).astype(F32).astype(BF)
        for j in range(16):
            sl = slice(j * 256, (j + 1) * 256)
            t = jnp.dot(pick, x[:, sl], preferred_element_type=F32).astype(BF)
            xp[:, sl] = t
            hs[j % 4, :, (j // 4) * 256 : (j // 4 + 1) * 256] = t
        for i in range(8):
            parts, grads = [], []
            for h in (2 * i, 2 * i + 1):
                sl = slice(h * HD, (h + 1) * HD)
                parts.append(jnp.dot(pick, q[:, sl], preferred_element_type=F32).reshape(16, 8, HD))
                grads.append(og[:, sl].astype(F32).reshape(16, 8, HD))
            qs[:, i * 16 : (i + 1) * 16, :] = jnp.concatenate(parts, 1).astype(BF)
            gs[i // 2, :, (i % 2) * 16 : (i % 2 + 1) * 16, :] = jnp.concatenate(grads, 1).astype(BF)

    acc[step] = rows_dot(xp[...], w[...])

    @pl.when(step == 3)
    def _():
        for g in range(4):
            sl = slice((g % 2) * HD, (g % 2 + 1) * HD)
            k = acc[g // 2][:, sl]
            v = acc[2 + g // 2][:, sl]
            k3 = k.reshape(16, 8, HD)
            r3 = pltpu.roll(k, 64, 1).reshape(16, 8, HD)
            rot = k3 * cos[...][None] + r3 * sin[...][None]
            kv[:, g * 16 : (g + 1) * 16, :] = jnp.concatenate([rot, v.reshape(16, 8, HD)], 1).astype(BF)


def project(plan, x, q, og, w, cos, sin):
    full = lambda *shape: pl.BlockSpec(shape, lambda i: (0,) * len(shape))
    return pl.pallas_call(
        project_kernel,
        grid=(4,),
        in_specs=[
            full(1, 128), full(128, 4096), full(128, 2048), full(128, 2048),
            pl.BlockSpec((256, 4096), lambda i: (i, 0)), full(8, HD), full(8, HD),
        ],
        out_specs=[full(16, 64, HD), full(16, 128, HD), full(4, 16, 32, HD), full(4, 128, 1024)],
        out_shape=[
            jax.ShapeDtypeStruct((16, 64, HD), BF),
            jax.ShapeDtypeStruct((16, 128, HD), BF),
            jax.ShapeDtypeStruct((4, 16, 32, HD), BF),
            jax.ShapeDtypeStruct((4, 128, 1024), BF),
        ],
        scratch_shapes=[pltpu.VMEM((128, 4096), BF), pltpu.VMEM((4, 128, 256), F32)],
        compiler_params=pltpu.CompilerParams(vmem_limit_bytes=40 * MIB),
        name="project",
    )(plan, x, q, og, w, cos, sin)


def remote(src, dst, send, recv, device):
    return pltpu.make_async_remote_copy(
        src_ref=src, dst_ref=dst, send_sem=send, recv_sem=recv, device_id=device, device_id_type=MESH
    )


def greet(devices):
    barrier = pltpu.get_barrier_semaphore()
    for device in devices:
        pl.semaphore_signal(barrier, inc=1, device_id=device, device_id_type=MESH)
    pl.semaphore_wait(barrier, len(devices))


def spread_kernel(kv_s, q_s, g_s, h_s, kv_all, q_rx, g_rx, h_rx, kv1, q1, ss, rs, ys, yr, zs, zr):
    d, c = lax.axis_index("dp"), lax.axis_index("ctx")
    z, y = c // 4, c % 4
    dp_of = [(d + k) % 16 for k in range(16)]
    y_of = [(y + k) % 4 for k in range(4)]
    on_dp = lambda k: {"dp": dp_of[k]}
    on_y = lambda k: {"ctx": z * 4 + y_of[k]}
    up, down = {"ctx": (c + 4) % 16}, {"ctx": (c + 12) % 16}
    z_up, z_down = (z + 1) % 4, (z + 3) % 4

    greet([on_dp(k) for k in range(1, 16)] + [on_y(k) for k in range(1, 4)] + [up, down])

    kv_first = [remote(kv_s.at[dp_of[k]], kv1.at[d], ss.at[0, k], rs.at[0, k], on_dp(k)) for k in range(1, 16)]
    for copy in kv_first:
        copy.start()
    grads = [remote(g_s.at[y_of[k]], g_rx.at[y], ys.at[0, k], yr.at[0, k], on_y(k)) for k in range(1, 4)]
    for copy in grads:
        copy.start()
    q_first = [remote(q_s.at[dp_of[k]], q1.at[d], ss.at[1, k], rs.at[1, k], on_dp(k)) for k in range(1, 16)]
    for copy in q_first:
        copy.start()
    kv1[d] = kv_s[d]
    q1[d] = q_s[d]
    g_rx[y] = g_s[y]
    h_rx[y] = h_s[y]

    for copy in kv_first:
        copy.wait_recv()
    group = lambda k: pl.ds(pl.multiple_of(y_of[k] * 16, 16), 16)
    kv_second = [
        remote(kv1.at[:, group(k), :], kv_all.at[z, y], ys.at[1, k], yr.at[1, k], on_y(k)) for k in range(1, 4)
    ]
    for copy in kv_second:
        copy.start()
    kv_all[z, y] = kv1[:, group(0), :]

    chunk = [(y + 4 - t) % 4 for t in range(4)]
    own_up, own_down = [], []
    for t in range(4):
        if t:
            kv_second[t - 1].wait_recv()
        place = kv_all.at[z, chunk[t]]
        own_up.append(remote(place, place, zs.at[0, t], zr.at[0, t], up))
        own_down.append(remote(place, place, zs.at[1, t], zr.at[1, t], down))
        own_up[t].start()
        own_down[t].start()

    for copy in q_first:
        copy.wait_recv()
    heads = lambda k: pl.ds(pl.multiple_of(y_of[k] * 32, 32), 32)
    q_second = [remote(q1.at[:, heads(k), :], q_rx.at[y], ys.at[2, k], yr.at[2, k], on_y(k)) for k in range(1, 4)]
    for copy in q_second:
        copy.start()
    q_rx[y] = q1[:, heads(0), :]
    hidden = [remote(h_s.at[y_of[k]], h_rx.at[y], ys.at[3, k], yr.at[3, k], on_y(k)) for k in range(1, 4)]
    for copy in hidden:
        copy.start()

    passed = []
    for t in range(4):
        own_up[t].wait_recv()
        own_down[t].wait_recv()
        if t % 2 == 0:
            place = kv_all.at[z_down, chunk[t]]
            passed.append(remote(place, place, zs.at[2, t], zr.at[2, t], up))
        else:
            place = kv_all.at[z_up, chunk[t]]
            passed.append(remote(place, place, zs.at[2, t], zr.at[2, t], down))
        passed[t].start()
    for copy in passed + q_second + grads + hidden:
        copy.wait_recv()
    for copy in kv_first + grads + q_first + kv_second + own_up + own_down + q_second + hidden + passed:
        copy.wait_send()


def spread(kv, qs, gs, hs):
    return pl.pallas_call(
        spread_kernel,
        in_specs=[vm()] * 4,
        out_specs=[vm()] * 4,
        out_shape=[
            jax.ShapeDtypeStruct((4, 4, 16, 16, HD), BF),
            jax.ShapeDtypeStruct((4, 16, 32, HD), BF),
            jax.ShapeDtypeStruct((4, 16, 32, HD), BF),
            jax.ShapeDtypeStruct((4, 128, 1024), BF),
        ],
        scratch_shapes=[
            pltpu.VMEM((16, 64, HD), BF),
            pltpu.VMEM((16, 128, HD), BF),
            pltpu.SemaphoreType.DMA((2, 16)),
            pltpu.SemaphoreType.DMA((2, 16)),
            pltpu.SemaphoreType.DMA((4, 4)),
            pltpu.SemaphoreType.DMA((4, 4)),
            pltpu.SemaphoreType.DMA((3, 4)),
            pltpu.SemaphoreType.DMA((3, 4)),
        ],
        compiler_params=pltpu.CompilerParams(collective_id=0, has_side_effects=True, vmem_limit_bytes=40 * MIB),
        name="spread",
    )(kv, qs, gs, hs)


def attend_kernel(info, q, og, kv, first, att, qg, dkv, keys, vals, dk, dv, sc, big, low, out):
    step = pl.program_id(0)
    base = info[0]

    @pl.when(step == 0)
    def _():
        for i in range(4):
            block = kv[pl.ds(i * 64, 64)].astype(F32)
            keys[i * 512 : (i + 1) * 512, :] = block[:, :8, :].reshape(512, HD).astype(BF)
            vals[i * 512 : (i + 1) * 512, :] = block[:, 8:, :].reshape(512, HD).astype(BF)
        dk[...] = jnp.zeros_like(dk)
        dv[...] = jnp.zeros_like(dv)

    start = info[1 + step] // KB
    stop = (base + (step + 1) * 128 + KB - 1) // KB
    row = lax.broadcasted_iota(jnp.int32, (512, 1), 0)
    position = base + step * 128 + (row // 32) * 8 + row % 8
    lowest = first[...]

    big[...] = jnp.full_like(big, MASK_VALUE)

    def scores(kb, carry):
        cols = pl.ds(pl.multiple_of(kb * KB, KB), KB)
        s = rows_dot(q[...], keys[cols, :]) * SCALE
        index = kb * KB + lax.broadcasted_iota(jnp.int32, (512, KB), 1)
        s = jnp.where((index <= position) & (index >= lowest), s, MASK_VALUE)
        sc[:, cols] = s
        big[...] = jnp.maximum(big[...], jnp.maximum(s[:, :128], s[:, 128:]))
        return carry

    lax.fori_loop(start, stop, scores, 0)
    top = jnp.max(big[...], axis=1, keepdims=True)
    low[...] = jnp.zeros_like(low)

    def expo(kb, carry):
        cols = pl.ds(pl.multiple_of(kb * KB, KB), KB)
        e = jnp.exp(sc[:, cols] - top)
        sc[:, cols] = e
        low[...] += e[:, :128] + e[:, 128:]
        return carry

    lax.fori_loop(start, stop, expo, 0)
    inverse = 1.0 / jnp.sum(low[...], axis=1, keepdims=True)
    out[...] = jnp.zeros_like(out)

    def forward(kb, carry):
        cols = pl.ds(pl.multiple_of(kb * KB, KB), KB)
        p = sc[:, cols] * inverse
        sc[:, cols] = p
        rounded = p.astype(BF)
        out[...] += jnp.dot(rounded, vals[cols, :], preferred_element_type=F32)
        dv[cols, :] += cols_dot(rounded, og[...])
        return carry

    lax.fori_loop(start, stop, forward, 0)
    att[...] = out[...].astype(BF)
    delta = jnp.sum(out[...] * og[...].astype(F32), axis=1, keepdims=True)
    out[...] = jnp.zeros_like(out)

    def backward(kb, carry):
        cols = pl.ds(pl.multiple_of(kb * KB, KB), KB)
        dp = rows_dot(og[...], vals[cols, :])
        ds = (sc[:, cols] * (dp - delta)).astype(BF)
        out[...] += jnp.dot(ds, keys[cols, :], preferred_element_type=F32)
        dk[cols, :] += cols_dot(ds, q[...])
        return carry

    lax.fori_loop(start, stop, backward, 0)
    qg[...] = (out[...] * SCALE).astype(BF)

    @pl.when(step == 3)
    def _():
        for i in range(4):
            dkv[i, 0] = (dk[i * 512 : (i + 1) * 512, :] * SCALE).astype(BF)
            dkv[i, 1] = dv[i * 512 : (i + 1) * 512, :].astype(BF)


def attend(info, q, og, kv, first):
    full = lambda *shape: pl.BlockSpec(shape, lambda i, s: (0,) * len(shape))
    rows = lambda n: pl.BlockSpec((512, n), lambda i, s: (i, 0))
    return pl.pallas_call(
        attend_kernel,
        grid_spec=pltpu.PrefetchScalarGridSpec(
            num_scalar_prefetch=1,
            grid=(4,),
            in_specs=[rows(HD), rows(HD), full(256, 16, HD), rows(1)],
            out_specs=[rows(HD), rows(HD), full(4, 2, 512, HD)],
            scratch_shapes=[
                pltpu.VMEM((2048, HD), BF),
                pltpu.VMEM((2048, HD), BF),
                pltpu.VMEM((2048, HD), F32),
                pltpu.VMEM((2048, HD), F32),
                pltpu.VMEM((512, 2048), F32),
                pltpu.VMEM((512, HD), F32),
                pltpu.VMEM((512, HD), F32),
                pltpu.VMEM((512, HD), F32),
            ],
        ),
        out_shape=[
            jax.ShapeDtypeStruct((2048, HD), BF),
            jax.ShapeDtypeStruct((2048, HD), BF),
            jax.ShapeDtypeStruct((4, 2, 512, HD), BF),
        ],
        compiler_params=pltpu.CompilerParams(vmem_limit_bytes=48 * MIB),
        name="attend",
    )(info, q, og, kv, first)


def collect_kernel(att, qg, dkv, cos, sin, att_rx, qg_rx, pg_rx, src, own, hop, mid, fin, ys, yr, zs, zr, ss, rs):
    d, c = lax.axis_index("dp"), lax.axis_index("ctx")
    z, y = c // 4, c % 4
    dp_of = [(d + k) % 16 for k in range(16)]
    y_of = [(y + k) % 4 for k in range(4)]
    on_dp = lambda k: {"dp": dp_of[k]}
    on_y = lambda k: {"ctx": z * 4 + y_of[k]}
    up, down = {"ctx": (c + 4) % 16}, {"ctx": (c + 12) % 16}
    z_up, z_down, z_far = (z + 1) % 4, (z + 3) % 4, (z + 2) % 4

    greet([on_dp(k) for k in range(1, 16)] + [on_y(k) for k in range(1, 4)] + [up, down])

    far = [
        remote(dkv.at[z_far, 0], hop.at[0], zs.at[0], zr.at[0], down),
        remote(dkv.at[z_far, 1], hop.at[1], zs.at[1], zr.at[1], up),
    ]
    near = [
        remote(dkv.at[z_down, 1], fin.at[1, 0], zs.at[2], zr.at[2], down),
        remote(dkv.at[z_up, 0], fin.at[0, 0], zs.at[3], zr.at[3], up),
    ]
    for copy in far + near:
        copy.start()
    back = []
    for i, (a, b) in enumerate(((att, att_rx), (qg, qg_rx))):
        for k in range(1, 4):
            back.append(remote(a.at[y_of[k]], b.at[y], ys.at[i, k], yr.at[i, k], on_y(k)))
            back[-1].start()
        b[y] = a[y]

    far[0].wait_recv()
    mid[0] = (hop[0].astype(F32) + dkv[z_down, 0].astype(F32)).astype(BF)
    sums = [remote(mid.at[0], fin.at[0, 1], zs.at[4], zr.at[4], down)]
    sums[0].start()
    far[1].wait_recv()
    mid[1] = (hop[1].astype(F32) + dkv[z_up, 1].astype(F32)).astype(BF)
    sums.append(remote(mid.at[1], fin.at[1, 1], zs.at[5], zr.at[5], up))
    sums[1].start()
    for copy in near + sums:
        copy.wait_recv()
    for i in range(4):
        sl = slice(i * 128, (i + 1) * 128)
        total = lambda j: (
            dkv[z, j, sl, :].astype(F32) + fin[j, 0, sl, :].astype(F32) + fin[j, 1, sl, :].astype(F32)
        ).astype(BF).astype(F32)
        k = total(0)
        k = k * cos[sl, :] - pltpu.roll(k, 64, 1) * sin[sl, :]
        own[i] = jnp.concatenate([k.reshape(16, 8, HD), total(1).reshape(16, 8, HD)], 1).astype(BF)

    first = [remote(own.at[:, dp_of[k]], src.at[y, d], ss.at[k], rs.at[k], on_dp(k)) for k in range(1, 16)]
    for copy in first:
        copy.start()
    packed = [remote(own.at[y_of[k]], pg_rx.at[y], ys.at[2, k], yr.at[2, k], on_y(k)) for k in range(1, 4)]
    for copy in packed:
        copy.start()
    pg_rx[y] = own[y]
    src[y, d] = own[:, d]
    for copy in first:
        copy.wait_recv()
    gather = [remote(src.at[y], src.at[y], ys.at[3, k], yr.at[3, k], on_y(k)) for k in range(1, 4)]
    for copy in gather:
        copy.start()
    for copy in back + packed + gather:
        copy.wait_recv()
    for copy in far + near + back + sums + first + packed + gather:
        copy.wait_send()


def collect(att, qg, dkv, cos, sin):
    return pl.pallas_call(
        collect_kernel,
        in_specs=[vm()] * 5,
        out_specs=[vm()] * 4,
        out_shape=[
            jax.ShapeDtypeStruct((4, 512, HD), BF),
            jax.ShapeDtypeStruct((4, 512, HD), BF),
            jax.ShapeDtypeStruct((4, 16, 16, HD), BF),
            jax.ShapeDtypeStruct((4, 16, 4, 16, HD), BF),
        ],
        scratch_shapes=[
            pltpu.VMEM((4, 16, 16, HD), BF),
            pltpu.VMEM((2, 512, HD), BF),
            pltpu.VMEM((2, 512, HD), BF),
            pltpu.VMEM((2, 2, 512, HD), BF),
            pltpu.SemaphoreType.DMA((4, 4)),
            pltpu.SemaphoreType.DMA((4, 4)),
            pltpu.SemaphoreType.DMA((6,)),
            pltpu.SemaphoreType.DMA((6,)),
            pltpu.SemaphoreType.DMA((16,)),
            pltpu.SemaphoreType.DMA((16,)),
        ],
        compiler_params=pltpu.CompilerParams(collective_id=1, has_side_effects=True, vmem_limit_bytes=40 * MIB),
        name="collect",
    )(att, qg, dkv, cos, sin)


def weight_kernel(src, hs, tile, pgm):
    step = pl.program_id(0)

    @pl.when(step == 0)
    def _():
        for g in range(4):
            for i in range(4):
                block = src[g, :, i].astype(F32)
                pgm[i * 128 : (i + 1) * 128, g * HD : (g + 1) * HD] = block[:, :8, :].reshape(128, HD).astype(BF)
                pgm[i * 128 : (i + 1) * 128, (4 + g) * HD : (5 + g) * HD] = (
                    block[:, 8:, :].reshape(128, HD).astype(BF)
                )

    t = cols_dot(pgm[...], hs[...])
    tile[...] = t.reshape(16, 1, 64, 256).astype(BF)


def weight(src, hs):
    return pl.pallas_call(
        weight_kernel,
        grid=(4,),
        in_specs=[
            pl.BlockSpec((4, 16, 4, 16, HD), lambda i: (0, 0, 0, 0, 0)),
            pl.BlockSpec((512, 256), lambda i: (0, i)),
        ],
        out_specs=pl.BlockSpec((16, 1, 64, 256), lambda i: (0, i, 0, 0)),
        out_shape=jax.ShapeDtypeStruct((16, 4, 64, 256), BF),
        scratch_shapes=[pltpu.VMEM((512, 1024), BF)],
        compiler_params=pltpu.CompilerParams(vmem_limit_bytes=40 * MIB),
        name="weight",
    )(src, hs)


def reduce_kernel(tile, grad, pair, mine, ring, part, last, cs, cr, xs, xr, zs, zr):
    d, c = lax.axis_index("dp"), lax.axis_index("ctx")
    zl, x, core = d // 8, (d // 2) % 4, d % 2
    z, y = c // 4, c % 4
    x_of = [(x + k) % 4 for k in range(4)]
    sibling = {"dp": d + 1 - 2 * core}
    on_x = lambda k: {"dp": zl * 8 + x_of[k] * 2 + core}
    zz = zl * 4 + z
    z_of = [(zz + k) % 8 for k in range(8)]
    on_z = lambda k: {"dp": (z_of[k] // 4) * 8 + x * 2 + core, "ctx": (z_of[k] % 4) * 4 + y}

    greet([sibling] + [on_x(k) for k in range(1, 4)] + [on_z(k) for k in range(1, 8)])

    order = [2, 1, 3, 0]
    swaps = [
        remote(tile.at[:, x_of[k], 1 - core], pair.at[:, x_of[k]], cs.at[k], cr.at[k], sibling) for k in order
    ]
    for copy in swaps:
        copy.start()
    sums = []
    for copy, k in zip(swaps, order):
        copy.wait_recv()
        for a in range(2):
            for b in range(4):
                mine[k, a, b] = (
                    tile[a, x_of[k], core, b].astype(F32) + pair[a, x_of[k], b].astype(F32)
                ).astype(BF)
        if k:
            sums.append(remote(mine.at[k], ring.at[k], xs.at[k], xr.at[k], on_x(k)))
            sums[-1].start()
    for copy in sums:
        copy.wait_recv()
    for a in range(2):
        for b in range(4):
            t = mine[0, a, b].astype(F32)
            for k in range(1, 4):
                t = t + ring[k, a, b].astype(F32)
            part[a * 4 + b] = t.astype(BF)
    ends = [remote(part.at[z_of[k]], last.at[k], zs.at[k], zr.at[k], on_z(k)) for k in range(1, 8)]
    for copy in ends:
        copy.start()
    for copy in ends:
        copy.wait_recv()
    t = part[zz].astype(F32)
    for k in range(1, 8):
        t = t + last[k].astype(F32)
    grad[...] = t * (1.0 / 16.0)
    for copy in swaps + sums + ends:
        copy.wait_send()


def reduce_tiles(tile):
    return pl.pallas_call(
        reduce_kernel,
        in_specs=[vm()],
        out_specs=vm(),
        out_shape=jax.ShapeDtypeStruct((64, 256), F32),
        scratch_shapes=[
            pltpu.VMEM((2, 4, 4, 64, 256), BF),
            pltpu.VMEM((4, 2, 4, 64, 256), BF),
            pltpu.VMEM((4, 2, 4, 64, 256), BF),
            pltpu.VMEM((8, 64, 256), BF),
            pltpu.VMEM((8, 64, 256), BF),
            pltpu.SemaphoreType.DMA((4,)),
            pltpu.SemaphoreType.DMA((4,)),
            pltpu.SemaphoreType.DMA((4,)),
            pltpu.SemaphoreType.DMA((4,)),
            pltpu.SemaphoreType.DMA((8,)),
            pltpu.SemaphoreType.DMA((8,)),
        ],
        compiler_params=pltpu.CompilerParams(collective_id=2, has_side_effects=True, vmem_limit_bytes=40 * MIB),
        name="reduce_tiles",
    )(tile)


def finish_kernel(att, qg, pg, w1, w2, att_o, qg_o, hg_o, pgm):
    step = pl.program_id(0)

    @pl.when(step == 0)
    def _():
        for g in range(4):
            block = pg[g].astype(F32)
            pgm[:, g * HD : (g + 1) * HD] = block[:, :8, :].reshape(128, HD).astype(BF)
            pgm[:, (4 + g) * HD : (5 + g) * HD] = block[:, 8:, :].reshape(128, HD).astype(BF)
            for source, target in ((att, att_o), (qg, qg_o)):
                block = source[g].reshape(16, 32, HD).astype(F32)
                for h in range(4):
                    cols = slice((g * 4 + h) * HD, (g * 4 + h + 1) * HD)
                    target[:, cols] = block[:, h * 8 : h * 8 + 8, :].reshape(128, HD).astype(BF)

    hg_o[...] = (
        jnp.dot(pgm[:, :512], w1[...], preferred_element_type=F32)
        + jnp.dot(pgm[:, 512:], w2[...], preferred_element_type=F32)
    ).astype(BF)


def finish(att, qg, pg, w):
    full = lambda *shape: pl.BlockSpec(shape, lambda i: (0,) * len(shape))
    return pl.pallas_call(
        finish_kernel,
        grid=(8,),
        in_specs=[
            full(4, 512, HD), full(4, 512, HD), full(4, 16, 16, HD),
            pl.BlockSpec((512, 512), lambda i: (0, i)), pl.BlockSpec((512, 512), lambda i: (1, i)),
        ],
        out_specs=[full(128, 2048), full(128, 2048), pl.BlockSpec((128, 512), lambda i: (0, i))],
        out_shape=[
            jax.ShapeDtypeStruct((128, 2048), BF),
            jax.ShapeDtypeStruct((128, 2048), BF),
            jax.ShapeDtypeStruct((128, 4096), BF),
        ],
        scratch_shapes=[pltpu.VMEM((128, 1024), BF)],
        compiler_params=pltpu.CompilerParams(vmem_limit_bytes=40 * MIB),
        name="finish",
    )(att, qg, pg, w, w)


def body(hidden_rows, query_rows, out_grad, projection, packing_plan, document_ids):
    d, c = lax.axis_index("dp"), lax.axis_index("ctx")
    z = c // 4
    near_cos, near_sin = angle_tables(c * 128 + d * 8 + jnp.arange(8, dtype=jnp.int32))
    cos, sin = angle_tables(z * 512 + jnp.arange(512, dtype=jnp.int32))
    documents = document_ids[0]
    own_documents = lax.dynamic_slice_in_dim(documents, z * 512, 512)
    first = jnp.sum((documents[None, :] < own_documents[:, None]).astype(jnp.int32), axis=1)
    info = jnp.concatenate([(z * 512)[None].astype(jnp.int32), first[::128]])
    first_rows = jnp.broadcast_to(first.reshape(64, 1, 8), (64, 4, 8)).reshape(2048, 1)

    kv, qs, gs, hs = project(packing_plan, hidden_rows, query_rows, out_grad, projection, near_cos, near_sin)
    kv_all, q_rx, g_rx, h_rx = spread(kv, qs, gs, hs)
    att, qg, dkv = attend(
        info, q_rx.reshape(2048, HD), g_rx.reshape(2048, HD), kv_all.reshape(256, 16, HD), first_rows
    )
    att_rx, qg_rx, pg_rx, src = collect(att.reshape(4, 512, HD), qg.reshape(4, 512, HD), dkv, cos, sin)
    tile = weight(src, h_rx.reshape(512, 1024))
    attended, query_grad, hidden_grad = finish(att_rx, qg_rx, pg_rx, projection)
    weight_grad = reduce_tiles(tile.reshape(2, 4, 2, 4, 64, 256))
    return attended, query_grad, hidden_grad, weight_grad


def solution(mesh):
    rows = P(("dp", "ctx"), None)
    return jax.shard_map(
        body,
        mesh=mesh,
        in_specs=(rows, rows, rows, P(), rows, P("dp", None)),
        out_specs=(rows, rows, rows, P("dp", "ctx")),
        check_vma=False,
    )
```

```python
import functools
import math

import jax
import jax.numpy as jnp
from jax import lax
from jax.experimental import pallas as pl
from jax.experimental.pallas import tpu as pltpu
from jax.sharding import PartitionSpec as P

ROPE_BASE = 500000.0
MASK_VALUE = -1e30
HD = 128
SCALE = HD ** (-0.5)
BF = jnp.bfloat16
F32 = jnp.float32
MESH = pl.DeviceIdType.MESH
KB = 256
MIB = 1024 * 1024


def vm():
    return pl.BlockSpec(memory_space=pltpu.VMEM)


def rows_dot(a, b):
    return lax.dot_general(a, b, (((1,), (1,)), ((), ())), preferred_element_type=F32)


def cols_dot(a, b):
    return lax.dot_general(a, b, (((0,), (0,)), ((), ())), preferred_element_type=F32)


def angle_tables(positions):
    half = HD // 2
    exponent = jnp.arange(half, dtype=F32) * (-2.0 * math.log(ROPE_BASE) / HD)
    angles = positions.astype(F32)[:, None] * jnp.exp(exponent)[None, :]
    cosine, sine = jnp.cos(angles), jnp.sin(angles)
    return jnp.concatenate([cosine, cosine], 1), jnp.concatenate([-sine, sine], 1)


def project_kernel(plan, x, q, og, w, cos, sin, kv, qs, gs, hs, xp, acc):
    step = pl.program_id(0)

    @pl.when(step == 0)
    def _():
        pick = (lax.broadcasted_iota(jnp.int32, (128, 128), 0) == plan[...]).astype(F32).astype(BF)
        for j in range(16):
            sl = slice(j * 256, (j + 1) * 256)
            t = jnp.dot(pick, x[:, sl], preferred_element_type=F32).astype(BF)
            xp[:, sl] = t
            hs[j % 4, :, (j // 4) * 256 : (j // 4 + 1) * 256] = t
        for i in range(8):
            parts, grads = [], []
            for h in (2 * i, 2 * i + 1):
                sl = slice(h * HD, (h + 1) * HD)
                parts.append(jnp.dot(pick, q[:, sl], preferred_element_type=F32).reshape(16, 8, HD))
                grads.append(og[:, sl].astype(F32).reshape(16, 8, HD))
            qs[:, i * 16 : (i + 1) * 16, :] = jnp.concatenate(parts, 1).astype(BF)
            gs[i // 2, :, (i % 2) * 16 : (i % 2 + 1) * 16, :] = jnp.concatenate(grads, 1).astype(BF)

    acc[step] = rows_dot(xp[...], w[...])

    @pl.when(step == 3)
    def _():
        for g in range(4):
            sl = slice((g % 2) * HD, (g % 2 + 1) * HD)
            k = acc[g // 2][:, sl]
            v = acc[2 + g // 2][:, sl]
            k3 = k.reshape(16, 8, HD)
            r3 = pltpu.roll(k, 64, 1).reshape(16, 8, HD)
            rot = k3 * cos[...][None] + r3 * sin[...][None]
            kv[:, g * 16 : (g + 1) * 16, :] = jnp.concatenate([rot, v.reshape(16, 8, HD)], 1).astype(BF)


def project(plan, x, q, og, w, cos, sin):
    full = lambda *shape: pl.BlockSpec(shape, lambda i: (0,) * len(shape))
    return pl.pallas_call(
        project_kernel,
        grid=(4,),
        in_specs=[
            full(1, 128), full(128, 4096), full(128, 2048), full(128, 2048),
            pl.BlockSpec((256, 4096), lambda i: (i, 0)), full(8, HD), full(8, HD),
        ],
        out_specs=[full(16, 64, HD), full(16, 128, HD), full(4, 16, 32, HD), full(4, 128, 1024)],
        out_shape=[
            jax.ShapeDtypeStruct((16, 64, HD), BF),
            jax.ShapeDtypeStruct((16, 128, HD), BF),
            jax.ShapeDtypeStruct((4, 16, 32, HD), BF),
            jax.ShapeDtypeStruct((4, 128, 1024), BF),
        ],
        scratch_shapes=[pltpu.VMEM((128, 4096), BF), pltpu.VMEM((4, 128, 256), F32)],
        compiler_params=pltpu.CompilerParams(vmem_limit_bytes=40 * MIB),
        name="project",
    )(plan, x, q, og, w, cos, sin)


def remote(src, dst, send, recv, device):
    return pltpu.make_async_remote_copy(
        src_ref=src, dst_ref=dst, send_sem=send, recv_sem=recv, device_id=device, device_id_type=MESH
    )


def greet(devices):
    barrier = pltpu.get_barrier_semaphore()
    for device in devices:
        pl.semaphore_signal(barrier, inc=1, device_id=device, device_id_type=MESH)
    pl.semaphore_wait(barrier, len(devices))


def spread_kernel(kv_s, q_s, g_s, h_s, kv_all, q_rx, g_rx, h_rx, kv1, q1, ss, rs, ys, yr, zs, zr):
    d, c = lax.axis_index("dp"), lax.axis_index("ctx")
    z, y = c // 4, c % 4
    dp_of = [(d + k) % 16 for k in range(16)]
    y_of = [(y + k) % 4 for k in range(4)]
    on_dp = lambda k: {"dp": dp_of[k]}
    on_y = lambda k: {"ctx": z * 4 + y_of[k]}
    up, down = {"ctx": (c + 4) % 16}, {"ctx": (c + 12) % 16}
    z_up, z_down = (z + 1) % 4, (z + 3) % 4

    greet([on_dp(k) for k in range(1, 16)] + [on_y(k) for k in range(1, 4)] + [up, down])

    kv_first = [remote(kv_s.at[dp_of[k]], kv1.at[d], ss.at[0, k], rs.at[0, k], on_dp(k)) for k in range(1, 16)]
    for copy in kv_first:
        copy.start()
    grads = [remote(g_s.at[y_of[k]], g_rx.at[y], ys.at[0, k], yr.at[0, k], on_y(k)) for k in range(1, 4)]
    for copy in grads:
        copy.start()
    q_first = [remote(q_s.at[dp_of[k]], q1.at[d], ss.at[1, k], rs.at[1, k], on_dp(k)) for k in range(1, 16)]
    for copy in q_first:
        copy.start()
    kv1[d] = kv_s[d]
    q1[d] = q_s[d]
    g_rx[y] = g_s[y]
    h_rx[y] = h_s[y]

    for copy in kv_first:
        copy.wait_recv()
    group = lambda k: pl.ds(pl.multiple_of(y_of[k] * 16, 16), 16)
    kv_second = [
        remote(kv1.at[:, group(k), :], kv_all.at[z, y], ys.at[1, k], yr.at[1, k], on_y(k)) for k in range(1, 4)
    ]
    for copy in kv_second:
        copy.start()
    kv_all[z, y] = kv1[:, group(0), :]

    chunk = [(y + 4 - t) % 4 for t in range(4)]
    own_up, own_down = [], []
    for t in range(4):
        if t:
            kv_second[t - 1].wait_recv()
        place = kv_all.at[z, chunk[t]]
        own_up.append(remote(place, place, zs.at[0, t], zr.at[0, t], up))
        own_down.append(remote(place, place, zs.at[1, t], zr.at[1, t], down))
        own_up[t].start()
        own_down[t].start()

    for copy in q_first:
        copy.wait_recv()
    heads = lambda k: pl.ds(pl.multiple_of(y_of[k] * 32, 32), 32)
    q_second = [remote(q1.at[:, heads(k), :], q_rx.at[y], ys.at[2, k], yr.at[2, k], on_y(k)) for k in range(1, 4)]
    for copy in q_second:
        copy.start()
    q_rx[y] = q1[:, heads(0), :]
    hidden = [remote(h_s.at[y_of[k]], h_rx.at[y], ys.at[3, k], yr.at[3, k], on_y(k)) for k in range(1, 4)]
    for copy in hidden:
        copy.start()

    passed = []
    for t in range(4):
        own_up[t].wait_recv()
        own_down[t].wait_recv()
        if t % 2 == 0:
            place = kv_all.at[z_down, chunk[t]]
            passed.append(remote(place, place, zs.at[2, t], zr.at[2, t], up))
        else:
            place = kv_all.at[z_up, chunk[t]]
            passed.append(remote(place, place, zs.at[2, t], zr.at[2, t], down))
        passed[t].start()
    for copy in passed + q_second + grads + hidden:
        copy.wait_recv()
    for copy in kv_first + grads + q_first + kv_second + own_up + own_down + q_second + hidden + passed:
        copy.wait_send()


def spread(kv, qs, gs, hs):
    return pl.pallas_call(
        spread_kernel,
        in_specs=[vm()] * 4,
        out_specs=[vm()] * 4,
        out_shape=[
            jax.ShapeDtypeStruct((4, 4, 16, 16, HD), BF),
            jax.ShapeDtypeStruct((4, 16, 32, HD), BF),
            jax.ShapeDtypeStruct((4, 16, 32, HD), BF),
            jax.ShapeDtypeStruct((4, 128, 1024), BF),
        ],
        scratch_shapes=[
            pltpu.VMEM((16, 64, HD), BF),
            pltpu.VMEM((16, 128, HD), BF),
            pltpu.SemaphoreType.DMA((2, 16)),
            pltpu.SemaphoreType.DMA((2, 16)),
            pltpu.SemaphoreType.DMA((4, 4)),
            pltpu.SemaphoreType.DMA((4, 4)),
            pltpu.SemaphoreType.DMA((3, 4)),
            pltpu.SemaphoreType.DMA((3, 4)),
        ],
        compiler_params=pltpu.CompilerParams(collective_id=0, has_side_effects=True, vmem_limit_bytes=40 * MIB),
        name="spread",
    )(kv, qs, gs, hs)


def attend_kernel(info, q, og, kv, first, att, qg, dkv, keys, vals, keys_t, vals_t, dk, dv, sc, gp, q_t, og_t, out_t, grad_t):
    base = info[0]
    for i in range(4):
        block = kv[pl.ds(i * 64, 64)].astype(F32)
        rows = slice(i * 512, (i + 1) * 512)
        k = block[:, :8, :].reshape(512, HD)
        v = block[:, 8:, :].reshape(512, HD)
        keys[rows, :] = k.astype(BF)
        vals[rows, :] = v.astype(BF)
        keys_t[:, rows] = k.T.astype(BF)
        vals_t[:, rows] = v.T.astype(BF)
    keys[2048:, :] = jnp.zeros((128, HD), BF)
    vals[2048:, :] = jnp.zeros((128, HD), BF)
    keys_t[:, 2048:] = jnp.zeros((HD, 128), BF)
    vals_t[:, 2048:] = jnp.zeros((HD, 128), BF)
    dk[...] = jnp.zeros_like(dk)
    dv[...] = jnp.zeros_like(dv)
    fold = SCALE * math.log2(math.e)

    def query_block(qb, carry):
        here = pl.ds(pl.multiple_of(qb * 512, 512), 512)
        q_t[...] = q[here, :].astype(F32).T.astype(BF)
        og_t[...] = og[here, :].astype(F32).T.astype(BF)
        start = (info[1 + qb] // 128) * 128
        count = (base + (qb + 1) * 128 - start + KB - 1) // KB
        lane = lax.broadcasted_iota(jnp.int32, (1, 512), 1)
        position = base + qb * 128 + (lane // 32) * 8 + lane % 8
        lowest = first[qb]
        out_t[...] = jnp.zeros_like(out_t)
        grad_t[...] = jnp.zeros_like(grad_t)

        def eights(t):
            return t.reshape(KB // 8, 8, 512)

        def scores(i, top):
            at = pl.multiple_of(start + i * KB, 128)
            rows = pl.ds(at, KB)
            s = jnp.dot(keys[rows, :], q_t[...], preferred_element_type=F32)
            index = at + lax.broadcasted_iota(jnp.int32, (KB, 512), 0)
            s = jnp.where((index <= position) & (index >= lowest), s, MASK_VALUE)
            sc[rows, :] = s
            return jnp.maximum(top, jnp.max(eights(s), axis=0))

        top = lax.fori_loop(0, count, scores, jnp.full((8, 512), MASK_VALUE, F32))
        top = jnp.max(top, axis=0, keepdims=True) * fold

        def expo(i, sums):
            rows = pl.ds(pl.multiple_of(start + i * KB, 128), KB)
            e = jnp.exp2(sc[rows, :] * fold - top)
            grad = jnp.dot(vals[rows, :], og_t[...], preferred_element_type=F32)
            sc[rows, :] = e
            gp[rows, :] = grad
            return sums[0] + jnp.sum(eights(e), axis=0), sums[1] + jnp.sum(eights(e * grad), axis=0)

        zero = jnp.zeros((8, 512), F32)
        total, product = lax.fori_loop(0, count, expo, (zero, zero))
        inverse = 1.0 / jnp.sum(total, axis=0, keepdims=True)
        delta = jnp.sum(product, axis=0, keepdims=True) * inverse

        def both(i, c):
            at = pl.multiple_of(start + i * KB, 128)
            rows = pl.ds(at, KB)
            p = sc[rows, :] * inverse
            rounded = p.astype(BF)
            ds = (p * (gp[rows, :] - delta)).astype(BF)
            dv[rows, :] += jnp.dot(rounded, og[here, :], preferred_element_type=F32)
            dk[rows, :] += jnp.dot(ds, q[here, :], preferred_element_type=F32)
            out_t[...] += jnp.dot(vals_t[:, rows], rounded, preferred_element_type=F32)
            grad_t[...] += jnp.dot(keys_t[:, rows], ds, preferred_element_type=F32)
            return c

        lax.fori_loop(0, count, both, 0)
        att[here, :] = out_t[...].T.astype(BF)
        qg[here, :] = (grad_t[...] * SCALE).T.astype(BF)
        return carry

    lax.fori_loop(0, 4, query_block, 0)
    for i in range(4):
        rows = slice(i * 512, (i + 1) * 512)
        dkv[i, 0] = (dk[rows, :] * SCALE).astype(BF)
        dkv[i, 1] = dv[rows, :].astype(BF)


def attend(info, q, og, kv, first):
    return pl.pallas_call(
        attend_kernel,
        in_specs=[pl.BlockSpec(memory_space=pltpu.SMEM)] + [vm()] * 4,
        out_specs=[vm()] * 3,
        scratch_shapes=[
            pltpu.VMEM((2176, HD), BF),
            pltpu.VMEM((2176, HD), BF),
            pltpu.VMEM((HD, 2176), BF),
            pltpu.VMEM((HD, 2176), BF),
            pltpu.VMEM((2176, HD), F32),
            pltpu.VMEM((2176, HD), F32),
            pltpu.VMEM((2176, 512), F32),
            pltpu.VMEM((2176, 512), F32),
            pltpu.VMEM((HD, 512), BF),
            pltpu.VMEM((HD, 512), BF),
            pltpu.VMEM((HD, 512), F32),
            pltpu.VMEM((HD, 512), F32),
        ],
        out_shape=[
            jax.ShapeDtypeStruct((2048, HD), BF),
            jax.ShapeDtypeStruct((2048, HD), BF),
            jax.ShapeDtypeStruct((4, 2, 512, HD), BF),
        ],
        compiler_params=pltpu.CompilerParams(vmem_limit_bytes=48 * MIB),
        name="attend",
    )(info, q, og, kv, first)


def collect_kernel(att, qg, dkv, cos, sin, att_rx, qg_rx, pg_rx, src, own, hop, mid, fin, ys, yr, zs, zr, ss, rs):
    d, c = lax.axis_index("dp"), lax.axis_index("ctx")
    z, y = c // 4, c % 4
    dp_of = [(d + k) % 16 for k in range(16)]
    y_of = [(y + k) % 4 for k in range(4)]
    on_dp = lambda k: {"dp": dp_of[k]}
    on_y = lambda k: {"ctx": z * 4 + y_of[k]}
    up, down = {"ctx": (c + 4) % 16}, {"ctx": (c + 12) % 16}
    z_up, z_down, z_far = (z + 1) % 4, (z + 3) % 4, (z + 2) % 4

    greet([on_dp(k) for k in range(1, 16)] + [on_y(k) for k in range(1, 4)] + [up, down])

    far = [
        remote(dkv.at[z_far, 0], hop.at[0], zs.at[0], zr.at[0], down),
        remote(dkv.at[z_far, 1], hop.at[1], zs.at[1], zr.at[1], up),
    ]
    near = [
        remote(dkv.at[z_down, 1], fin.at[1, 0], zs.at[2], zr.at[2], down),
        remote(dkv.at[z_up, 0], fin.at[0, 0], zs.at[3], zr.at[3], up),
    ]
    for copy in far + near:
        copy.start()
    back = []
    for i, (a, b) in enumerate(((att, att_rx), (qg, qg_rx))):
        for k in range(1, 4):
            back.append(remote(a.at[y_of[k]], b.at[y], ys.at[i, k], yr.at[i, k], on_y(k)))
            back[-1].start()
        b[y] = a[y]

    far[0].wait_recv()
    mid[0] = (hop[0].astype(F32) + dkv[z_down, 0].astype(F32)).astype(BF)
    sums = [remote(mid.at[0], fin.at[0, 1], zs.at[4], zr.at[4], down)]
    sums[0].start()
    far[1].wait_recv()
    mid[1] = (hop[1].astype(F32) + dkv[z_up, 1].astype(F32)).astype(BF)
    sums.append(remote(mid.at[1], fin.at[1, 1], zs.at[5], zr.at[5], up))
    sums[1].start()
    for copy in near + sums:
        copy.wait_recv()
    for i in range(4):
        sl = slice(i * 128, (i + 1) * 128)
        total = lambda j: (
            dkv[z, j, sl, :].astype(F32) + fin[j, 0, sl, :].astype(F32) + fin[j, 1, sl, :].astype(F32)
        ).astype(BF).astype(F32)
        k = total(0)
        k = k * cos[sl, :] - pltpu.roll(k, 64, 1) * sin[sl, :]
        own[i] = jnp.concatenate([k.reshape(16, 8, HD), total(1).reshape(16, 8, HD)], 1).astype(BF)

    first = [remote(own.at[:, dp_of[k]], src.at[y, d], ss.at[k], rs.at[k], on_dp(k)) for k in range(1, 16)]
    for copy in first:
        copy.start()
    packed = [remote(own.at[y_of[k]], pg_rx.at[y], ys.at[2, k], yr.at[2, k], on_y(k)) for k in range(1, 4)]
    for copy in packed:
        copy.start()
    pg_rx[y] = own[y]
    src[y, d] = own[:, d]
    for copy in first:
        copy.wait_recv()
    gather = [remote(src.at[y], src.at[y], ys.at[3, k], yr.at[3, k], on_y(k)) for k in range(1, 4)]
    for copy in gather:
        copy.start()
    for copy in back + packed + gather:
        copy.wait_recv()
    for copy in far + near + back + sums + first + packed + gather:
        copy.wait_send()


def collect(att, qg, dkv, cos, sin):
    return pl.pallas_call(
        collect_kernel,
        in_specs=[vm()] * 5,
        out_specs=[vm()] * 4,
        out_shape=[
            jax.ShapeDtypeStruct((4, 512, HD), BF),
            jax.ShapeDtypeStruct((4, 512, HD), BF),
            jax.ShapeDtypeStruct((4, 16, 16, HD), BF),
            jax.ShapeDtypeStruct((4, 16, 4, 16, HD), BF),
        ],
        scratch_shapes=[
            pltpu.VMEM((4, 16, 16, HD), BF),
            pltpu.VMEM((2, 512, HD), BF),
            pltpu.VMEM((2, 512, HD), BF),
            pltpu.VMEM((2, 2, 512, HD), BF),
            pltpu.SemaphoreType.DMA((4, 4)),
            pltpu.SemaphoreType.DMA((4, 4)),
            pltpu.SemaphoreType.DMA((6,)),
            pltpu.SemaphoreType.DMA((6,)),
            pltpu.SemaphoreType.DMA((16,)),
            pltpu.SemaphoreType.DMA((16,)),
        ],
        compiler_params=pltpu.CompilerParams(collective_id=1, has_side_effects=True, vmem_limit_bytes=40 * MIB),
        name="collect",
    )(att, qg, dkv, cos, sin)


def weight_kernel(src, hs, tile, pgm):
    step = pl.program_id(0)

    @pl.when(step == 0)
    def _():
        for g in range(4):
            for i in range(4):
                block = src[g, :, i].astype(F32)
                pgm[i * 128 : (i + 1) * 128, g * HD : (g + 1) * HD] = block[:, :8, :].reshape(128, HD).astype(BF)
                pgm[i * 128 : (i + 1) * 128, (4 + g) * HD : (5 + g) * HD] = (
                    block[:, 8:, :].reshape(128, HD).astype(BF)
                )

    t = cols_dot(pgm[...], hs[...])
    tile[...] = t.reshape(16, 1, 64, 256).astype(BF)


def weight(src, hs):
    return pl.pallas_call(
        weight_kernel,
        grid=(4,),
        in_specs=[
            pl.BlockSpec((4, 16, 4, 16, HD), lambda i: (0, 0, 0, 0, 0)),
            pl.BlockSpec((512, 256), lambda i: (0, i)),
        ],
        out_specs=pl.BlockSpec((16, 1, 64, 256), lambda i: (0, i, 0, 0)),
        out_shape=jax.ShapeDtypeStruct((16, 4, 64, 256), BF),
        scratch_shapes=[pltpu.VMEM((512, 1024), BF)],
        compiler_params=pltpu.CompilerParams(vmem_limit_bytes=40 * MIB),
        name="weight",
    )(src, hs)


def reduce_kernel(tile, grad, pair, mine, ring, part, last, cs, cr, xs, xr, zs, zr):
    d, c = lax.axis_index("dp"), lax.axis_index("ctx")
    zl, x, core = d // 8, (d // 2) % 4, d % 2
    z, y = c // 4, c % 4
    x_of = [(x + k) % 4 for k in range(4)]
    sibling = {"dp": d + 1 - 2 * core}
    on_x = lambda k: {"dp": zl * 8 + x_of[k] * 2 + core}
    zz = zl * 4 + z
    z_of = [(zz + k) % 8 for k in range(8)]
    on_z = lambda k: {"dp": (z_of[k] // 4) * 8 + x * 2 + core, "ctx": (z_of[k] % 4) * 4 + y}

    greet([sibling] + [on_x(k) for k in range(1, 4)] + [on_z(k) for k in range(1, 8)])

    order = [2, 1, 3, 0]
    swaps = [
        remote(tile.at[:, x_of[k], 1 - core], pair.at[:, x_of[k]], cs.at[k], cr.at[k], sibling) for k in order
    ]
    for copy in swaps:
        copy.start()
    sums = []
    for copy, k in zip(swaps, order):
        copy.wait_recv()
        for a in range(2):
            for b in range(4):
                mine[k, a, b] = (
                    tile[a, x_of[k], core, b].astype(F32) + pair[a, x_of[k], b].astype(F32)
                ).astype(BF)
        if k:
            sums.append(remote(mine.at[k], ring.at[k], xs.at[k], xr.at[k], on_x(k)))
            sums[-1].start()
    for copy in sums:
        copy.wait_recv()
    for a in range(2):
        for b in range(4):
            t = mine[0, a, b].astype(F32)
            for k in range(1, 4):
                t = t + ring[k, a, b].astype(F32)
            part[a * 4 + b] = t.astype(BF)
    ends = [remote(part.at[z_of[k]], last.at[k], zs.at[k], zr.at[k], on_z(k)) for k in range(1, 8)]
    for copy in ends:
        copy.start()
    for copy in ends:
        copy.wait_recv()
    t = part[zz].astype(F32)
    for k in range(1, 8):
        t = t + last[k].astype(F32)
    grad[...] = t * (1.0 / 16.0)
    for copy in swaps + sums + ends:
        copy.wait_send()


def reduce_tiles(tile):
    return pl.pallas_call(
        reduce_kernel,
        in_specs=[vm()],
        out_specs=vm(),
        out_shape=jax.ShapeDtypeStruct((64, 256), F32),
        scratch_shapes=[
            pltpu.VMEM((2, 4, 4, 64, 256), BF),
            pltpu.VMEM((4, 2, 4, 64, 256), BF),
            pltpu.VMEM((4, 2, 4, 64, 256), BF),
            pltpu.VMEM((8, 64, 256), BF),
            pltpu.VMEM((8, 64, 256), BF),
            pltpu.SemaphoreType.DMA((4,)),
            pltpu.SemaphoreType.DMA((4,)),
            pltpu.SemaphoreType.DMA((4,)),
            pltpu.SemaphoreType.DMA((4,)),
            pltpu.SemaphoreType.DMA((8,)),
            pltpu.SemaphoreType.DMA((8,)),
        ],
        compiler_params=pltpu.CompilerParams(collective_id=2, has_side_effects=True, vmem_limit_bytes=40 * MIB),
        name="reduce_tiles",
    )(tile)


def finish_kernel(att, qg, pg, w1, w2, att_o, qg_o, hg_o, pgm):
    step = pl.program_id(0)

    @pl.when(step == 0)
    def _():
        for g in range(4):
            block = pg[g].astype(F32)
            pgm[:, g * HD : (g + 1) * HD] = block[:, :8, :].reshape(128, HD).astype(BF)
            pgm[:, (4 + g) * HD : (5 + g) * HD] = block[:, 8:, :].reshape(128, HD).astype(BF)
            for source, target in ((att, att_o), (qg, qg_o)):
                block = source[g].reshape(16, 32, HD).astype(F32)
                for h in range(4):
                    cols = slice((g * 4 + h) * HD, (g * 4 + h + 1) * HD)
                    target[:, cols] = block[:, h * 8 : h * 8 + 8, :].reshape(128, HD).astype(BF)

    hg_o[...] = (
        jnp.dot(pgm[:, :512], w1[...], preferred_element_type=F32)
        + jnp.dot(pgm[:, 512:], w2[...], preferred_element_type=F32)
    ).astype(BF)


def finish(att, qg, pg, w):
    full = lambda *shape: pl.BlockSpec(shape, lambda i: (0,) * len(shape))
    return pl.pallas_call(
        finish_kernel,
        grid=(8,),
        in_specs=[
            full(4, 512, HD), full(4, 512, HD), full(4, 16, 16, HD),
            pl.BlockSpec((512, 512), lambda i: (0, i)), pl.BlockSpec((512, 512), lambda i: (1, i)),
        ],
        out_specs=[full(128, 2048), full(128, 2048), pl.BlockSpec((128, 512), lambda i: (0, i))],
        out_shape=[
            jax.ShapeDtypeStruct((128, 2048), BF),
            jax.ShapeDtypeStruct((128, 2048), BF),
            jax.ShapeDtypeStruct((128, 4096), BF),
        ],
        scratch_shapes=[pltpu.VMEM((128, 1024), BF)],
        compiler_params=pltpu.CompilerParams(vmem_limit_bytes=40 * MIB),
        name="finish",
    )(att, qg, pg, w, w)


def body(hidden_rows, query_rows, out_grad, projection, packing_plan, document_ids):
    d, c = lax.axis_index("dp"), lax.axis_index("ctx")
    z = c // 4
    near_cos, near_sin = angle_tables(c * 128 + d * 8 + jnp.arange(8, dtype=jnp.int32))
    cos, sin = angle_tables(z * 512 + jnp.arange(512, dtype=jnp.int32))
    documents = document_ids[0]
    own_documents = lax.dynamic_slice_in_dim(documents, z * 512, 512)
    first = jnp.sum((documents[None, :] < own_documents[:, None]).astype(jnp.int32), axis=1)
    info = jnp.concatenate([(z * 512)[None].astype(jnp.int32), first[::128]])
    first_rows = jnp.broadcast_to(first.reshape(64, 1, 8), (64, 4, 8)).reshape(4, 1, 512)

    kv, qs, gs, hs = project(packing_plan, hidden_rows, query_rows, out_grad, projection, near_cos, near_sin)
    kv_all, q_rx, g_rx, h_rx = spread(kv, qs, gs, hs)
    att, qg, dkv = attend(
        info, q_rx.reshape(2048, HD), g_rx.reshape(2048, HD), kv_all.reshape(256, 16, HD), first_rows
    )
    att_rx, qg_rx, pg_rx, src = collect(att.reshape(4, 512, HD), qg.reshape(4, 512, HD), dkv, cos, sin)
    tile = weight(src, h_rx.reshape(512, 1024))
    attended, query_grad, hidden_grad = finish(att_rx, qg_rx, pg_rx, projection)
    weight_grad = reduce_tiles(tile.reshape(2, 4, 2, 4, 64, 256))
    return attended, query_grad, hidden_grad, weight_grad


def solution(mesh):
    rows = P(("dp", "ctx"), None)
    return jax.shard_map(
        body,
        mesh=mesh,
        in_specs=(rows, rows, rows, P(), rows, P("dp", None)),
        out_specs=(rows, rows, rows, P("dp", "ctx")),
        check_vma=False,
    )
```

```python
import functools
import math

import jax
import jax.numpy as jnp
from jax import lax
from jax.experimental import pallas as pl
from jax.experimental.pallas import tpu as pltpu
from jax.sharding import PartitionSpec as P

ROPE_BASE = 500000.0
MASK_VALUE = -1e30
HD = 128
SCALE = HD ** (-0.5)
BF = jnp.bfloat16
F32 = jnp.float32
MESH = pl.DeviceIdType.MESH
KB = 256
MIB = 1024 * 1024


def vm():
    return pl.BlockSpec(memory_space=pltpu.VMEM)


def rows_dot(a, b):
    return lax.dot_general(a, b, (((1,), (1,)), ((), ())), preferred_element_type=F32)


def cols_dot(a, b):
    return lax.dot_general(a, b, (((0,), (0,)), ((), ())), preferred_element_type=F32)


def angle_tables(positions):
    half = HD // 2
    exponent = jnp.arange(half, dtype=F32) * (-2.0 * math.log(ROPE_BASE) / HD)
    angles = positions.astype(F32)[:, None] * jnp.exp(exponent)[None, :]
    cosine, sine = jnp.cos(angles), jnp.sin(angles)
    return jnp.concatenate([cosine, cosine], 1), jnp.concatenate([-sine, sine], 1)


def remote(src, dst, send, recv, device):
    return pltpu.make_async_remote_copy(
        src_ref=src, dst_ref=dst, send_sem=send, recv_sem=recv, device_id=device, device_id_type=MESH
    )


def greet(devices):
    barrier = pltpu.get_barrier_semaphore()
    for device in devices:
        pl.semaphore_signal(barrier, inc=1, device_id=device, device_id_type=MESH)
    pl.semaphore_wait(barrier, len(devices))


def front_kernel(
    plan, cos, sin, x_h, q_h, og_h, w_h, kv_all, q_rx, g_rx, h_rx,
    x, q, og, w, xp, acc, kv_s, q_s, g_s, h_s, kv1, q1, ls, ss, rs, ys, yr, zs, zr,
):
    d, c = lax.axis_index("dp"), lax.axis_index("ctx")
    z, y = c // 4, c % 4
    dp_of = [(d + k) % 16 for k in range(16)]
    y_of = [(y + k) % 4 for k in range(4)]
    on_dp = lambda k: {"dp": dp_of[k]}
    on_y = lambda k: {"ctx": z * 4 + y_of[k]}
    up, down = {"ctx": (c + 4) % 16}, {"ctx": (c + 12) % 16}
    z_up, z_down = (z + 1) % 4, (z + 3) % 4

    loads = [
        pltpu.make_async_copy(og_h, og, ls.at[0]),
        pltpu.make_async_copy(q_h, q, ls.at[1]),
        pltpu.make_async_copy(x_h, x, ls.at[2]),
    ]
    loads += [pltpu.make_async_copy(w_h.at[pl.ds(i * 256, 256)], w.at[i], ls.at[3 + i]) for i in range(4)]
    for copy in loads:
        copy.start()
    partners = [on_dp(k) for k in range(1, 16)] + [on_y(k) for k in range(1, 4)] + [up, down]
    barrier = pltpu.get_barrier_semaphore()
    for device in partners:
        pl.semaphore_signal(barrier, inc=1, device_id=device, device_id_type=MESH)

    loads[0].wait()
    for i in range(8):
        grads = [og[:, h * HD : (h + 1) * HD].astype(F32).reshape(16, 8, HD) for h in (2 * i, 2 * i + 1)]
        g_s[i // 2, :, (i % 2) * 16 : (i % 2 + 1) * 16, :] = jnp.concatenate(grads, 1).astype(BF)
    pl.semaphore_wait(barrier, len(partners))
    grads = [remote(g_s.at[y_of[k]], g_rx.at[y], ys.at[0, k], yr.at[0, k], on_y(k)) for k in range(1, 4)]
    for copy in grads:
        copy.start()

    pick = (lax.broadcasted_iota(jnp.int32, (128, 128), 0) == plan[...]).astype(F32).astype(BF)
    loads[1].wait()
    for i in range(8):
        parts = [
            jnp.dot(pick, q[:, h * HD : (h + 1) * HD], preferred_element_type=F32).reshape(16, 8, HD)
            for h in (2 * i, 2 * i + 1)
        ]
        q_s[:, i * 16 : (i + 1) * 16, :] = jnp.concatenate(parts, 1).astype(BF)
    q_first = [remote(q_s.at[dp_of[k]], q1.at[d], ss.at[1, k], rs.at[1, k], on_dp(k)) for k in range(1, 16)]
    for copy in q_first:
        copy.start()

    loads[2].wait()
    for j in range(16):
        sl = slice(j * 256, (j + 1) * 256)
        t = jnp.dot(pick, x[:, sl], preferred_element_type=F32).astype(BF)
        xp[:, sl] = t
        h_s[j % 4, :, (j // 4) * 256 : (j // 4 + 1) * 256] = t
    for i in range(4):
        loads[3 + i].wait()
        acc[i] = rows_dot(xp[...], w[i])
    for g in range(4):
        sl = slice((g % 2) * HD, (g % 2 + 1) * HD)
        k = acc[g // 2][:, sl]
        v = acc[2 + g // 2][:, sl]
        k3 = k.reshape(16, 8, HD)
        r3 = pltpu.roll(k, 64, 1).reshape(16, 8, HD)
        rot = k3 * cos[...][None] + r3 * sin[...][None]
        kv_s[:, g * 16 : (g + 1) * 16, :] = jnp.concatenate([rot, v.reshape(16, 8, HD)], 1).astype(BF)
    kv_first = [remote(kv_s.at[dp_of[k]], kv1.at[d], ss.at[0, k], rs.at[0, k], on_dp(k)) for k in range(1, 16)]
    for copy in kv_first:
        copy.start()
    kv1[d] = kv_s[d]
    q1[d] = q_s[d]
    g_rx[y] = g_s[y]
    h_rx[y] = h_s[y]

    for copy in q_first:
        copy.wait_recv()
    heads = lambda k: pl.ds(pl.multiple_of(y_of[k] * 32, 32), 32)
    q_second = [remote(q1.at[:, heads(k), :], q_rx.at[y], ys.at[2, k], yr.at[2, k], on_y(k)) for k in range(1, 4)]
    for copy in q_second:
        copy.start()
    q_rx[y] = q1[:, heads(0), :]

    for copy in kv_first:
        copy.wait_recv()
    group = lambda k: pl.ds(pl.multiple_of(y_of[k] * 16, 16), 16)
    kv_second = [
        remote(kv1.at[:, group(k), :], kv_all.at[z, y], ys.at[1, k], yr.at[1, k], on_y(k)) for k in range(1, 4)
    ]
    for copy in kv_second:
        copy.start()
    kv_all[z, y] = kv1[:, group(0), :]

    chunk = [(y + 4 - t) % 4 for t in range(4)]
    own_up, own_down = [], []
    for t in range(4):
        if t:
            kv_second[t - 1].wait_recv()
        place = kv_all.at[z, chunk[t]]
        own_up.append(remote(place, place, zs.at[0, t], zr.at[0, t], up))
        own_down.append(remote(place, place, zs.at[1, t], zr.at[1, t], down))
        own_up[t].start()
        own_down[t].start()
    hidden = [remote(h_s.at[y_of[k]], h_rx.at[y], ys.at[3, k], yr.at[3, k], on_y(k)) for k in range(1, 4)]
    for copy in hidden:
        copy.start()

    passed = []
    for t in range(4):
        if t % 2 == 0:
            own_up[t].wait_recv()
            place = kv_all.at[z_down, chunk[t]]
            passed.append(remote(place, place, zs.at[2, t], zr.at[2, t], up))
        else:
            own_down[t].wait_recv()
            place = kv_all.at[z_up, chunk[t]]
            passed.append(remote(place, place, zs.at[2, t], zr.at[2, t], down))
        passed[t].start()
    for t in range(4):
        (own_down if t % 2 == 0 else own_up)[t].wait_recv()
    for copy in passed + q_second + grads + hidden:
        copy.wait_recv()
    for copy in kv_first + grads + q_first + kv_second + own_up + own_down + q_second + hidden + passed:
        copy.wait_send()


def front(plan, cos, sin, x, q, og, w):
    hbm = pl.BlockSpec(memory_space=pltpu.HBM)
    return pl.pallas_call(
        front_kernel,
        in_specs=[vm()] * 3 + [hbm] * 4,
        out_specs=[vm()] * 4,
        out_shape=[
            jax.ShapeDtypeStruct((4, 4, 16, 16, HD), BF),
            jax.ShapeDtypeStruct((4, 16, 32, HD), BF),
            jax.ShapeDtypeStruct((4, 16, 32, HD), BF),
            jax.ShapeDtypeStruct((4, 128, 1024), BF),
        ],
        scratch_shapes=[
            pltpu.VMEM((128, 4096), BF),
            pltpu.VMEM((128, 2048), BF),
            pltpu.VMEM((128, 2048), BF),
            pltpu.VMEM((4, 256, 4096), BF),
            pltpu.VMEM((128, 4096), BF),
            pltpu.VMEM((4, 128, 256), F32),
            pltpu.VMEM((16, 64, HD), BF),
            pltpu.VMEM((16, 128, HD), BF),
            pltpu.VMEM((4, 16, 32, HD), BF),
            pltpu.VMEM((4, 128, 1024), BF),
            pltpu.VMEM((16, 64, HD), BF),
            pltpu.VMEM((16, 128, HD), BF),
            pltpu.SemaphoreType.DMA((7,)),
            pltpu.SemaphoreType.DMA((2, 16)),
            pltpu.SemaphoreType.DMA((2, 16)),
            pltpu.SemaphoreType.DMA((4, 4)),
            pltpu.SemaphoreType.DMA((4, 4)),
            pltpu.SemaphoreType.DMA((3, 4)),
            pltpu.SemaphoreType.DMA((3, 4)),
        ],
        compiler_params=pltpu.CompilerParams(collective_id=0, has_side_effects=True, vmem_limit_bytes=40 * MIB),
        name="front",
    )(plan, cos, sin, x, q, og, w)


def attend_kernel(info, q, og, kv, first, att, qg, dkv, keys, vals, keys_t, vals_t, dk, dv, sc, gp, q_t, og_t, out_t, grad_t):
    base = info[0]
    for i in range(4):
        block = kv[pl.ds(i * 64, 64)].astype(F32)
        rows = slice(i * 512, (i + 1) * 512)
        k = block[:, :8, :].reshape(512, HD)
        v = block[:, 8:, :].reshape(512, HD)
        keys[rows, :] = k.astype(BF)
        vals[rows, :] = v.astype(BF)
        keys_t[:, rows] = k.T.astype(BF)
        vals_t[:, rows] = v.T.astype(BF)
    keys[2048:, :] = jnp.zeros((128, HD), BF)
    vals[2048:, :] = jnp.zeros((128, HD), BF)
    keys_t[:, 2048:] = jnp.zeros((HD, 128), BF)
    vals_t[:, 2048:] = jnp.zeros((HD, 128), BF)
    dk[...] = jnp.zeros_like(dk)
    dv[...] = jnp.zeros_like(dv)
    fold = SCALE * math.log2(math.e)

    def query_block(qb, carry):
        here = pl.ds(pl.multiple_of(qb * 512, 512), 512)
        q_t[...] = q[here, :].astype(F32).T.astype(BF)
        og_t[...] = og[here, :].astype(F32).T.astype(BF)
        start = (info[1 + qb] // 128) * 128
        count = (base + (qb + 1) * 128 - start + KB - 1) // KB
        lane = lax.broadcasted_iota(jnp.int32, (1, 512), 1)
        position = base + qb * 128 + (lane // 32) * 8 + lane % 8
        lowest = first[qb]
        out_t[...] = jnp.zeros_like(out_t)
        grad_t[...] = jnp.zeros_like(grad_t)

        def eights(t):
            return t.reshape(KB // 8, 8, 512)

        def scores(i, top):
            at = pl.multiple_of(start + i * KB, 128)
            rows = pl.ds(at, KB)
            s = jnp.dot(keys[rows, :], q_t[...], preferred_element_type=F32)
            index = at + lax.broadcasted_iota(jnp.int32, (KB, 512), 0)
            s = jnp.where((index <= position) & (index >= lowest), s, MASK_VALUE)
            sc[rows, :] = s
            return jnp.maximum(top, jnp.max(eights(s), axis=0))

        top = lax.fori_loop(0, count, scores, jnp.full((8, 512), MASK_VALUE, F32))
        top = jnp.max(top, axis=0, keepdims=True) * fold

        def expo(i, sums):
            rows = pl.ds(pl.multiple_of(start + i * KB, 128), KB)
            e = jnp.exp2(sc[rows, :] * fold - top)
            grad = jnp.dot(vals[rows, :], og_t[...], preferred_element_type=F32)
            sc[rows, :] = e
            gp[rows, :] = grad
            return sums[0] + jnp.sum(eights(e), axis=0), sums[1] + jnp.sum(eights(e * grad), axis=0)

        zero = jnp.zeros((8, 512), F32)
        total, product = lax.fori_loop(0, count, expo, (zero, zero))
        inverse = 1.0 / jnp.sum(total, axis=0, keepdims=True)
        delta = jnp.sum(product, axis=0, keepdims=True) * inverse

        def both(i, c):
            at = pl.multiple_of(start + i * KB, 128)
            rows = pl.ds(at, KB)
            p = sc[rows, :] * inverse
            rounded = p.astype(BF)
            ds = (p * (gp[rows, :] - delta)).astype(BF)
            dv[rows, :] += jnp.dot(rounded, og[here, :], preferred_element_type=F32)
            dk[rows, :] += jnp.dot(ds, q[here, :], preferred_element_type=F32)
            out_t[...] += jnp.dot(vals_t[:, rows], rounded, preferred_element_type=F32)
            grad_t[...] += jnp.dot(keys_t[:, rows], ds, preferred_element_type=F32)
            return c

        lax.fori_loop(0, count, both, 0)
        att[here, :] = out_t[...].T.astype(BF)
        qg[here, :] = (grad_t[...] * SCALE).T.astype(BF)
        return carry

    lax.fori_loop(0, 4, query_block, 0)
    for i in range(4):
        rows = slice(i * 512, (i + 1) * 512)
        dkv[i, 0] = (dk[rows, :] * SCALE).astype(BF)
        dkv[i, 1] = dv[rows, :].astype(BF)


def attend(info, q, og, kv, first):
    return pl.pallas_call(
        attend_kernel,
        in_specs=[pl.BlockSpec(memory_space=pltpu.SMEM)] + [vm()] * 4,
        out_specs=[vm()] * 3,
        scratch_shapes=[
            pltpu.VMEM((2176, HD), BF),
            pltpu.VMEM((2176, HD), BF),
            pltpu.VMEM((HD, 2176), BF),
            pltpu.VMEM((HD, 2176), BF),
            pltpu.VMEM((2176, HD), F32),
            pltpu.VMEM((2176, HD), F32),
            pltpu.VMEM((2176, 512), F32),
            pltpu.VMEM((2176, 512), F32),
            pltpu.VMEM((HD, 512), BF),
            pltpu.VMEM((HD, 512), BF),
            pltpu.VMEM((HD, 512), F32),
            pltpu.VMEM((HD, 512), F32),
        ],
        out_shape=[
            jax.ShapeDtypeStruct((2048, HD), BF),
            jax.ShapeDtypeStruct((2048, HD), BF),
            jax.ShapeDtypeStruct((4, 2, 512, HD), BF),
        ],
        compiler_params=pltpu.CompilerParams(vmem_limit_bytes=48 * MIB),
        name="attend",
    )(info, q, og, kv, first)


def back_kernel(
    att, qg, dkv, cos, sin, hs, w_h, att_o, qg_o, hg_o, grad,
    att_rx, qg_rx, hop, mid, fin, own_a, own_b, src, pg_rx, hsr, pgh, w, tile, pair, mine, ring, part, last,
    ws, ys, yr, zs, zr, ss, rs, cs, cr, xs, xr, es, er,
):
    d, c = lax.axis_index("dp"), lax.axis_index("ctx")
    z, y = c // 4, c % 4
    zl, x, core = d // 8, (d // 2) % 4, d % 2
    dp_of = [(d + k) % 16 for k in range(16)]
    y_of = [(y + k) % 4 for k in range(4)]
    x_of = [(x + k) % 4 for k in range(4)]
    z_of = [(z + k) % 4 for k in range(4)]
    on_dp = lambda k: {"dp": dp_of[k]}
    on_y = lambda k: {"ctx": z * 4 + y_of[k]}
    on_x = lambda k: {"dp": zl * 8 + x_of[k] * 2 + core}
    on_z = lambda lo, k: {"dp": lo * 8 + x * 2 + core, "ctx": z_of[k] * 4 + y}
    sibling = {"dp": d + 1 - 2 * core}
    up, down = {"ctx": (c + 4) % 16}, {"ctx": (c + 12) % 16}
    z_up, z_far, z_down = z_of[1], z_of[2], z_of[3]
    low, high = pl.ds(0, 256), pl.ds(256, 256)

    weights = pltpu.make_async_copy(w_h, w, ws)
    weights.start()
    greet(
        [on_dp(k) for k in range(1, 16)]
        + [on_y(k) for k in range(1, 4)]
        + [on_z(zl, k) for k in range(1, 4)]
        + [on_z(1 - zl, k) for k in range(1, 4)]
    )

    far, near = {}, {}
    for s in (1, 0):
        far[s] = [
            remote(dkv.at[z_far, s, low], hop.at[s, 0], zs.at[s, 0], zr.at[s, 0], down),
            remote(dkv.at[z_far, s, high], hop.at[s, 1], zs.at[s, 1], zr.at[s, 1], up),
        ]
        near[s] = [
            remote(dkv.at[z_down, s, high], fin.at[s, 0, high], zs.at[s, 2], zr.at[s, 2], down),
            remote(dkv.at[z_up, s, low], fin.at[s, 0, low], zs.at[s, 3], zr.at[s, 3], up),
        ]
        for copy in far[s] + near[s]:
            copy.start()
    outs = []
    for i, (a, b) in enumerate(((att, att_rx), (qg, qg_rx))):
        for k in range(1, 4):
            outs.append(remote(a.at[y_of[k]], b.at[y], ys.at[i, k], yr.at[i, k], on_y(k)))
            outs[-1].start()
        b[y] = a[y]

    sums = {}

    def pass_on(s):
        far[s][0].wait_recv()
        mid[s, 0] = (hop[s, 0].astype(F32) + dkv[z_down, s, 0:256, :].astype(F32)).astype(BF)
        first = remote(mid.at[s, 0], fin.at[s, 1, low], zs.at[s, 4], zr.at[s, 4], down)
        first.start()
        far[s][1].wait_recv()
        mid[s, 1] = (hop[s, 1].astype(F32) + dkv[z_up, s, 256:512, :].astype(F32)).astype(BF)
        second = remote(mid.at[s, 1], fin.at[s, 1, high], zs.at[s, 5], zr.at[s, 5], up)
        second.start()
        sums[s] = [first, second]

    exchanged, packed = {}, {}

    def complete(s):
        for copy in near[s] + sums[s]:
            copy.wait_recv()
        for i in range(2):
            pieces = []
            for j in (2 * i, 2 * i + 1):
                sl = slice(j * 128, (j + 1) * 128)
                t = dkv[z, s, sl, :].astype(F32) + fin[s, 0, sl, :].astype(F32) + fin[s, 1, sl, :].astype(F32)
                t = t.astype(BF).astype(F32)
                if s == 0:
                    t = t * cos[sl, :] - pltpu.roll(t, 64, 1) * sin[sl, :]
                own_b[s, j] = t.astype(BF)
                pieces.append(t.reshape(16, 8, HD))
            own_a[s, :, i * 16 : (i + 1) * 16, :] = jnp.concatenate(pieces, 1).astype(BF)
        exchanged[s] = [
            remote(own_a.at[s, dp_of[k]], src.at[s, y, d], ss.at[s, k], rs.at[s, k], on_dp(k)) for k in range(1, 16)
        ]
        for copy in exchanged[s]:
            copy.start()
        packed[s] = [
            remote(own_b.at[s, y_of[k]], pg_rx.at[s, y], ys.at[2 + s, k], yr.at[2 + s, k], on_y(k))
            for k in range(1, 4)
        ]
        for copy in packed[s]:
            copy.start()
        src[s, y, d] = own_a[s, d]
        pg_rx[s, y] = own_b[s, y]

    gathered = {}

    def gather(s):
        for copy in exchanged[s]:
            copy.wait_recv()
        gathered[s] = [
            remote(src.at[s, y], src.at[s, y], ys.at[4 + s, k], yr.at[4 + s, k], on_y(k)) for k in range(1, 4)
        ]
        for copy in gathered[s]:
            copy.start()

    swaps = {0: [], 1: []}
    order = [2, 1, 3, 0]

    def multiply(s):
        for copy in gathered[s]:
            copy.wait_recv()
        for k in order:
            g = x_of[k]
            rows = src[s, g].reshape(512, HD)
            for j in range(4):
                sl = slice(j * 256, (j + 1) * 256)
                tile[s, k, :, :, sl] = cols_dot(rows, hsr[:, sl]).reshape(2, 64, 256).astype(BF)
            copy = remote(tile.at[s, k, 1 - core], pair.at[s, k], cs.at[s, k], cr.at[s, k], sibling)
            copy.start()
            swaps[s].append(copy)

    rings = {0: [], 1: []}

    def add_pair(s):
        for copy, k in zip(swaps[s], order):
            copy.wait_recv()
            for j in range(4):
                sl = slice(j * 256, (j + 1) * 256)
                mine[s, k, :, sl] = (
                    tile[s, k, core, :, sl].astype(F32) + pair[s, k, :, sl].astype(F32)
                ).astype(BF)
            if k:
                copy = remote(mine.at[s, k], ring.at[s, k], xs.at[s, k], xr.at[s, k], on_x(k))
                copy.start()
                rings[s].append(copy)

    same = lambda s, k: remote(part.at[s, z_of[k]], last.at[k], es.at[k], er.at[k], on_z(s, k))
    other = lambda s, k: remote(part.at[s, z_of[k]], last.at[4 + k], es.at[4 + k], er.at[4 + k], on_z(s, k))

    def add_ring(s):
        for copy in rings[s]:
            copy.wait_recv()
        for j in range(4):
            sl = slice(j * 256, (j + 1) * 256)
            t = mine[s, 0, :, sl].astype(F32)
            for k in range(1, 4):
                t = t + ring[s, k, :, sl].astype(F32)
            part[s, j] = t.astype(BF)

        @pl.when(zl == s)
        def _():
            for k in range(1, 4):
                same(s, k).start()

        @pl.when(zl != s)
        def _():
            for k in range(4):
                other(s, k).start()

    for j in range(4):
        sl = slice(j * 256, (j + 1) * 256)
        pieces = [hs[i, :, sl].astype(F32).reshape(16, 8, 256) for i in range(4)]
        hsr[:, sl] = jnp.concatenate(pieces, 1).reshape(512, 256).astype(BF)
    pass_on(1)
    pass_on(0)
    complete(1)
    for copy in outs:
        copy.wait_recv()
    for g in range(4):
        for source, target in ((att_rx, att_o), (qg_rx, qg_o)):
            block = source[g].reshape(16, 32, HD).astype(F32)
            for h in range(4):
                cols = slice((g * 4 + h) * HD, (g * 4 + h + 1) * HD)
                target[:, cols] = block[:, h * 8 : h * 8 + 8, :].reshape(128, HD).astype(BF)
    gather(1)
    complete(0)
    multiply(1)
    gather(0)
    add_pair(1)
    multiply(0)
    add_ring(1)
    for s in (1, 0):
        for copy in packed[s]:
            copy.wait_recv()
        for g in range(4):
            cols = slice(s * 512 + g * HD, s * 512 + (g + 1) * HD)
            pgh[:, cols] = pg_rx[s, g]
    add_pair(0)
    weights.wait()
    for j in range(8):
        sl = slice(j * 512, (j + 1) * 512)
        hg_o[:, sl] = jnp.dot(pgh[...], w[:, sl], preferred_element_type=F32).astype(BF)
    add_ring(0)
    ends = [same(zl, k) for k in range(1, 4)] + [other(1 - zl, k) for k in range(4)]
    for copy in ends:
        copy.wait_recv()
    t = part[zl, z].astype(F32)
    for k in range(1, 8):
        t = t + last[k].astype(F32)
    grad[...] = t * (1.0 / 16.0)
    for s in (0, 1):
        for copy in far[s] + near[s] + sums[s] + exchanged[s] + packed[s] + gathered[s] + swaps[s] + rings[s]:
            copy.wait_send()
    for copy in outs + ends:
        copy.wait_send()


def back(att, qg, dkv, cos, sin, hs, w):
    dma = pltpu.SemaphoreType.DMA
    return pl.pallas_call(
        back_kernel,
        in_specs=[vm()] * 6 + [pl.BlockSpec(memory_space=pltpu.HBM)],
        out_specs=[vm()] * 4,
        out_shape=[
            jax.ShapeDtypeStruct((128, 2048), BF),
            jax.ShapeDtypeStruct((128, 2048), BF),
            jax.ShapeDtypeStruct((128, 4096), BF),
            jax.ShapeDtypeStruct((64, 256), F32),
        ],
        scratch_shapes=[
            pltpu.VMEM((4, 512, HD), BF),
            pltpu.VMEM((4, 512, HD), BF),
            pltpu.VMEM((2, 2, 256, HD), BF),
            pltpu.VMEM((2, 2, 256, HD), BF),
            pltpu.VMEM((2, 2, 512, HD), BF),
            pltpu.VMEM((2, 16, 32, HD), BF),
            pltpu.VMEM((2, 4, 128, HD), BF),
            pltpu.VMEM((2, 4, 16, 32, HD), BF),
            pltpu.VMEM((2, 4, 128, HD), BF),
            pltpu.VMEM((512, 1024), BF),
            pltpu.VMEM((128, 1024), BF),
            pltpu.VMEM((1024, 4096), BF),
            pltpu.VMEM((2, 4, 2, 64, 1024), BF),
            pltpu.VMEM((2, 4, 64, 1024), BF),
            pltpu.VMEM((2, 4, 64, 1024), BF),
            pltpu.VMEM((2, 4, 64, 1024), BF),
            pltpu.VMEM((2, 4, 64, 256), BF),
            pltpu.VMEM((8, 64, 256), BF),
            dma, dma((6, 4)), dma((6, 4)), dma((2, 6)), dma((2, 6)), dma((2, 16)), dma((2, 16)),
            dma((2, 4)), dma((2, 4)), dma((2, 4)), dma((2, 4)), dma((8,)), dma((8,)),
        ],
        compiler_params=pltpu.CompilerParams(collective_id=1, has_side_effects=True, vmem_limit_bytes=48 * MIB),
        name="back",
    )(att, qg, dkv, cos, sin, hs, w)


def body(hidden_rows, query_rows, out_grad, projection, packing_plan, document_ids):
    d, c = lax.axis_index("dp"), lax.axis_index("ctx")
    z = c // 4
    near_cos, near_sin = angle_tables(c * 128 + d * 8 + jnp.arange(8, dtype=jnp.int32))
    cos, sin = angle_tables(z * 512 + jnp.arange(512, dtype=jnp.int32))
    documents = document_ids[0]
    own_documents = lax.dynamic_slice_in_dim(documents, z * 512, 512)
    first = jnp.sum((documents[None, :] < own_documents[:, None]).astype(jnp.int32), axis=1)
    info = jnp.concatenate([(z * 512)[None].astype(jnp.int32), first[::128]])
    first_rows = jnp.broadcast_to(first.reshape(64, 1, 8), (64, 4, 8)).reshape(4, 1, 512)

    kv_all, q_rx, g_rx, h_rx = front(
        packing_plan, near_cos, near_sin, hidden_rows, query_rows, out_grad, projection
    )
    att, qg, dkv = attend(
        info, q_rx.reshape(2048, HD), g_rx.reshape(2048, HD), kv_all.reshape(256, 16, HD), first_rows
    )
    attended, query_grad, hidden_grad, weight_grad = back(
        att.reshape(4, 512, HD), qg.reshape(4, 512, HD), dkv, cos, sin, h_rx, projection
    )
    return attended, query_grad, hidden_grad, weight_grad


def solution(mesh):
    rows = P(("dp", "ctx"), None)
    return jax.shard_map(
        body,
        mesh=mesh,
        in_specs=(rows, rows, rows, P(), rows, P("dp", None)),
        out_specs=(rows, rows, rows, P("dp", "ctx")),
        check_vma=False,
    )
```

```python
import functools
import math

import jax
import jax.numpy as jnp
from jax import lax
from jax.experimental import pallas as pl
from jax.experimental.pallas import tpu as pltpu
from jax.sharding import PartitionSpec as P

ROPE_BASE = 500000.0
MASK_VALUE = -1e30
HD = 128
SCALE = HD ** (-0.5)
BF = jnp.bfloat16
F32 = jnp.float32
MESH = pl.DeviceIdType.MESH
KB = 256
MIB = 1024 * 1024


def vm():
    return pl.BlockSpec(memory_space=pltpu.VMEM)


def rows_dot(a, b):
    return lax.dot_general(a, b, (((1,), (1,)), ((), ())), preferred_element_type=F32)


def cols_dot(a, b):
    return lax.dot_general(a, b, (((0,), (0,)), ((), ())), preferred_element_type=F32)


def angle_tables(positions):
    half = HD // 2
    exponent = jnp.arange(half, dtype=F32) * (-2.0 * math.log(ROPE_BASE) / HD)
    angles = positions.astype(F32)[:, None] * jnp.exp(exponent)[None, :]
    cosine, sine = jnp.cos(angles), jnp.sin(angles)
    return jnp.concatenate([cosine, cosine], 1), jnp.concatenate([-sine, sine], 1)


def turn(cos, sin, rows):
    c, s, c8, s8 = cos[rows, :], sin[rows, :], cos[64:, :], sin[64:, :]
    return c * c8 - s * s8, s * c8 + c * s8


def remote(src, dst, send, recv, device):
    return pltpu.make_async_remote_copy(
        src_ref=src, dst_ref=dst, send_sem=send, recv_sem=recv, device_id=device, device_id_type=MESH
    )


def greet(devices):
    barrier = pltpu.get_barrier_semaphore()
    for device in devices:
        pl.semaphore_signal(barrier, inc=1, device_id=device, device_id_type=MESH)
    pl.semaphore_wait(barrier, len(devices))


def front_kernel(
    plan, documents, cos, sin, x_h, q_h, og_h, w_h, kv_all, q_rx, g_rx, h_rx, lowest,
    x, q, og, w, xp, acc, kv_s, q_s, g_s, h_s, kv1, q1, ls, ss, rs, ys, yr, zs, zr,
):
    d, c = lax.axis_index("dp"), lax.axis_index("ctx")
    z, y = c // 4, c % 4
    dp_of = [(d + k) % 16 for k in range(16)]
    y_of = [(y + k) % 4 for k in range(4)]
    on_dp = lambda k: {"dp": dp_of[k]}
    on_y = lambda k: {"ctx": z * 4 + y_of[k]}
    up, down = {"ctx": (c + 4) % 16}, {"ctx": (c + 12) % 16}
    z_up, z_down = (z + 1) % 4, (z + 3) % 4

    loads = [
        pltpu.make_async_copy(og_h, og, ls.at[0]),
        pltpu.make_async_copy(q_h, q, ls.at[1]),
        pltpu.make_async_copy(x_h, x, ls.at[2]),
    ]
    loads += [pltpu.make_async_copy(w_h.at[pl.ds(i * 256, 256)], w.at[i], ls.at[3 + i]) for i in range(4)]
    for copy in loads:
        copy.start()
    partners = [on_dp(k) for k in range(1, 16)] + [on_y(k) for k in range(1, 4)] + [up, down]
    barrier = pltpu.get_barrier_semaphore()
    for device in partners:
        pl.semaphore_signal(barrier, inc=1, device_id=device, device_id_type=MESH)

    loads[0].wait()
    for i in range(8):
        grads = [og[:, h * HD : (h + 1) * HD].astype(F32).reshape(16, 8, HD) for h in (2 * i, 2 * i + 1)]
        g_s[i // 2, :, (i % 2) * 16 : (i % 2 + 1) * 16, :] = jnp.concatenate(grads, 1).astype(BF)
    pl.semaphore_wait(barrier, len(partners))
    grads = [remote(g_s.at[y_of[k]], g_rx.at[y], ys.at[0, k], yr.at[0, k], on_y(k)) for k in range(1, 4)]
    for copy in grads:
        copy.start()

    pick = (lax.broadcasted_iota(jnp.int32, (128, 128), 0) == plan[...]).astype(F32).astype(BF)
    loads[1].wait()
    for i in range(8):
        parts = [
            jnp.dot(pick, q[:, h * HD : (h + 1) * HD], preferred_element_type=F32).reshape(16, 8, HD)
            for h in (2 * i, 2 * i + 1)
        ]
        q_s[:, i * 16 : (i + 1) * 16, :] = jnp.concatenate(parts, 1).astype(BF)
    q_first = [remote(q_s.at[dp_of[k]], q1.at[d], ss.at[1, k], rs.at[1, k], on_dp(k)) for k in range(1, 16)]
    for copy in q_first:
        copy.start()

    loads[2].wait()
    for j in range(16):
        sl = slice(j * 256, (j + 1) * 256)
        t = jnp.dot(pick, x[:, sl], preferred_element_type=F32).astype(BF)
        xp[:, sl] = t
        h_s[j % 4, :, (j // 4) * 256 : (j // 4 + 1) * 256] = t
    for i in range(4):
        loads[3 + i].wait()
        acc[i] = rows_dot(xp[...], w[i])
    near_cos, near_sin = turn(cos, sin, pl.ds(y * 16 + d, 1))
    for g in range(4):
        sl = slice((g % 2) * HD, (g % 2 + 1) * HD)
        k = acc[g // 2][:, sl]
        v = acc[2 + g // 2][:, sl]
        k3 = k.reshape(16, 8, HD)
        r3 = pltpu.roll(k, 64, 1).reshape(16, 8, HD)
        rot = k3 * near_cos[None] + r3 * near_sin[None]
        kv_s[:, g * 16 : (g + 1) * 16, :] = jnp.concatenate([rot, v.reshape(16, 8, HD)], 1).astype(BF)
    kv_first = [remote(kv_s.at[dp_of[k]], kv1.at[d], ss.at[0, k], rs.at[0, k], on_dp(k)) for k in range(1, 16)]
    for copy in kv_first:
        copy.start()
    kv1[d] = kv_s[d]
    q1[d] = q_s[d]
    g_rx[y] = g_s[y]
    h_rx[y] = h_s[y]

    lane = lax.broadcasted_iota(jnp.int32, (128, 512), 1)
    take = (lax.broadcasted_iota(jnp.int32, (128, 512), 0) == (lane // 32) * 8 + lane % 8).astype(F32).astype(BF)
    ids = documents[...].astype(F32)
    counts = [jnp.sum((ids < k).astype(F32), axis=1, keepdims=True) for k in range(1, 8)]
    for i in range(4):
        mine = documents[:, pl.ds(pl.multiple_of(z * 512 + i * 128, 128), 128)].astype(F32)
        mine = jnp.dot(jnp.broadcast_to(mine, (16, 128)).astype(BF), take, preferred_element_type=F32)[:1]
        begin = jnp.zeros((1, 512), F32)
        for k in range(1, 8):
            begin = jnp.where(mine == k, counts[k - 1], begin)
        lowest[i] = begin.astype(jnp.int32)

    for copy in q_first:
        copy.wait_recv()
    heads = lambda k: pl.ds(pl.multiple_of(y_of[k] * 32, 32), 32)
    q_second = [remote(q1.at[:, heads(k), :], q_rx.at[y], ys.at[2, k], yr.at[2, k], on_y(k)) for k in range(1, 4)]
    for copy in q_second:
        copy.start()
    q_rx[y] = q1[:, heads(0), :]

    for copy in kv_first:
        copy.wait_recv()
    group = lambda k: pl.ds(pl.multiple_of(y_of[k] * 16, 16), 16)
    kv_second = [
        remote(kv1.at[:, group(k), :], kv_all.at[z, y], ys.at[1, k], yr.at[1, k], on_y(k)) for k in range(1, 4)
    ]
    for copy in kv_second:
        copy.start()
    kv_all[z, y] = kv1[:, group(0), :]

    chunk = [(y + 4 - t) % 4 for t in range(4)]
    own_up, own_down = [], []
    for t in range(4):
        if t:
            kv_second[t - 1].wait_recv()
        place = kv_all.at[z, chunk[t]]
        own_up.append(remote(place, place, zs.at[0, t], zr.at[0, t], up))
        own_down.append(remote(place, place, zs.at[1, t], zr.at[1, t], down))
        own_up[t].start()
        own_down[t].start()
    hidden = [remote(h_s.at[y_of[k]], h_rx.at[y], ys.at[3, k], yr.at[3, k], on_y(k)) for k in range(1, 4)]
    for copy in hidden:
        copy.start()

    passed = []
    for t in range(4):
        if t % 2 == 0:
            own_up[t].wait_recv()
            place = kv_all.at[z_down, chunk[t]]
            passed.append(remote(place, place, zs.at[2, t], zr.at[2, t], up))
        else:
            own_down[t].wait_recv()
            place = kv_all.at[z_up, chunk[t]]
            passed.append(remote(place, place, zs.at[2, t], zr.at[2, t], down))
        passed[t].start()
    for t in range(4):
        (own_down if t % 2 == 0 else own_up)[t].wait_recv()
    for copy in passed + q_second + grads + hidden:
        copy.wait_recv()
    for copy in kv_first + grads + q_first + kv_second + own_up + own_down + q_second + hidden + passed:
        copy.wait_send()


def front(plan, documents, cos, sin, x, q, og, w):
    hbm = pl.BlockSpec(memory_space=pltpu.HBM)
    return pl.pallas_call(
        front_kernel,
        in_specs=[vm()] * 4 + [hbm] * 4,
        out_specs=[vm()] * 5,
        out_shape=[
            jax.ShapeDtypeStruct((4, 4, 16, 16, HD), BF),
            jax.ShapeDtypeStruct((4, 16, 32, HD), BF),
            jax.ShapeDtypeStruct((4, 16, 32, HD), BF),
            jax.ShapeDtypeStruct((4, 128, 1024), BF),
            jax.ShapeDtypeStruct((4, 1, 512), jnp.int32),
        ],
        scratch_shapes=[
            pltpu.VMEM((128, 4096), BF),
            pltpu.VMEM((128, 2048), BF),
            pltpu.VMEM((128, 2048), BF),
            pltpu.VMEM((4, 256, 4096), BF),
            pltpu.VMEM((128, 4096), BF),
            pltpu.VMEM((4, 128, 256), F32),
            pltpu.VMEM((16, 64, HD), BF),
            pltpu.VMEM((16, 128, HD), BF),
            pltpu.VMEM((4, 16, 32, HD), BF),
            pltpu.VMEM((4, 128, 1024), BF),
            pltpu.VMEM((16, 64, HD), BF),
            pltpu.VMEM((16, 128, HD), BF),
            pltpu.SemaphoreType.DMA((7,)),
            pltpu.SemaphoreType.DMA((2, 16)),
            pltpu.SemaphoreType.DMA((2, 16)),
            pltpu.SemaphoreType.DMA((4, 4)),
            pltpu.SemaphoreType.DMA((4, 4)),
            pltpu.SemaphoreType.DMA((3, 4)),
            pltpu.SemaphoreType.DMA((3, 4)),
        ],
        compiler_params=pltpu.CompilerParams(collective_id=0, has_side_effects=True, vmem_limit_bytes=49 * MIB),
        name="front",
    )(plan, documents, cos, sin, x, q, og, w)


def attend_kernel(q, og, kv, first, att, qg, dkv, keys, vals, keys_t, vals_t, dk, dv, sc, gp, q_t, og_t, out_t, grad_t):
    base = (lax.axis_index("ctx") // 4) * 512
    for i in range(4):
        block = kv[pl.ds(i * 64, 64)].astype(F32)
        rows = slice(i * 512, (i + 1) * 512)
        k = block[:, :8, :].reshape(512, HD)
        v = block[:, 8:, :].reshape(512, HD)
        keys[rows, :] = k.astype(BF)
        vals[rows, :] = v.astype(BF)
        keys_t[:, rows] = k.T.astype(BF)
        vals_t[:, rows] = v.T.astype(BF)
    keys[2048:, :] = jnp.zeros((128, HD), BF)
    vals[2048:, :] = jnp.zeros((128, HD), BF)
    keys_t[:, 2048:] = jnp.zeros((HD, 128), BF)
    vals_t[:, 2048:] = jnp.zeros((HD, 128), BF)
    dk[...] = jnp.zeros_like(dk)
    dv[...] = jnp.zeros_like(dv)
    fold = SCALE * math.log2(math.e)

    def query_block(qb, carry):
        here = pl.ds(pl.multiple_of(qb * 512, 512), 512)
        q_t[...] = q[here, :].astype(F32).T.astype(BF)
        og_t[...] = og[here, :].astype(F32).T.astype(BF)
        lowest = first[qb]
        start = (jnp.min(lowest) // 128) * 128
        count = (base + (qb + 1) * 128 - start + KB - 1) // KB
        lane = lax.broadcasted_iota(jnp.int32, (1, 512), 1)
        position = base + qb * 128 + (lane // 32) * 8 + lane % 8
        out_t[...] = jnp.zeros_like(out_t)
        grad_t[...] = jnp.zeros_like(grad_t)

        def eights(t):
            return t.reshape(KB // 8, 8, 512)

        def scores(i, top):
            at = pl.multiple_of(start + i * KB, 128)
            rows = pl.ds(at, KB)
            s = jnp.dot(keys[rows, :], q_t[...], preferred_element_type=F32)
            index = at + lax.broadcasted_iota(jnp.int32, (KB, 512), 0)
            s = jnp.where((index <= position) & (index >= lowest), s, MASK_VALUE)
            sc[rows, :] = s
            return jnp.maximum(top, jnp.max(eights(s), axis=0))

        top = lax.fori_loop(0, count, scores, jnp.full((8, 512), MASK_VALUE, F32))
        top = jnp.max(top, axis=0, keepdims=True) * fold

        def expo(i, sums):
            rows = pl.ds(pl.multiple_of(start + i * KB, 128), KB)
            e = jnp.exp2(sc[rows, :] * fold - top)
            grad = jnp.dot(vals[rows, :], og_t[...], preferred_element_type=F32)
            sc[rows, :] = e
            gp[rows, :] = grad
            return sums[0] + jnp.sum(eights(e), axis=0), sums[1] + jnp.sum(eights(e * grad), axis=0)

        zero = jnp.zeros((8, 512), F32)
        total, product = lax.fori_loop(0, count, expo, (zero, zero))
        inverse = 1.0 / jnp.sum(total, axis=0, keepdims=True)
        delta = jnp.sum(product, axis=0, keepdims=True) * inverse

        def both(i, c):
            at = pl.multiple_of(start + i * KB, 128)
            rows = pl.ds(at, KB)
            p = sc[rows, :] * inverse
            rounded = p.astype(BF)
            ds = (p * (gp[rows, :] - delta)).astype(BF)
            dv[rows, :] += jnp.dot(rounded, og[here, :], preferred_element_type=F32)
            dk[rows, :] += jnp.dot(ds, q[here, :], preferred_element_type=F32)
            out_t[...] += jnp.dot(vals_t[:, rows], rounded, preferred_element_type=F32)
            grad_t[...] += jnp.dot(keys_t[:, rows], ds, preferred_element_type=F32)
            return c

        lax.fori_loop(0, count, both, 0)
        att[here, :] = out_t[...].T.astype(BF)
        qg[here, :] = (grad_t[...] * SCALE).T.astype(BF)
        return carry

    lax.fori_loop(0, 4, query_block, 0)
    for i in range(4):
        rows = slice(i * 512, (i + 1) * 512)
        dkv[i, 0] = (dk[rows, :] * SCALE).astype(BF)
        dkv[i, 1] = dv[rows, :].astype(BF)


def attend(q, og, kv, first):
    return pl.pallas_call(
        attend_kernel,
        in_specs=[vm()] * 4,
        out_specs=[vm()] * 3,
        scratch_shapes=[
            pltpu.VMEM((2176, HD), BF),
            pltpu.VMEM((2176, HD), BF),
            pltpu.VMEM((HD, 2176), BF),
            pltpu.VMEM((HD, 2176), BF),
            pltpu.VMEM((2176, HD), F32),
            pltpu.VMEM((2176, HD), F32),
            pltpu.VMEM((2176, 512), F32),
            pltpu.VMEM((2176, 512), F32),
            pltpu.VMEM((HD, 512), BF),
            pltpu.VMEM((HD, 512), BF),
            pltpu.VMEM((HD, 512), F32),
            pltpu.VMEM((HD, 512), F32),
        ],
        out_shape=[
            jax.ShapeDtypeStruct((2048, HD), BF),
            jax.ShapeDtypeStruct((2048, HD), BF),
            jax.ShapeDtypeStruct((4, 2, 512, HD), BF),
        ],
        compiler_params=pltpu.CompilerParams(vmem_limit_bytes=48 * MIB),
        name="attend",
    )(q, og, kv, first)


def back_kernel(
    att, qg, dkv, cos, sin, hs, w_h, att_o, qg_o, hg_o, grad,
    att_rx, qg_rx, hop, mid, fin, own_a, own_b, src, pg_rx, hsr, pgh, w, tile, pair, mine, ring, part, last,
    ws, ys, yr, zs, zr, ss, rs, cs, cr, xs, xr, es, er,
):
    d, c = lax.axis_index("dp"), lax.axis_index("ctx")
    z, y = c // 4, c % 4
    zl, x, core = d // 8, (d // 2) % 4, d % 2
    dp_of = [(d + k) % 16 for k in range(16)]
    y_of = [(y + k) % 4 for k in range(4)]
    x_of = [(x + k) % 4 for k in range(4)]
    z_of = [(z + k) % 4 for k in range(4)]
    on_dp = lambda k: {"dp": dp_of[k]}
    on_y = lambda k: {"ctx": z * 4 + y_of[k]}
    on_x = lambda k: {"dp": zl * 8 + x_of[k] * 2 + core}
    on_z = lambda lo, k: {"dp": lo * 8 + x * 2 + core, "ctx": z_of[k] * 4 + y}
    sibling = {"dp": d + 1 - 2 * core}
    up, down = {"ctx": (c + 4) % 16}, {"ctx": (c + 12) % 16}
    z_up, z_far, z_down = z_of[1], z_of[2], z_of[3]
    low, high = pl.ds(0, 256), pl.ds(256, 256)

    weights = pltpu.make_async_copy(w_h, w, ws)
    weights.start()
    greet(
        [on_dp(k) for k in range(1, 16)]
        + [on_y(k) for k in range(1, 4)]
        + [on_z(zl, k) for k in range(1, 4)]
        + [on_z(1 - zl, k) for k in range(1, 4)]
    )

    far, near = {}, {}
    for s in (1, 0):
        far[s] = [
            remote(dkv.at[z_far, s, low], hop.at[s, 0], zs.at[s, 0], zr.at[s, 0], down),
            remote(dkv.at[z_far, s, high], hop.at[s, 1], zs.at[s, 1], zr.at[s, 1], up),
        ]
        near[s] = [
            remote(dkv.at[z_down, s, high], fin.at[s, 0, high], zs.at[s, 2], zr.at[s, 2], down),
            remote(dkv.at[z_up, s, low], fin.at[s, 0, low], zs.at[s, 3], zr.at[s, 3], up),
        ]
        for copy in far[s] + near[s]:
            copy.start()
    outs = []
    for i, (a, b) in enumerate(((att, att_rx), (qg, qg_rx))):
        for k in range(1, 4):
            outs.append(remote(a.at[y_of[k]], b.at[y], ys.at[i, k], yr.at[i, k], on_y(k)))
            outs[-1].start()
        b[y] = a[y]

    sums = {}

    def pass_on(s):
        far[s][0].wait_recv()
        mid[s, 0] = (hop[s, 0].astype(F32) + dkv[z_down, s, 0:256, :].astype(F32)).astype(BF)
        first = remote(mid.at[s, 0], fin.at[s, 1, low], zs.at[s, 4], zr.at[s, 4], down)
        first.start()
        far[s][1].wait_recv()
        mid[s, 1] = (hop[s, 1].astype(F32) + dkv[z_up, s, 256:512, :].astype(F32)).astype(BF)
        second = remote(mid.at[s, 1], fin.at[s, 1, high], zs.at[s, 5], zr.at[s, 5], up)
        second.start()
        sums[s] = [first, second]

    exchanged, packed = {}, {}

    def complete(s):
        for copy in near[s] + sums[s]:
            copy.wait_recv()
        for i in range(2):
            pieces = []
            for j in (2 * i, 2 * i + 1):
                sl = slice(j * 128, (j + 1) * 128)
                t = dkv[z, s, sl, :].astype(F32) + fin[s, 0, sl, :].astype(F32) + fin[s, 1, sl, :].astype(F32)
                t = t.astype(BF).astype(F32)
                if s == 0:
                    swapped = pltpu.roll(t, 64, 1)
                    turned = []
                    for a in range(16):
                        rows = slice(a * 8, (a + 1) * 8)
                        c8, s8 = turn(cos, sin, slice(j * 16 + a, j * 16 + a + 1))
                        turned.append(t[rows, :] * c8 - swapped[rows, :] * s8)
                    t = jnp.concatenate(turned, 0)
                own_b[s, j] = t.astype(BF)
                pieces.append(t.reshape(16, 8, HD))
            own_a[s, :, i * 16 : (i + 1) * 16, :] = jnp.concatenate(pieces, 1).astype(BF)
        exchanged[s] = [
            remote(own_a.at[s, dp_of[k]], src.at[s, y, d], ss.at[s, k], rs.at[s, k], on_dp(k)) for k in range(1, 16)
        ]
        for copy in exchanged[s]:
            copy.start()
        packed[s] = [
            remote(own_b.at[s, y_of[k]], pg_rx.at[s, y], ys.at[2 + s, k], yr.at[2 + s, k], on_y(k))
            for k in range(1, 4)
        ]
        for copy in packed[s]:
            copy.start()
        src[s, y, d] = own_a[s, d]
        pg_rx[s, y] = own_b[s, y]

    gathered = {}

    def gather(s):
        for copy in exchanged[s]:
            copy.wait_recv()
        gathered[s] = [
            remote(src.at[s, y], src.at[s, y], ys.at[4 + s, k], yr.at[4 + s, k], on_y(k)) for k in range(1, 4)
        ]
        for copy in gathered[s]:
            copy.start()

    swaps = {0: [], 1: []}
    order = [2, 1, 3, 0]

    def multiply(s):
        for copy in gathered[s]:
            copy.wait_recv()
        for k in order:
            g = x_of[k]
            rows = src[s, g].reshape(512, HD)
            for j in range(4):
                sl = slice(j * 256, (j + 1) * 256)
                tile[s, k, :, :, sl] = cols_dot(rows, hsr[:, sl]).reshape(2, 64, 256).astype(BF)
            copy = remote(tile.at[s, k, 1 - core], pair.at[s, k], cs.at[s, k], cr.at[s, k], sibling)
            copy.start()
            swaps[s].append(copy)

    rings = {0: [], 1: []}

    def add_pair(s):
        for copy, k in zip(swaps[s], order):
            copy.wait_recv()
            for j in range(4):
                sl = slice(j * 256, (j + 1) * 256)
                mine[s, k, :, sl] = (
                    tile[s, k, core, :, sl].astype(F32) + pair[s, k, :, sl].astype(F32)
                ).astype(BF)
            if k:
                copy = remote(mine.at[s, k], ring.at[s, k], xs.at[s, k], xr.at[s, k], on_x(k))
                copy.start()
                rings[s].append(copy)

    same = lambda s, k: remote(part.at[s, z_of[k]], last.at[k], es.at[k], er.at[k], on_z(s, k))
    other = lambda s, k: remote(part.at[s, z_of[k]], last.at[4 + k], es.at[4 + k], er.at[4 + k], on_z(s, k))

    def add_ring(s):
        for copy in rings[s]:
            copy.wait_recv()
        for j in range(4):
            sl = slice(j * 256, (j + 1) * 256)
            t = mine[s, 0, :, sl].astype(F32)
            for k in range(1, 4):
                t = t + ring[s, k, :, sl].astype(F32)
            part[s, j] = t.astype(BF)

        @pl.when(zl == s)
        def _():
            for k in range(1, 4):
                same(s, k).start()

        @pl.when(zl != s)
        def _():
            for k in range(4):
                other(s, k).start()

    for j in range(4):
        sl = slice(j * 256, (j + 1) * 256)
        pieces = [hs[i, :, sl].astype(F32).reshape(16, 8, 256) for i in range(4)]
        hsr[:, sl] = jnp.concatenate(pieces, 1).reshape(512, 256).astype(BF)
    pass_on(1)
    pass_on(0)
    complete(1)
    for copy in outs:
        copy.wait_recv()
    for g in range(4):
        for source, target in ((att_rx, att_o), (qg_rx, qg_o)):
            block = source[g].reshape(16, 32, HD).astype(F32)
            for h in range(4):
                cols = slice((g * 4 + h) * HD, (g * 4 + h + 1) * HD)
                target[:, cols] = block[:, h * 8 : h * 8 + 8, :].reshape(128, HD).astype(BF)
    complete(0)
    gather(1)
    gather(0)
    multiply(1)
    add_pair(1)
    multiply(0)
    add_ring(1)
    for s in (1, 0):
        for copy in packed[s]:
            copy.wait_recv()
        for g in range(4):
            cols = slice(s * 512 + g * HD, s * 512 + (g + 1) * HD)
            pgh[:, cols] = pg_rx[s, g]
    add_pair(0)
    weights.wait()
    for j in range(8):
        sl = slice(j * 512, (j + 1) * 512)
        hg_o[:, sl] = jnp.dot(pgh[...], w[:, sl], preferred_element_type=F32).astype(BF)
    add_ring(0)
    ends = [same(zl, k) for k in range(1, 4)] + [other(1 - zl, k) for k in range(4)]
    for copy in ends:
        copy.wait_recv()
    t = part[zl, z].astype(F32)
    for k in range(1, 8):
        t = t + last[k].astype(F32)
    grad[...] = t * (1.0 / 16.0)
    for s in (0, 1):
        for copy in far[s] + near[s] + sums[s] + exchanged[s] + packed[s] + gathered[s] + swaps[s] + rings[s]:
            copy.wait_send()
    for copy in outs + ends:
        copy.wait_send()


def back(att, qg, dkv, cos, sin, hs, w):
    dma = pltpu.SemaphoreType.DMA
    return pl.pallas_call(
        back_kernel,
        in_specs=[vm()] * 6 + [pl.BlockSpec(memory_space=pltpu.HBM)],
        out_specs=[vm()] * 4,
        out_shape=[
            jax.ShapeDtypeStruct((128, 2048), BF),
            jax.ShapeDtypeStruct((128, 2048), BF),
            jax.ShapeDtypeStruct((128, 4096), BF),
            jax.ShapeDtypeStruct((64, 256), F32),
        ],
        scratch_shapes=[
            pltpu.VMEM((4, 512, HD), BF),
            pltpu.VMEM((4, 512, HD), BF),
            pltpu.VMEM((2, 2, 256, HD), BF),
            pltpu.VMEM((2, 2, 256, HD), BF),
            pltpu.VMEM((2, 2, 512, HD), BF),
            pltpu.VMEM((2, 16, 32, HD), BF),
            pltpu.VMEM((2, 4, 128, HD), BF),
            pltpu.VMEM((2, 4, 16, 32, HD), BF),
            pltpu.VMEM((2, 4, 128, HD), BF),
            pltpu.VMEM((512, 1024), BF),
            pltpu.VMEM((128, 1024), BF),
            pltpu.VMEM((1024, 4096), BF),
            pltpu.VMEM((2, 4, 2, 64, 1024), BF),
            pltpu.VMEM((2, 4, 64, 1024), BF),
            pltpu.VMEM((2, 4, 64, 1024), BF),
            pltpu.VMEM((2, 4, 64, 1024), BF),
            pltpu.VMEM((2, 4, 64, 256), BF),
            pltpu.VMEM((8, 64, 256), BF),
            dma, dma((6, 4)), dma((6, 4)), dma((2, 6)), dma((2, 6)), dma((2, 16)), dma((2, 16)),
            dma((2, 4)), dma((2, 4)), dma((2, 4)), dma((2, 4)), dma((8,)), dma((8,)),
        ],
        compiler_params=pltpu.CompilerParams(collective_id=1, has_side_effects=True, vmem_limit_bytes=48 * MIB),
        name="back",
    )(att, qg, dkv, cos, sin, hs, w)


def store_kernel(a, b, c, e, a_o, b_o, c_o, e_o, sems):
    copies = [pltpu.make_async_copy(p, o, sems.at[i]) for i, (p, o) in enumerate(((a, a_o), (b, b_o), (c, c_o), (e, e_o)))]
    for copy in copies:
        copy.start()
    for copy in copies:
        copy.wait()


def store(*arrays):
    hbm = pl.BlockSpec(memory_space=pltpu.HBM)
    return pl.pallas_call(
        store_kernel,
        in_specs=[vm()] * 4,
        out_specs=[hbm] * 4,
        out_shape=[jax.ShapeDtypeStruct(a.shape, a.dtype) for a in arrays],
        scratch_shapes=[pltpu.SemaphoreType.DMA((4,))],
        compiler_params=pltpu.CompilerParams(vmem_limit_bytes=16 * MIB),
        name="store",
    )(*arrays)


def body(hidden_rows, query_rows, out_grad, projection, packing_plan, document_ids):
    z = lax.axis_index("ctx") // 4
    small = jnp.arange(8, dtype=jnp.int32)
    cos, sin = angle_tables(jnp.concatenate([z * 512 + jnp.arange(64, dtype=jnp.int32) * 8, small]))
    kv_all, q_rx, g_rx, h_rx, first = front(
        packing_plan, document_ids, cos, sin, hidden_rows, query_rows, out_grad, projection
    )
    att, qg, dkv = attend(
        q_rx.reshape(2048, HD), g_rx.reshape(2048, HD), kv_all.reshape(256, 16, HD), first
    )
    return store(*back(att.reshape(4, 512, HD), qg.reshape(4, 512, HD), dkv, cos, sin, h_rx, projection))


def solution(mesh):
    rows = P(("dp", "ctx"), None)
    return jax.shard_map(
        body,
        mesh=mesh,
        in_specs=(rows, rows, rows, P(), rows, P("dp", None)),
        out_specs=(rows, rows, rows, P("dp", "ctx")),
        check_vma=False,
    )
```

```python
import functools
import math

import jax
import jax.numpy as jnp
from jax import lax
from jax.experimental import pallas as pl
from jax.experimental.pallas import tpu as pltpu
from jax.sharding import PartitionSpec as P

ROPE_BASE = 500000.0
MASK_VALUE = -1e30
HD = 128
SCALE = HD ** (-0.5)
BF = jnp.bfloat16
F32 = jnp.float32
MESH = pl.DeviceIdType.MESH
KB = 256
MIB = 1024 * 1024


def vm():
    return pl.BlockSpec(memory_space=pltpu.VMEM)


def rows_dot(a, b):
    return lax.dot_general(a, b, (((1,), (1,)), ((), ())), preferred_element_type=F32)


def cols_dot(a, b):
    return lax.dot_general(a, b, (((0,), (0,)), ((), ())), preferred_element_type=F32)


def angle_tables(positions):
    half = HD // 2
    exponent = jnp.arange(half, dtype=F32) * (-2.0 * math.log(ROPE_BASE) / HD)
    angles = positions.astype(F32)[:, None] * jnp.exp(exponent)[None, :]
    cosine, sine = jnp.cos(angles), jnp.sin(angles)
    return jnp.concatenate([cosine, cosine], 1), jnp.concatenate([-sine, sine], 1)


def turn(cos, sin, rows):
    c, s, c8, s8 = cos[rows, :], sin[rows, :], cos[64:, :], sin[64:, :]
    return c * c8 - s * s8, s * c8 + c * s8


def remote(src, dst, send, recv, device):
    return pltpu.make_async_remote_copy(
        src_ref=src, dst_ref=dst, send_sem=send, recv_sem=recv, device_id=device, device_id_type=MESH
    )


def greet(devices):
    barrier = pltpu.get_barrier_semaphore()
    for device in devices:
        pl.semaphore_signal(barrier, inc=1, device_id=device, device_id_type=MESH)
    pl.semaphore_wait(barrier, len(devices))


def front_kernel(
    plan, documents, cos, sin, x_h, q_h, og_h, w_h, kv_all, q_rx, g_rx, h_rx, lowest,
    x, q, og, w, xp, acc, kv_s, q_s, g_s, h_s, kv1, q1, ls, ss, rs, ys, yr, zs, zr,
):
    d, c = lax.axis_index("dp"), lax.axis_index("ctx")
    z, y = c // 4, c % 4
    dp_of = [(d + k) % 16 for k in range(16)]
    y_of = [(y + k) % 4 for k in range(4)]
    on_dp = lambda k: {"dp": dp_of[k]}
    on_y = lambda k: {"ctx": z * 4 + y_of[k]}
    up, down = {"ctx": (c + 4) % 16}, {"ctx": (c + 12) % 16}
    z_up, z_down = (z + 1) % 4, (z + 3) % 4

    loads = [pltpu.make_async_copy(x_h, x, ls.at[2])]
    loads += [pltpu.make_async_copy(w_h.at[pl.ds(i * 256, 256)], w.at[i], ls.at[3 + i]) for i in range(4)]
    loads += [pltpu.make_async_copy(og_h, og, ls.at[0]), pltpu.make_async_copy(q_h, q, ls.at[1])]
    for copy in loads:
        copy.start()
    partners = [on_dp(k) for k in range(1, 16)] + [on_y(k) for k in range(1, 4)] + [up, down]
    barrier = pltpu.get_barrier_semaphore()
    for device in partners:
        pl.semaphore_signal(barrier, inc=1, device_id=device, device_id_type=MESH)

    pick = (lax.broadcasted_iota(jnp.int32, (128, 128), 0) == plan[...]).astype(F32).astype(BF)
    loads[0].wait()
    for j in range(16):
        sl = slice(j * 256, (j + 1) * 256)
        t = jnp.dot(pick, x[:, sl], preferred_element_type=F32).astype(BF)
        xp[:, sl] = t
        h_s[j % 4, :, (j // 4) * 256 : (j // 4 + 1) * 256] = t
    loads[5].wait()
    for i in range(8):
        grads = [og[:, h * HD : (h + 1) * HD].astype(F32).reshape(16, 8, HD) for h in (2 * i, 2 * i + 1)]
        g_s[i // 2, :, (i % 2) * 16 : (i % 2 + 1) * 16, :] = jnp.concatenate(grads, 1).astype(BF)
    pl.semaphore_wait(barrier, len(partners))
    grads = [remote(g_s.at[y_of[k]], g_rx.at[y], ys.at[0, k], yr.at[0, k], on_y(k)) for k in range(1, 4)]
    for copy in grads:
        copy.start()

    for i in range(4):
        loads[1 + i].wait()
        acc[i] = rows_dot(xp[...], w[i])
    near_cos, near_sin = turn(cos, sin, pl.ds(y * 16 + d, 1))
    for g in range(4):
        sl = slice((g % 2) * HD, (g % 2 + 1) * HD)
        k = acc[g // 2][:, sl]
        v = acc[2 + g // 2][:, sl]
        k3 = k.reshape(16, 8, HD)
        r3 = pltpu.roll(k, 64, 1).reshape(16, 8, HD)
        rot = k3 * near_cos[None] + r3 * near_sin[None]
        kv_s[:, g * 16 : (g + 1) * 16, :] = jnp.concatenate([rot, v.reshape(16, 8, HD)], 1).astype(BF)
    kv_first = [remote(kv_s.at[dp_of[k]], kv1.at[d], ss.at[0, k], rs.at[0, k], on_dp(k)) for k in range(1, 16)]
    for copy in kv_first:
        copy.start()

    loads[6].wait()
    for i in range(8):
        parts = [
            jnp.dot(pick, q[:, h * HD : (h + 1) * HD], preferred_element_type=F32).reshape(16, 8, HD)
            for h in (2 * i, 2 * i + 1)
        ]
        q_s[:, i * 16 : (i + 1) * 16, :] = jnp.concatenate(parts, 1).astype(BF)
    q_first = [remote(q_s.at[dp_of[k]], q1.at[d], ss.at[1, k], rs.at[1, k], on_dp(k)) for k in range(1, 16)]
    for copy in q_first:
        copy.start()
    hidden = [remote(h_s.at[y_of[k]], h_rx.at[y], ys.at[3, k], yr.at[3, k], on_y(k)) for k in (1, 3, 2)]
    hidden[0].start()
    hidden[1].start()
    kv1[d] = kv_s[d]
    q1[d] = q_s[d]
    g_rx[y] = g_s[y]
    h_rx[y] = h_s[y]

    for copy in kv_first:
        copy.wait_recv()
    group = lambda k: pl.ds(pl.multiple_of(y_of[k] * 16, 16), 16)
    kv_second = [
        remote(kv1.at[:, group(k), :], kv_all.at[z, y], ys.at[1, k], yr.at[1, k], on_y(k)) for k in range(1, 4)
    ]
    for copy in kv_second:
        copy.start()
    kv_all[z, y] = kv1[:, group(0), :]

    chunk = [(y + 4 - t) % 4 for t in range(4)]
    own_up, own_down = [], []
    for t in range(4):
        if t:
            kv_second[t - 1].wait_recv()
        place = kv_all.at[z, chunk[t]]
        own_up.append(remote(place, place, zs.at[0, t], zr.at[0, t], up))
        own_down.append(remote(place, place, zs.at[1, t], zr.at[1, t], down))
        own_up[t].start()
        own_down[t].start()

    for copy in q_first:
        copy.wait_recv()
    heads = lambda k: pl.ds(pl.multiple_of(y_of[k] * 32, 32), 32)
    q_second = [remote(q1.at[:, heads(k), :], q_rx.at[y], ys.at[2, k], yr.at[2, k], on_y(k)) for k in range(1, 4)]
    for copy in q_second:
        copy.start()
    hidden[2].start()
    q_rx[y] = q1[:, heads(0), :]

    passed = []
    for t in range(4):
        if t % 2 == 0:
            own_up[t].wait_recv()
            place = kv_all.at[z_down, chunk[t]]
            passed.append(remote(place, place, zs.at[2, t], zr.at[2, t], up))
        else:
            own_down[t].wait_recv()
            place = kv_all.at[z_up, chunk[t]]
            passed.append(remote(place, place, zs.at[2, t], zr.at[2, t], down))
        passed[t].start()
    for t in range(4):
        (own_down if t % 2 == 0 else own_up)[t].wait_recv()
    lane = lax.broadcasted_iota(jnp.int32, (128, 512), 1)
    take = (lax.broadcasted_iota(jnp.int32, (128, 512), 0) == (lane // 32) * 8 + lane % 8).astype(F32).astype(BF)
    ids = documents[...].astype(F32)
    counts = [jnp.sum((ids < k).astype(F32), axis=1, keepdims=True) for k in range(1, 8)]
    for i in range(4):
        mine = documents[:, pl.ds(pl.multiple_of(z * 512 + i * 128, 128), 128)].astype(F32)
        mine = jnp.dot(jnp.broadcast_to(mine, (16, 128)).astype(BF), take, preferred_element_type=F32)[:1]
        begin = jnp.zeros((1, 512), F32)
        for k in range(1, 8):
            begin = jnp.where(mine == k, counts[k - 1], begin)
        lowest[i] = begin.astype(jnp.int32)

    for copy in passed + q_second + grads + hidden:
        copy.wait_recv()
    for copy in kv_first + grads + q_first + kv_second + own_up + own_down + q_second + hidden + passed:
        copy.wait_send()


def front(plan, documents, cos, sin, x, q, og, w):
    hbm = pl.BlockSpec(memory_space=pltpu.HBM)
    return pl.pallas_call(
        front_kernel,
        in_specs=[vm()] * 4 + [hbm] * 4,
        out_specs=[vm()] * 5,
        out_shape=[
            jax.ShapeDtypeStruct((4, 4, 16, 16, HD), BF),
            jax.ShapeDtypeStruct((4, 16, 32, HD), BF),
            jax.ShapeDtypeStruct((4, 16, 32, HD), BF),
            jax.ShapeDtypeStruct((4, 128, 1024), BF),
            jax.ShapeDtypeStruct((4, 1, 512), jnp.int32),
        ],
        scratch_shapes=[
            pltpu.VMEM((128, 4096), BF),
            pltpu.VMEM((128, 2048), BF),
            pltpu.VMEM((128, 2048), BF),
            pltpu.VMEM((4, 256, 4096), BF),
            pltpu.VMEM((128, 4096), BF),
            pltpu.VMEM((4, 128, 256), F32),
            pltpu.VMEM((16, 64, HD), BF),
            pltpu.VMEM((16, 128, HD), BF),
            pltpu.VMEM((4, 16, 32, HD), BF),
            pltpu.VMEM((4, 128, 1024), BF),
            pltpu.VMEM((16, 64, HD), BF),
            pltpu.VMEM((16, 128, HD), BF),
            pltpu.SemaphoreType.DMA((7,)),
            pltpu.SemaphoreType.DMA((2, 16)),
            pltpu.SemaphoreType.DMA((2, 16)),
            pltpu.SemaphoreType.DMA((4, 4)),
            pltpu.SemaphoreType.DMA((4, 4)),
            pltpu.SemaphoreType.DMA((3, 4)),
            pltpu.SemaphoreType.DMA((3, 4)),
        ],
        compiler_params=pltpu.CompilerParams(collective_id=0, has_side_effects=True, vmem_limit_bytes=49 * MIB),
        name="front",
    )(plan, documents, cos, sin, x, q, og, w)


def attend_kernel(q, og, kv, first, att, qg, dkv, keys, vals, keys_t, vals_t, dk, dv, sc, gp, q_t, og_t, out_t, grad_t):
    base = (lax.axis_index("ctx") // 4) * 512
    for i in range(4):
        block = kv[pl.ds(i * 64, 64)].astype(F32)
        rows = slice(i * 512, (i + 1) * 512)
        k = block[:, :8, :].reshape(512, HD)
        v = block[:, 8:, :].reshape(512, HD)
        keys[rows, :] = k.astype(BF)
        vals[rows, :] = v.astype(BF)
        keys_t[:, rows] = k.T.astype(BF)
        vals_t[:, rows] = v.T.astype(BF)
    keys[2048:, :] = jnp.zeros((128, HD), BF)
    vals[2048:, :] = jnp.zeros((128, HD), BF)
    keys_t[:, 2048:] = jnp.zeros((HD, 128), BF)
    vals_t[:, 2048:] = jnp.zeros((HD, 128), BF)
    dk[...] = jnp.zeros_like(dk)
    dv[...] = jnp.zeros_like(dv)
    fold = SCALE * math.log2(math.e)

    def query_block(qb, carry):
        here = pl.ds(pl.multiple_of(qb * 512, 512), 512)
        q_t[...] = q[here, :].astype(F32).T.astype(BF)
        og_t[...] = og[here, :].astype(F32).T.astype(BF)
        lowest = first[qb]
        start = (jnp.min(lowest) // 128) * 128
        count = (base + (qb + 1) * 128 - start + KB - 1) // KB
        lane = lax.broadcasted_iota(jnp.int32, (1, 512), 1)
        position = base + qb * 128 + (lane // 32) * 8 + lane % 8
        out_t[...] = jnp.zeros_like(out_t)
        grad_t[...] = jnp.zeros_like(grad_t)

        def eights(t):
            return t.reshape(KB // 8, 8, 512)

        def scores(i, top):
            at = pl.multiple_of(start + i * KB, 128)
            rows = pl.ds(at, KB)
            s = jnp.dot(keys[rows, :], q_t[...], preferred_element_type=F32)
            index = at + lax.broadcasted_iota(jnp.int32, (KB, 512), 0)
            s = jnp.where((index <= position) & (index >= lowest), s, MASK_VALUE)
            sc[rows, :] = s
            return jnp.maximum(top, jnp.max(eights(s), axis=0))

        top = lax.fori_loop(0, count, scores, jnp.full((8, 512), MASK_VALUE, F32))
        top = jnp.max(top, axis=0, keepdims=True) * fold

        def expo(i, sums):
            rows = pl.ds(pl.multiple_of(start + i * KB, 128), KB)
            e = jnp.exp2(sc[rows, :] * fold - top)
            grad = jnp.dot(vals[rows, :], og_t[...], preferred_element_type=F32)
            sc[rows, :] = e
            gp[rows, :] = grad
            return sums[0] + jnp.sum(eights(e), axis=0), sums[1] + jnp.sum(eights(e * grad), axis=0)

        zero = jnp.zeros((8, 512), F32)
        total, product = lax.fori_loop(0, count, expo, (zero, zero))
        inverse = 1.0 / jnp.sum(total, axis=0, keepdims=True)
        delta = jnp.sum(product, axis=0, keepdims=True) * inverse

        def both(i, c):
            at = pl.multiple_of(start + i * KB, 128)
            rows = pl.ds(at, KB)
            p = sc[rows, :] * inverse
            rounded = p.astype(BF)
            ds = (p * (gp[rows, :] - delta)).astype(BF)
            dv[rows, :] += jnp.dot(rounded, og[here, :], preferred_element_type=F32)
            dk[rows, :] += jnp.dot(ds, q[here, :], preferred_element_type=F32)
            out_t[...] += jnp.dot(vals_t[:, rows], rounded, preferred_element_type=F32)
            grad_t[...] += jnp.dot(keys_t[:, rows], ds, preferred_element_type=F32)
            return c

        lax.fori_loop(0, count, both, 0)
        att[here, :] = out_t[...].T.astype(BF)
        qg[here, :] = (grad_t[...] * SCALE).T.astype(BF)
        return carry

    lax.fori_loop(0, 4, query_block, 0)
    for i in range(4):
        rows = slice(i * 512, (i + 1) * 512)
        dkv[i, 0] = (dk[rows, :] * SCALE).astype(BF)
        dkv[i, 1] = dv[rows, :].astype(BF)


def attend(q, og, kv, first):
    return pl.pallas_call(
        attend_kernel,
        in_specs=[vm()] * 4,
        out_specs=[vm()] * 3,
        scratch_shapes=[
            pltpu.VMEM((2176, HD), BF),
            pltpu.VMEM((2176, HD), BF),
            pltpu.VMEM((HD, 2176), BF),
            pltpu.VMEM((HD, 2176), BF),
            pltpu.VMEM((2176, HD), F32),
            pltpu.VMEM((2176, HD), F32),
            pltpu.VMEM((2176, 512), F32),
            pltpu.VMEM((2176, 512), F32),
            pltpu.VMEM((HD, 512), BF),
            pltpu.VMEM((HD, 512), BF),
            pltpu.VMEM((HD, 512), F32),
            pltpu.VMEM((HD, 512), F32),
        ],
        out_shape=[
            jax.ShapeDtypeStruct((2048, HD), BF),
            jax.ShapeDtypeStruct((2048, HD), BF),
            jax.ShapeDtypeStruct((4, 2, 512, HD), BF),
        ],
        compiler_params=pltpu.CompilerParams(vmem_limit_bytes=48 * MIB),
        name="attend",
    )(q, og, kv, first)


def back_kernel(
    att, qg, dkv, cos, sin, hs, w_h, att_o, qg_o, hg_o, grad,
    att_rx, qg_rx, hop, mid, fin, own_a, own_b, src, pg_rx, hsr, pgh, w, tile, pair, mine, ring, part, last,
    ws, ys, yr, zs, zr, ss, rs, cs, cr, xs, xr, es, er,
):
    d, c = lax.axis_index("dp"), lax.axis_index("ctx")
    z, y = c // 4, c % 4
    zl, x, core = d // 8, (d // 2) % 4, d % 2
    dp_of = [(d + k) % 16 for k in range(16)]
    y_of = [(y + k) % 4 for k in range(4)]
    x_of = [(x + k) % 4 for k in range(4)]
    z_of = [(z + k) % 4 for k in range(4)]
    on_dp = lambda k: {"dp": dp_of[k]}
    on_y = lambda k: {"ctx": z * 4 + y_of[k]}
    on_x = lambda k: {"dp": zl * 8 + x_of[k] * 2 + core}
    on_z = lambda lo, k: {"dp": lo * 8 + x * 2 + core, "ctx": z_of[k] * 4 + y}
    sibling = {"dp": d + 1 - 2 * core}
    up, down = {"ctx": (c + 4) % 16}, {"ctx": (c + 12) % 16}
    z_up, z_far, z_down = z_of[1], z_of[2], z_of[3]
    low, high = pl.ds(0, 256), pl.ds(256, 256)

    weights = pltpu.make_async_copy(w_h, w, ws)
    weights.start()
    greet(
        [on_dp(k) for k in range(1, 16)]
        + [on_y(k) for k in range(1, 4)]
        + [on_z(zl, k) for k in range(1, 4)]
        + [on_z(1 - zl, k) for k in range(1, 4)]
    )

    far, near = {}, {}
    for s in (1, 0):
        far[s] = [
            remote(dkv.at[z_far, s, low], hop.at[s, 0], zs.at[s, 0], zr.at[s, 0], down),
            remote(dkv.at[z_far, s, high], hop.at[s, 1], zs.at[s, 1], zr.at[s, 1], up),
        ]
        near[s] = [
            remote(dkv.at[z_down, s, high], fin.at[s, 0, high], zs.at[s, 2], zr.at[s, 2], down),
            remote(dkv.at[z_up, s, low], fin.at[s, 0, low], zs.at[s, 3], zr.at[s, 3], up),
        ]
    for copy in far[1] + near[1]:
        copy.start()
    outs = []
    for i, (a, b) in enumerate(((att, att_rx), (qg, qg_rx))):
        for k in range(1, 4):
            outs.append(remote(a.at[y_of[k]], b.at[y], ys.at[i, k], yr.at[i, k], on_y(k)))
            outs[-1].start()
        b[y] = a[y]

    sums = {}

    def pass_on(s):
        far[s][0].wait_recv()
        mid[s, 0] = (hop[s, 0].astype(F32) + dkv[z_down, s, 0:256, :].astype(F32)).astype(BF)
        first = remote(mid.at[s, 0], fin.at[s, 1, low], zs.at[s, 4], zr.at[s, 4], down)
        first.start()
        far[s][1].wait_recv()
        mid[s, 1] = (hop[s, 1].astype(F32) + dkv[z_up, s, 256:512, :].astype(F32)).astype(BF)
        second = remote(mid.at[s, 1], fin.at[s, 1, high], zs.at[s, 5], zr.at[s, 5], up)
        second.start()
        sums[s] = [first, second]

    exchanged, packed = {}, {}

    def complete(s):
        for copy in near[s] + sums[s]:
            copy.wait_recv()
        for i in range(2):
            pieces = []
            for j in (2 * i, 2 * i + 1):
                sl = slice(j * 128, (j + 1) * 128)
                t = dkv[z, s, sl, :].astype(F32) + fin[s, 0, sl, :].astype(F32) + fin[s, 1, sl, :].astype(F32)
                t = t.astype(BF).astype(F32)
                if s == 0:
                    swapped = pltpu.roll(t, 64, 1)
                    turned = []
                    for a in range(16):
                        rows = slice(a * 8, (a + 1) * 8)
                        c8, s8 = turn(cos, sin, slice(j * 16 + a, j * 16 + a + 1))
                        turned.append(t[rows, :] * c8 - swapped[rows, :] * s8)
                    t = jnp.concatenate(turned, 0)
                own_b[s, j] = t.astype(BF)
                pieces.append(t.reshape(16, 8, HD))
            own_a[s, :, i * 16 : (i + 1) * 16, :] = jnp.concatenate(pieces, 1).astype(BF)
        exchanged[s] = [
            remote(own_a.at[s, dp_of[k]], src.at[s, y, d], ss.at[s, k], rs.at[s, k], on_dp(k)) for k in range(1, 16)
        ]
        for copy in exchanged[s]:
            copy.start()
        packed[s] = [
            remote(own_b.at[s, y_of[k]], pg_rx.at[s, y], ys.at[2 + s, k], yr.at[2 + s, k], on_y(k))
            for k in range(1, 4)
        ]
        for copy in packed[s]:
            copy.start()
        src[s, y, d] = own_a[s, d]
        pg_rx[s, y] = own_b[s, y]

    gathered = {}

    def gather(s):
        for copy in exchanged[s]:
            copy.wait_recv()
        gathered[s] = [
            remote(src.at[s, y], src.at[s, y], ys.at[4 + s, k], yr.at[4 + s, k], on_y(k)) for k in range(1, 4)
        ]
        for copy in gathered[s]:
            copy.start()

    swaps = {0: [], 1: []}
    order = [2, 1, 3, 0]

    def multiply(s):
        for copy in gathered[s]:
            copy.wait_recv()
        for k in order:
            g = x_of[k]
            rows = src[s, g].reshape(512, HD)
            for j in range(4):
                sl = slice(j * 256, (j + 1) * 256)
                tile[s, k, :, :, sl] = cols_dot(rows, hsr[:, sl]).reshape(2, 64, 256).astype(BF)
            copy = remote(tile.at[s, k, 1 - core], pair.at[s, k], cs.at[s, k], cr.at[s, k], sibling)
            copy.start()
            swaps[s].append(copy)

    rings = {0: [], 1: []}

    def add_pair(s):
        for copy, k in zip(swaps[s], order):
            copy.wait_recv()
            for j in range(4):
                sl = slice(j * 256, (j + 1) * 256)
                mine[s, k, :, sl] = (
                    tile[s, k, core, :, sl].astype(F32) + pair[s, k, :, sl].astype(F32)
                ).astype(BF)
            if k:
                copy = remote(mine.at[s, k], ring.at[s, k], xs.at[s, k], xr.at[s, k], on_x(k))
                copy.start()
                rings[s].append(copy)

    same = lambda s, k: remote(part.at[s, z_of[k]], last.at[k], es.at[k], er.at[k], on_z(s, k))
    other = lambda s, k: remote(part.at[s, z_of[k]], last.at[4 + k], es.at[4 + k], er.at[4 + k], on_z(s, k))

    def add_ring(s):
        for copy in rings[s]:
            copy.wait_recv()
        for j in range(4):
            sl = slice(j * 256, (j + 1) * 256)
            t = mine[s, 0, :, sl].astype(F32)
            for k in range(1, 4):
                t = t + ring[s, k, :, sl].astype(F32)
            part[s, j] = t.astype(BF)

        @pl.when(zl == s)
        def _():
            for k in range(1, 4):
                same(s, k).start()

        @pl.when(zl != s)
        def _():
            for k in range(4):
                other(s, k).start()

    for j in range(4):
        sl = slice(j * 256, (j + 1) * 256)
        pieces = [hs[i, :, sl].astype(F32).reshape(16, 8, 256) for i in range(4)]
        hsr[:, sl] = jnp.concatenate(pieces, 1).reshape(512, 256).astype(BF)
    pass_on(1)
    for copy in far[0] + near[0]:
        copy.start()
    complete(1)
    pass_on(0)
    gather(1)
    for copy in outs:
        copy.wait_recv()
    for g in range(4):
        for source, target in ((att_rx, att_o), (qg_rx, qg_o)):
            block = source[g].reshape(16, 32, HD).astype(F32)
            for h in range(4):
                cols = slice((g * 4 + h) * HD, (g * 4 + h + 1) * HD)
                target[:, cols] = block[:, h * 8 : h * 8 + 8, :].reshape(128, HD).astype(BF)
    complete(0)
    multiply(1)
    gather(0)
    add_pair(1)
    multiply(0)
    add_ring(1)
    for s in (1, 0):
        for copy in packed[s]:
            copy.wait_recv()
        for g in range(4):
            cols = slice(s * 512 + g * HD, s * 512 + (g + 1) * HD)
            pgh[:, cols] = pg_rx[s, g]
    add_pair(0)
    weights.wait()
    for j in range(8):
        sl = slice(j * 512, (j + 1) * 512)
        hg_o[:, sl] = jnp.dot(pgh[...], w[:, sl], preferred_element_type=F32).astype(BF)
    add_ring(0)
    ends = [same(zl, k) for k in range(1, 4)] + [other(1 - zl, k) for k in range(4)]
    for copy in ends:
        copy.wait_recv()
    t = part[zl, z].astype(F32)
    for k in range(1, 8):
        t = t + last[k].astype(F32)
    grad[...] = t * (1.0 / 16.0)
    for s in (0, 1):
        for copy in far[s] + near[s] + sums[s] + exchanged[s] + packed[s] + gathered[s] + swaps[s] + rings[s]:
            copy.wait_send()
    for copy in outs + ends:
        copy.wait_send()


def back(att, qg, dkv, cos, sin, hs, w):
    dma = pltpu.SemaphoreType.DMA
    return pl.pallas_call(
        back_kernel,
        in_specs=[vm()] * 6 + [pl.BlockSpec(memory_space=pltpu.HBM)],
        out_specs=[vm()] * 4,
        out_shape=[
            jax.ShapeDtypeStruct((128, 2048), BF),
            jax.ShapeDtypeStruct((128, 2048), BF),
            jax.ShapeDtypeStruct((128, 4096), BF),
            jax.ShapeDtypeStruct((64, 256), F32),
        ],
        scratch_shapes=[
            pltpu.VMEM((4, 512, HD), BF),
            pltpu.VMEM((4, 512, HD), BF),
            pltpu.VMEM((2, 2, 256, HD), BF),
            pltpu.VMEM((2, 2, 256, HD), BF),
            pltpu.VMEM((2, 2, 512, HD), BF),
            pltpu.VMEM((2, 16, 32, HD), BF),
            pltpu.VMEM((2, 4, 128, HD), BF),
            pltpu.VMEM((2, 4, 16, 32, HD), BF),
            pltpu.VMEM((2, 4, 128, HD), BF),
            pltpu.VMEM((512, 1024), BF),
            pltpu.VMEM((128, 1024), BF),
            pltpu.VMEM((1024, 4096), BF),
            pltpu.VMEM((2, 4, 2, 64, 1024), BF),
            pltpu.VMEM((2, 4, 64, 1024), BF),
            pltpu.VMEM((2, 4, 64, 1024), BF),
            pltpu.VMEM((2, 4, 64, 1024), BF),
            pltpu.VMEM((2, 4, 64, 256), BF),
            pltpu.VMEM((8, 64, 256), BF),
            dma, dma((6, 4)), dma((6, 4)), dma((2, 6)), dma((2, 6)), dma((2, 16)), dma((2, 16)),
            dma((2, 4)), dma((2, 4)), dma((2, 4)), dma((2, 4)), dma((8,)), dma((8,)),
        ],
        compiler_params=pltpu.CompilerParams(collective_id=1, has_side_effects=True, vmem_limit_bytes=48 * MIB),
        name="back",
    )(att, qg, dkv, cos, sin, hs, w)


def store_kernel(a, b, c, e, a_o, b_o, c_o, e_o, sems):
    copies = [pltpu.make_async_copy(p, o, sems.at[i]) for i, (p, o) in enumerate(((a, a_o), (b, b_o), (c, c_o), (e, e_o)))]
    for copy in copies:
        copy.start()
    for copy in copies:
        copy.wait()


def store(*arrays):
    hbm = pl.BlockSpec(memory_space=pltpu.HBM)
    return pl.pallas_call(
        store_kernel,
        in_specs=[vm()] * 4,
        out_specs=[hbm] * 4,
        out_shape=[jax.ShapeDtypeStruct(a.shape, a.dtype) for a in arrays],
        scratch_shapes=[pltpu.SemaphoreType.DMA((4,))],
        compiler_params=pltpu.CompilerParams(vmem_limit_bytes=16 * MIB),
        name="store",
    )(*arrays)


def body(hidden_rows, query_rows, out_grad, projection, packing_plan, document_ids):
    z = lax.axis_index("ctx") // 4
    small = jnp.arange(8, dtype=jnp.int32)
    cos, sin = angle_tables(jnp.concatenate([z * 512 + jnp.arange(64, dtype=jnp.int32) * 8, small]))
    kv_all, q_rx, g_rx, h_rx, first = front(
        packing_plan, document_ids, cos, sin, hidden_rows, query_rows, out_grad, projection
    )
    att, qg, dkv = attend(
        q_rx.reshape(2048, HD), g_rx.reshape(2048, HD), kv_all.reshape(256, 16, HD), first
    )
    return store(*back(att.reshape(4, 512, HD), qg.reshape(4, 512, HD), dkv, cos, sin, h_rx, projection))


def solution(mesh):
    rows = P(("dp", "ctx"), None)
    return jax.shard_map(
        body,
        mesh=mesh,
        in_specs=(rows, rows, rows, P(), rows, P("dp", None)),
        out_specs=(rows, rows, rows, P("dp", "ctx")),
        check_vma=False,
    )
```

```python
import functools
import math

import jax
import jax.numpy as jnp
from jax import lax
from jax.experimental import pallas as pl
from jax.experimental.pallas import tpu as pltpu
from jax.sharding import PartitionSpec as P

ROPE_BASE = 500000.0
MASK_VALUE = -1e30
HD = 128
SCALE = HD ** (-0.5)
BF = jnp.bfloat16
F32 = jnp.float32
MESH = pl.DeviceIdType.MESH
MIB = 1024 * 1024


def vm():
    return pl.BlockSpec(memory_space=pltpu.VMEM)


def rows_dot(a, b):
    return lax.dot_general(a, b, (((1,), (1,)), ((), ())), preferred_element_type=F32)


def cols_dot(a, b):
    return lax.dot_general(a, b, (((0,), (0,)), ((), ())), preferred_element_type=F32)


def angle_tables(positions):
    half = HD // 2
    exponent = jnp.arange(half, dtype=F32) * (-2.0 * math.log(ROPE_BASE) / HD)
    angles = positions.astype(F32)[:, None] * jnp.exp(exponent)[None, :]
    cosine, sine = jnp.cos(angles), jnp.sin(angles)
    return jnp.concatenate([cosine, cosine], 1), jnp.concatenate([-sine, sine], 1)


def turn(cos, sin, rows):
    c, s, c8, s8 = cos[rows, :], sin[rows, :], cos[64:, :], sin[64:, :]
    return c * c8 - s * s8, s * c8 + c * s8


def remote(src, dst, send, recv, device):
    return pltpu.make_async_remote_copy(
        src_ref=src, dst_ref=dst, send_sem=send, recv_sem=recv, device_id=device, device_id_type=MESH
    )


def greet(devices):
    barrier = pltpu.get_barrier_semaphore()
    for device in devices:
        pl.semaphore_signal(barrier, inc=1, device_id=device, device_id_type=MESH)
    pl.semaphore_wait(barrier, len(devices))


def front_kernel(
    plan, documents, cos, sin, x_h, q_h, og_h, w_h, kv_all, q_rx, g_rx, h_rx, lowest,
    x, q, og, w, xp, acc, kv_s, q_s, g_s, h_s, kv1, q1, ls, ss, rs, ys, yr, zs, zr,
):
    d, c = lax.axis_index("dp"), lax.axis_index("ctx")
    z, y = c // 4, c % 4
    dp_of = [(d + k) % 16 for k in range(16)]
    y_of = [(y + k) % 4 for k in range(4)]
    on_dp = lambda k: {"dp": dp_of[k]}
    on_y = lambda k: {"ctx": z * 4 + y_of[k]}
    up, down = {"ctx": (c + 4) % 16}, {"ctx": (c + 12) % 16}
    z_up, z_down = (z + 1) % 4, (z + 3) % 4

    loads = [pltpu.make_async_copy(x_h, x, ls.at[2])]
    loads += [pltpu.make_async_copy(w_h.at[pl.ds(i * 256, 256)], w.at[i], ls.at[3 + i]) for i in range(4)]
    loads += [pltpu.make_async_copy(og_h, og, ls.at[0]), pltpu.make_async_copy(q_h, q, ls.at[1])]
    for copy in loads:
        copy.start()
    partners = [on_dp(k) for k in range(1, 16)] + [on_y(k) for k in range(1, 4)] + [up, down]
    barrier = pltpu.get_barrier_semaphore()
    for device in partners:
        pl.semaphore_signal(barrier, inc=1, device_id=device, device_id_type=MESH)

    pick = (lax.broadcasted_iota(jnp.int32, (128, 128), 0) == plan[...]).astype(F32).astype(BF)
    loads[0].wait()
    for j in range(16):
        sl = slice(j * 256, (j + 1) * 256)
        t = jnp.dot(pick, x[:, sl], preferred_element_type=F32).astype(BF)
        xp[:, sl] = t
        h_s[j % 4, :, (j // 4) * 256 : (j // 4 + 1) * 256] = t
    loads[5].wait()
    for i in range(8):
        grads = [og[:, h * HD : (h + 1) * HD].astype(F32).reshape(16, 8, HD) for h in (2 * i, 2 * i + 1)]
        g_s[i // 2, :, (i % 2) * 16 : (i % 2 + 1) * 16, :] = jnp.concatenate(grads, 1).astype(BF)
    pl.semaphore_wait(barrier, len(partners))
    grads = [remote(g_s.at[y_of[k]], g_rx.at[y], ys.at[0, k], yr.at[0, k], on_y(k)) for k in range(1, 4)]
    for copy in grads:
        copy.start()

    for i in range(4):
        loads[1 + i].wait()
        acc[i] = rows_dot(xp[...], w[i])
    near_cos, near_sin = turn(cos, sin, pl.ds(y * 16 + d, 1))
    for g in range(4):
        sl = slice((g % 2) * HD, (g % 2 + 1) * HD)
        k = acc[g // 2][:, sl]
        v = acc[2 + g // 2][:, sl]
        k3 = k.reshape(16, 8, HD)
        r3 = pltpu.roll(k, 64, 1).reshape(16, 8, HD)
        rot = k3 * near_cos[None] + r3 * near_sin[None]
        kv_s[:, g * 16 : (g + 1) * 16, :] = jnp.concatenate([rot, v.reshape(16, 8, HD)], 1).astype(BF)
    kv_first = [remote(kv_s.at[dp_of[k]], kv1.at[d], ss.at[0, k], rs.at[0, k], on_dp(k)) for k in range(1, 16)]
    for copy in kv_first:
        copy.start()

    loads[6].wait()
    for i in range(8):
        parts = [
            jnp.dot(pick, q[:, h * HD : (h + 1) * HD], preferred_element_type=F32).reshape(16, 8, HD)
            for h in (2 * i, 2 * i + 1)
        ]
        q_s[:, i * 16 : (i + 1) * 16, :] = jnp.concatenate(parts, 1).astype(BF)
    q_first = [remote(q_s.at[dp_of[k]], q1.at[d], ss.at[1, k], rs.at[1, k], on_dp(k)) for k in range(1, 16)]
    for copy in q_first:
        copy.start()
    hidden = [remote(h_s.at[y_of[k]], h_rx.at[y], ys.at[3, k], yr.at[3, k], on_y(k)) for k in (1, 3, 2)]
    hidden[0].start()
    hidden[1].start()
    kv1[d] = kv_s[d]
    q1[d] = q_s[d]
    g_rx[y] = g_s[y]
    h_rx[y] = h_s[y]

    for copy in kv_first:
        copy.wait_recv()
    group = lambda k: pl.ds(pl.multiple_of(y_of[k] * 16, 16), 16)
    kv_second = [
        remote(kv1.at[:, group(k), :], kv_all.at[z, y], ys.at[1, k], yr.at[1, k], on_y(k)) for k in range(1, 4)
    ]
    for copy in kv_second:
        copy.start()
    kv_all[z, y] = kv1[:, group(0), :]

    chunk = [(y + 4 - t) % 4 for t in range(4)]
    own_up, own_down = [], []
    for t in range(4):
        if t:
            kv_second[t - 1].wait_recv()
        place = kv_all.at[z, chunk[t]]
        own_up.append(remote(place, place, zs.at[0, t], zr.at[0, t], up))
        own_down.append(remote(place, place, zs.at[1, t], zr.at[1, t], down))
        own_up[t].start()
        own_down[t].start()

    for copy in q_first:
        copy.wait_recv()
    heads = lambda k: pl.ds(pl.multiple_of(y_of[k] * 32, 32), 32)
    q_second = [remote(q1.at[:, heads(k), :], q_rx.at[y], ys.at[2, k], yr.at[2, k], on_y(k)) for k in range(1, 4)]
    for copy in q_second:
        copy.start()
    hidden[2].start()
    q_rx[y] = q1[:, heads(0), :]

    passed = []
    for t in range(4):
        if t % 2 == 0:
            own_up[t].wait_recv()
            place = kv_all.at[z_down, chunk[t]]
            passed.append(remote(place, place, zs.at[2, t], zr.at[2, t], up))
        else:
            own_down[t].wait_recv()
            place = kv_all.at[z_up, chunk[t]]
            passed.append(remote(place, place, zs.at[2, t], zr.at[2, t], down))
        passed[t].start()
    for t in range(4):
        (own_down if t % 2 == 0 else own_up)[t].wait_recv()
    lane = lax.broadcasted_iota(jnp.int32, (128, 512), 1)
    take = (lax.broadcasted_iota(jnp.int32, (128, 512), 0) == (lane // 32) * 8 + lane % 8).astype(F32).astype(BF)
    ids = documents[...].astype(F32)
    counts = [jnp.sum((ids < k).astype(F32), axis=1, keepdims=True) for k in range(1, 8)]
    for i in range(4):
        mine = documents[:, pl.ds(pl.multiple_of(z * 512 + i * 128, 128), 128)].astype(F32)
        mine = jnp.dot(jnp.broadcast_to(mine, (16, 128)).astype(BF), take, preferred_element_type=F32)[:1]
        begin = jnp.zeros((1, 512), F32)
        for k in range(1, 8):
            begin = jnp.where(mine == k, counts[k - 1], begin)
        lowest[i] = begin.astype(jnp.int32)

    for copy in passed + q_second + grads + hidden:
        copy.wait_recv()
    for copy in kv_first + grads + q_first + kv_second + own_up + own_down + q_second + hidden + passed:
        copy.wait_send()


def front(plan, documents, cos, sin, x, q, og, w):
    hbm = pl.BlockSpec(memory_space=pltpu.HBM)
    return pl.pallas_call(
        front_kernel,
        in_specs=[vm()] * 4 + [hbm] * 4,
        out_specs=[vm()] * 5,
        out_shape=[
            jax.ShapeDtypeStruct((4, 4, 16, 16, HD), BF),
            jax.ShapeDtypeStruct((4, 16, 32, HD), BF),
            jax.ShapeDtypeStruct((4, 16, 32, HD), BF),
            jax.ShapeDtypeStruct((4, 128, 1024), BF),
            jax.ShapeDtypeStruct((4, 1, 512), jnp.int32),
        ],
        scratch_shapes=[
            pltpu.VMEM((128, 4096), BF),
            pltpu.VMEM((128, 2048), BF),
            pltpu.VMEM((128, 2048), BF),
            pltpu.VMEM((4, 256, 4096), BF),
            pltpu.VMEM((128, 4096), BF),
            pltpu.VMEM((4, 128, 256), F32),
            pltpu.VMEM((16, 64, HD), BF),
            pltpu.VMEM((16, 128, HD), BF),
            pltpu.VMEM((4, 16, 32, HD), BF),
            pltpu.VMEM((4, 128, 1024), BF),
            pltpu.VMEM((16, 64, HD), BF),
            pltpu.VMEM((16, 128, HD), BF),
            pltpu.SemaphoreType.DMA((7,)),
            pltpu.SemaphoreType.DMA((2, 16)),
            pltpu.SemaphoreType.DMA((2, 16)),
            pltpu.SemaphoreType.DMA((4, 4)),
            pltpu.SemaphoreType.DMA((4, 4)),
            pltpu.SemaphoreType.DMA((3, 4)),
            pltpu.SemaphoreType.DMA((3, 4)),
        ],
        compiler_params=pltpu.CompilerParams(collective_id=0, has_side_effects=True, vmem_limit_bytes=49 * MIB),
        name="front",
    )(plan, documents, cos, sin, x, q, og, w)


def attend_kernel(q, og, kv, first, att, qg, dkv, keys, vals, keys_t, vals_t, dk, dv, sc, gp, q_t, og_t, out_t, grad_t):
    base = (lax.axis_index("ctx") // 4) * 512
    for i in range(4):
        block = kv[pl.ds(i * 64, 64)].astype(F32)
        rows = slice(i * 512, (i + 1) * 512)
        k = block[:, :8, :].reshape(512, HD)
        v = block[:, 8:, :].reshape(512, HD)
        keys[rows, :] = k.astype(BF)
        vals[rows, :] = v.astype(BF)
        keys_t[:, rows] = k.T.astype(BF)
        vals_t[:, rows] = v.T.astype(BF)
    keys[2048:, :] = jnp.zeros((128, HD), BF)
    vals[2048:, :] = jnp.zeros((128, HD), BF)
    keys_t[:, 2048:] = jnp.zeros((HD, 128), BF)
    vals_t[:, 2048:] = jnp.zeros((HD, 128), BF)
    dk[...] = jnp.zeros_like(dk)
    dv[...] = jnp.zeros_like(dv)
    fold = SCALE * math.log2(math.e)

    def query_block(qb, carry):
        here = pl.ds(pl.multiple_of(qb * 512, 512), 512)
        q_t[...] = q[here, :].astype(F32).T.astype(BF)
        og_t[...] = og[here, :].astype(F32).T.astype(BF)
        lowest = first[qb]
        start = (jnp.min(lowest) // 128) * 128
        span = base + (qb + 1) * 128 - start
        blocks = []
        for size in (1024, 512, 256, 128):
            count = (span + 128) // size if size == 512 else span // size
            blocks.append((size, count))
            span = jnp.maximum(span - size * count, 0)

        def sweep(part, carry):
            first_row = start
            for size, count in blocks:
                carry = lax.fori_loop(0, count, functools.partial(part, size, first_row), carry)
                first_row = first_row + size * count
            return carry

        lane = lax.broadcasted_iota(jnp.int32, (1, 512), 1)
        position = base + qb * 128 + (lane // 32) * 8 + lane % 8
        out_t[...] = jnp.zeros_like(out_t)
        grad_t[...] = jnp.zeros_like(grad_t)

        def eights(t):
            return t.reshape(t.shape[0] // 8, 8, 512)

        def scores(size, at, i, top):
            at = pl.multiple_of(at + i * size, 128)
            rows = pl.ds(at, size)
            s = jnp.dot(keys[rows, :], q_t[...], preferred_element_type=F32)
            index = at + lax.broadcasted_iota(jnp.int32, (size, 512), 0)
            s = jnp.where((index <= position) & (index >= lowest), s, MASK_VALUE)
            sc[rows, :] = s
            return jnp.maximum(top, jnp.max(eights(s), axis=0))

        top = sweep(scores, jnp.full((8, 512), MASK_VALUE, F32))
        top = jnp.max(top, axis=0, keepdims=True) * fold

        def expo(size, at, i, sums):
            rows = pl.ds(pl.multiple_of(at + i * size, 128), size)
            e = jnp.exp2(sc[rows, :] * fold - top)
            grad = jnp.dot(vals[rows, :], og_t[...], preferred_element_type=F32)
            sc[rows, :] = e
            gp[rows, :] = grad
            return sums[0] + jnp.sum(eights(e), axis=0), sums[1] + jnp.sum(eights(e * grad), axis=0)

        zero = jnp.zeros((8, 512), F32)
        total, product = sweep(expo, (zero, zero))
        inverse = 1.0 / jnp.sum(total, axis=0, keepdims=True)
        delta = jnp.sum(product, axis=0, keepdims=True) * inverse

        def both(size, at, i, c):
            rows = pl.ds(pl.multiple_of(at + i * size, 128), size)
            p = sc[rows, :] * inverse
            rounded = p.astype(BF)
            ds = (p * (gp[rows, :] - delta)).astype(BF)
            dv[rows, :] += jnp.dot(rounded, og[here, :], preferred_element_type=F32)
            dk[rows, :] += jnp.dot(ds, q[here, :], preferred_element_type=F32)
            out_t[...] += jnp.dot(vals_t[:, rows], rounded, preferred_element_type=F32)
            grad_t[...] += jnp.dot(keys_t[:, rows], ds, preferred_element_type=F32)
            return c

        sweep(both, 0)
        att[here, :] = out_t[...].T.astype(BF)
        qg[here, :] = (grad_t[...] * SCALE).T.astype(BF)
        return carry

    lax.fori_loop(0, 4, query_block, 0)
    for i in range(4):
        rows = slice(i * 512, (i + 1) * 512)
        dkv[i, 0] = (dk[rows, :] * SCALE).astype(BF)
        dkv[i, 1] = dv[rows, :].astype(BF)


def attend(q, og, kv, first):
    return pl.pallas_call(
        attend_kernel,
        in_specs=[vm()] * 4,
        out_specs=[vm()] * 3,
        scratch_shapes=[
            pltpu.VMEM((2176, HD), BF),
            pltpu.VMEM((2176, HD), BF),
            pltpu.VMEM((HD, 2176), BF),
            pltpu.VMEM((HD, 2176), BF),
            pltpu.VMEM((2176, HD), F32),
            pltpu.VMEM((2176, HD), F32),
            pltpu.VMEM((2176, 512), F32),
            pltpu.VMEM((2176, 512), F32),
            pltpu.VMEM((HD, 512), BF),
            pltpu.VMEM((HD, 512), BF),
            pltpu.VMEM((HD, 512), F32),
            pltpu.VMEM((HD, 512), F32),
        ],
        out_shape=[
            jax.ShapeDtypeStruct((2048, HD), BF),
            jax.ShapeDtypeStruct((2048, HD), BF),
            jax.ShapeDtypeStruct((4, 2, 512, HD), BF),
        ],
        compiler_params=pltpu.CompilerParams(vmem_limit_bytes=48 * MIB),
        name="attend",
    )(q, og, kv, first)


def back_kernel(
    att, qg, dkv, cos, sin, hs, w_h, att_o, qg_o, hg_o, grad,
    att_rx, qg_rx, hop, mid, fin, own_a, own_b, src, pg_rx, hsr, pgh, w, tile, pair, mine, ring, part, last,
    ws, ys, yr, zs, zr, ss, rs, cs, cr, xs, xr, es, er,
):
    d, c = lax.axis_index("dp"), lax.axis_index("ctx")
    z, y = c // 4, c % 4
    zl, x, core = d // 8, (d // 2) % 4, d % 2
    dp_of = [(d + k) % 16 for k in range(16)]
    y_of = [(y + k) % 4 for k in range(4)]
    x_of = [(x + k) % 4 for k in range(4)]
    z_of = [(z + k) % 4 for k in range(4)]
    on_dp = lambda k: {"dp": dp_of[k]}
    on_y = lambda k: {"ctx": z * 4 + y_of[k]}
    on_x = lambda k: {"dp": zl * 8 + x_of[k] * 2 + core}
    on_z = lambda lo, k: {"dp": lo * 8 + x * 2 + core, "ctx": z_of[k] * 4 + y}
    sibling = {"dp": d + 1 - 2 * core}
    up, down = {"ctx": (c + 4) % 16}, {"ctx": (c + 12) % 16}
    z_up, z_far, z_down = z_of[1], z_of[2], z_of[3]
    low, high = pl.ds(0, 256), pl.ds(256, 256)

    weights = pltpu.make_async_copy(w_h, w, ws)
    weights.start()
    greet(
        [on_dp(k) for k in range(1, 16)]
        + [on_y(k) for k in range(1, 4)]
        + [on_z(zl, k) for k in range(1, 4)]
        + [on_z(1 - zl, k) for k in range(1, 4)]
    )

    far, near = {}, {}
    for s in (1, 0):
        far[s] = [
            remote(dkv.at[z_far, s, low], hop.at[s, 0], zs.at[s, 0], zr.at[s, 0], down),
            remote(dkv.at[z_far, s, high], hop.at[s, 1], zs.at[s, 1], zr.at[s, 1], up),
        ]
        near[s] = [
            remote(dkv.at[z_down, s, high], fin.at[s, 0, high], zs.at[s, 2], zr.at[s, 2], down),
            remote(dkv.at[z_up, s, low], fin.at[s, 0, low], zs.at[s, 3], zr.at[s, 3], up),
        ]
    for copy in far[1] + near[1]:
        copy.start()
    outs = []
    for i, (a, b) in enumerate(((att, att_rx), (qg, qg_rx))):
        for k in range(1, 4):
            outs.append(remote(a.at[y_of[k]], b.at[y], ys.at[i, k], yr.at[i, k], on_y(k)))
            outs[-1].start()
        b[y] = a[y]

    sums = {}

    def pass_on(s):
        far[s][0].wait_recv()
        mid[s, 0] = (hop[s, 0].astype(F32) + dkv[z_down, s, 0:256, :].astype(F32)).astype(BF)
        first = remote(mid.at[s, 0], fin.at[s, 1, low], zs.at[s, 4], zr.at[s, 4], down)
        first.start()
        far[s][1].wait_recv()
        mid[s, 1] = (hop[s, 1].astype(F32) + dkv[z_up, s, 256:512, :].astype(F32)).astype(BF)
        second = remote(mid.at[s, 1], fin.at[s, 1, high], zs.at[s, 5], zr.at[s, 5], up)
        second.start()
        sums[s] = [first, second]

    exchanged, packed = {}, {}

    def complete(s):
        for copy in near[s] + sums[s]:
            copy.wait_recv()
        for i in range(2):
            pieces = []
            for j in (2 * i, 2 * i + 1):
                sl = slice(j * 128, (j + 1) * 128)
                t = dkv[z, s, sl, :].astype(F32) + fin[s, 0, sl, :].astype(F32) + fin[s, 1, sl, :].astype(F32)
                t = t.astype(BF).astype(F32)
                if s == 0:
                    swapped = pltpu.roll(t, 64, 1)
                    turned = []
                    for a in range(16):
                        rows = slice(a * 8, (a + 1) * 8)
                        c8, s8 = turn(cos, sin, slice(j * 16 + a, j * 16 + a + 1))
                        turned.append(t[rows, :] * c8 - swapped[rows, :] * s8)
                    t = jnp.concatenate(turned, 0)
                own_b[s, j] = t.astype(BF)
                pieces.append(t.reshape(16, 8, HD))
            own_a[s, :, i * 16 : (i + 1) * 16, :] = jnp.concatenate(pieces, 1).astype(BF)
        exchanged[s] = [
            remote(own_a.at[s, dp_of[k]], src.at[s, y, d], ss.at[s, k], rs.at[s, k], on_dp(k)) for k in range(1, 16)
        ]
        for copy in exchanged[s]:
            copy.start()
        packed[s] = [
            remote(own_b.at[s, y_of[k]], pg_rx.at[s, y], ys.at[2 + s, k], yr.at[2 + s, k], on_y(k))
            for k in range(1, 4)
        ]
        for copy in packed[s]:
            copy.start()
        src[s, y, d] = own_a[s, d]
        pg_rx[s, y] = own_b[s, y]

    gathered = {}

    def gather(s):
        for copy in exchanged[s]:
            copy.wait_recv()
        gathered[s] = [
            remote(src.at[s, y], src.at[s, y], ys.at[4 + s, k], yr.at[4 + s, k], on_y(k)) for k in range(1, 4)
        ]
        for copy in gathered[s]:
            copy.start()

    swaps = {0: [], 1: []}
    order = [2, 1, 3, 0]

    def multiply(s):
        for copy in gathered[s]:
            copy.wait_recv()
        for k in order:
            g = x_of[k]
            rows = src[s, g].reshape(512, HD)
            tile[s, k] = cols_dot(rows, hsr[...]).reshape(2, 64, 1024).astype(BF)
            copy = remote(tile.at[s, k, 1 - core], pair.at[s, k], cs.at[s, k], cr.at[s, k], sibling)
            copy.start()
            swaps[s].append(copy)

    rings = {0: [], 1: []}

    def add_pair(s):
        for copy, k in zip(swaps[s], order):
            copy.wait_recv()
            for j in range(4):
                sl = slice(j * 256, (j + 1) * 256)
                mine[s, k, :, sl] = (
                    tile[s, k, core, :, sl].astype(F32) + pair[s, k, :, sl].astype(F32)
                ).astype(BF)
            if k:
                copy = remote(mine.at[s, k], ring.at[s, k], xs.at[s, k], xr.at[s, k], on_x(k))
                copy.start()
                rings[s].append(copy)

    same = lambda s, k: remote(part.at[s, z_of[k]], last.at[k], es.at[k], er.at[k], on_z(s, k))
    other = lambda s, k: remote(part.at[s, z_of[k]], last.at[4 + k], es.at[4 + k], er.at[4 + k], on_z(s, k))

    def add_ring(s):
        for copy in rings[s]:
            copy.wait_recv()
        for j in range(4):
            sl = slice(j * 256, (j + 1) * 256)
            t = mine[s, 0, :, sl].astype(F32)
            for k in range(1, 4):
                t = t + ring[s, k, :, sl].astype(F32)
            part[s, j] = t.astype(BF)

        @pl.when(zl == s)
        def _():
            for k in range(1, 4):
                same(s, k).start()

        @pl.when(zl != s)
        def _():
            for k in range(4):
                other(s, k).start()

    for j in range(4):
        sl = slice(j * 256, (j + 1) * 256)
        pieces = [hs[i, :, sl].astype(F32).reshape(16, 8, 256) for i in range(4)]
        hsr[:, sl] = jnp.concatenate(pieces, 1).reshape(512, 256).astype(BF)
    pass_on(1)
    for copy in far[0] + near[0]:
        copy.start()
    complete(1)
    pass_on(0)
    gather(1)
    for copy in outs:
        copy.wait_recv()
    for g in range(4):
        for source, target in ((att_rx, att_o), (qg_rx, qg_o)):
            block = source[g].reshape(16, 32, HD).astype(F32)
            for h in range(4):
                cols = slice((g * 4 + h) * HD, (g * 4 + h + 1) * HD)
                target[:, cols] = block[:, h * 8 : h * 8 + 8, :].reshape(128, HD).astype(BF)
    complete(0)
    multiply(1)
    gather(0)
    add_pair(1)
    multiply(0)
    add_ring(1)
    for s in (1, 0):
        for copy in packed[s]:
            copy.wait_recv()
        for g in range(4):
            cols = slice(s * 512 + g * HD, s * 512 + (g + 1) * HD)
            pgh[:, cols] = pg_rx[s, g]
    add_pair(0)
    weights.wait()
    for j in range(8):
        sl = slice(j * 512, (j + 1) * 512)
        hg_o[:, sl] = jnp.dot(pgh[...], w[:, sl], preferred_element_type=F32).astype(BF)
    add_ring(0)
    ends = [same(zl, k) for k in range(1, 4)] + [other(1 - zl, k) for k in range(4)]
    for copy in ends:
        copy.wait_recv()
    t = part[zl, z].astype(F32)
    for k in range(1, 8):
        t = t + last[k].astype(F32)
    grad[...] = t * (1.0 / 16.0)
    for s in (0, 1):
        for copy in far[s] + near[s] + sums[s] + exchanged[s] + packed[s] + gathered[s] + swaps[s] + rings[s]:
            copy.wait_send()
    for copy in outs + ends:
        copy.wait_send()


def back(att, qg, dkv, cos, sin, hs, w):
    dma = pltpu.SemaphoreType.DMA
    return pl.pallas_call(
        back_kernel,
        in_specs=[vm()] * 6 + [pl.BlockSpec(memory_space=pltpu.HBM)],
        out_specs=[vm()] * 4,
        out_shape=[
            jax.ShapeDtypeStruct((128, 2048), BF),
            jax.ShapeDtypeStruct((128, 2048), BF),
            jax.ShapeDtypeStruct((128, 4096), BF),
            jax.ShapeDtypeStruct((64, 256), F32),
        ],
        scratch_shapes=[
            pltpu.VMEM((4, 512, HD), BF),
            pltpu.VMEM((4, 512, HD), BF),
            pltpu.VMEM((2, 2, 256, HD), BF),
            pltpu.VMEM((2, 2, 256, HD), BF),
            pltpu.VMEM((2, 2, 512, HD), BF),
            pltpu.VMEM((2, 16, 32, HD), BF),
            pltpu.VMEM((2, 4, 128, HD), BF),
            pltpu.VMEM((2, 4, 16, 32, HD), BF),
            pltpu.VMEM((2, 4, 128, HD), BF),
            pltpu.VMEM((512, 1024), BF),
            pltpu.VMEM((128, 1024), BF),
            pltpu.VMEM((1024, 4096), BF),
            pltpu.VMEM((2, 4, 2, 64, 1024), BF),
            pltpu.VMEM((2, 4, 64, 1024), BF),
            pltpu.VMEM((2, 4, 64, 1024), BF),
            pltpu.VMEM((2, 4, 64, 1024), BF),
            pltpu.VMEM((2, 4, 64, 256), BF),
            pltpu.VMEM((8, 64, 256), BF),
            dma, dma((6, 4)), dma((6, 4)), dma((2, 6)), dma((2, 6)), dma((2, 16)), dma((2, 16)),
            dma((2, 4)), dma((2, 4)), dma((2, 4)), dma((2, 4)), dma((8,)), dma((8,)),
        ],
        compiler_params=pltpu.CompilerParams(collective_id=1, has_side_effects=True, vmem_limit_bytes=48 * MIB),
        name="back",
    )(att, qg, dkv, cos, sin, hs, w)


def store_kernel(a, b, c, e, a_o, b_o, c_o, e_o, sems):
    copies = [pltpu.make_async_copy(p, o, sems.at[i]) for i, (p, o) in enumerate(((a, a_o), (b, b_o), (c, c_o), (e, e_o)))]
    for copy in copies:
        copy.start()
    for copy in copies:
        copy.wait()


def store(*arrays):
    hbm = pl.BlockSpec(memory_space=pltpu.HBM)
    return pl.pallas_call(
        store_kernel,
        in_specs=[vm()] * 4,
        out_specs=[hbm] * 4,
        out_shape=[jax.ShapeDtypeStruct(a.shape, a.dtype) for a in arrays],
        scratch_shapes=[pltpu.SemaphoreType.DMA((4,))],
        compiler_params=pltpu.CompilerParams(vmem_limit_bytes=16 * MIB),
        name="store",
    )(*arrays)


def body(hidden_rows, query_rows, out_grad, projection, packing_plan, document_ids):
    z = lax.axis_index("ctx") // 4
    small = jnp.arange(8, dtype=jnp.int32)
    cos, sin = angle_tables(jnp.concatenate([z * 512 + jnp.arange(64, dtype=jnp.int32) * 8, small]))
    kv_all, q_rx, g_rx, h_rx, first = front(
        packing_plan, document_ids, cos, sin, hidden_rows, query_rows, out_grad, projection
    )
    att, qg, dkv = attend(
        q_rx.reshape(2048, HD), g_rx.reshape(2048, HD), kv_all.reshape(256, 16, HD), first
    )
    return store(*back(att.reshape(4, 512, HD), qg.reshape(4, 512, HD), dkv, cos, sin, h_rx, projection))


def solution(mesh):
    rows = P(("dp", "ctx"), None)
    return jax.shard_map(
        body,
        mesh=mesh,
        in_specs=(rows, rows, rows, P(), rows, P("dp", None)),
        out_specs=(rows, rows, rows, P("dp", "ctx")),
        check_vma=False,
    )
```

```python
import functools
import math

import jax
import jax.numpy as jnp
from jax import lax
from jax.experimental import pallas as pl
from jax.experimental.pallas import tpu as pltpu
from jax.sharding import PartitionSpec as P

ROPE_BASE = 500000.0
MASK_VALUE = -1e30
HD = 128
SCALE = HD ** (-0.5)
BF = jnp.bfloat16
F32 = jnp.float32
MESH = pl.DeviceIdType.MESH
MIB = 1024 * 1024


def vm():
    return pl.BlockSpec(memory_space=pltpu.VMEM)


def rows_dot(a, b):
    return lax.dot_general(a, b, (((1,), (1,)), ((), ())), preferred_element_type=F32)


def cols_dot(a, b):
    return lax.dot_general(a, b, (((0,), (0,)), ((), ())), preferred_element_type=F32)


def angle_tables(positions):
    half = HD // 2
    exponent = jnp.arange(half, dtype=F32) * (-2.0 * math.log(ROPE_BASE) / HD)
    angles = positions.astype(F32)[:, None] * jnp.exp(exponent)[None, :]
    cosine, sine = jnp.cos(angles), jnp.sin(angles)
    return jnp.concatenate([cosine, cosine], 1), jnp.concatenate([-sine, sine], 1)


def turn(cos, sin, rows):
    c, s, c8, s8 = cos[rows, :], sin[rows, :], cos[64:, :], sin[64:, :]
    return c * c8 - s * s8, s * c8 + c * s8


def remote(src, dst, send, recv, device):
    return pltpu.make_async_remote_copy(
        src_ref=src, dst_ref=dst, send_sem=send, recv_sem=recv, device_id=device, device_id_type=MESH
    )


def greet(devices):
    barrier = pltpu.get_barrier_semaphore()
    for device in devices:
        pl.semaphore_signal(barrier, inc=1, device_id=device, device_id_type=MESH)
    pl.semaphore_wait(barrier, len(devices))


def front_kernel(
    plan_ids, cos, sin, x_h, q_h, og_h, w_h, kv_all, q_rx, g_rx, h_rx, lowest,
    x, q, og, w, xp, acc, kv_s, q_s, g_s, h_s, kv1, q1, ls, ss, rs, ys, yr, zs, zr,
):
    d, c = lax.axis_index("dp"), lax.axis_index("ctx")
    z, y = c // 4, c % 4
    dp_of = [(d + k) % 16 for k in range(16)]
    y_of = [(y + k) % 4 for k in range(4)]
    on_dp = lambda k: {"dp": dp_of[k]}
    on_y = lambda k: {"ctx": z * 4 + y_of[k]}
    up, down = {"ctx": (c + 4) % 16}, {"ctx": (c + 12) % 16}
    z_up, z_down = (z + 1) % 4, (z + 3) % 4

    loads = [pltpu.make_async_copy(x_h, x, ls.at[2])]
    loads += [pltpu.make_async_copy(w_h.at[pl.ds(i * 256, 256)], w.at[i], ls.at[3 + i]) for i in range(4)]
    loads += [pltpu.make_async_copy(og_h, og, ls.at[0]), pltpu.make_async_copy(q_h, q, ls.at[1])]
    for copy in loads:
        copy.start()
    partners = [on_dp(k) for k in range(1, 16)] + [on_y(k) for k in range(1, 4)] + [up, down]
    barrier = pltpu.get_barrier_semaphore()
    for device in partners:
        pl.semaphore_signal(barrier, inc=1, device_id=device, device_id_type=MESH)

    pick = (lax.broadcasted_iota(jnp.int32, (128, 128), 0) == plan_ids[:, :128]).astype(F32).astype(BF)
    loads[0].wait()
    for j in range(16):
        sl = slice(j * 256, (j + 1) * 256)
        t = jnp.dot(pick, x[:, sl], preferred_element_type=F32).astype(BF)
        xp[:, sl] = t
        h_s[j % 4, :, (j // 4) * 256 : (j // 4 + 1) * 256] = t
    loads[5].wait()
    for i in range(8):
        grads = [og[:, h * HD : (h + 1) * HD].astype(F32).reshape(16, 8, HD) for h in (2 * i, 2 * i + 1)]
        g_s[i // 2, :, (i % 2) * 16 : (i % 2 + 1) * 16, :] = jnp.concatenate(grads, 1).astype(BF)
    pl.semaphore_wait(barrier, len(partners))
    grads = [remote(g_s.at[y_of[k]], g_rx.at[y], ys.at[0, k], yr.at[0, k], on_y(k)) for k in range(1, 4)]
    for copy in grads:
        copy.start()

    for i in range(4):
        loads[1 + i].wait()
        acc[i] = rows_dot(xp[...], w[i])
    near_cos, near_sin = turn(cos, sin, pl.ds(y * 16 + d, 1))
    for g in range(4):
        sl = slice((g % 2) * HD, (g % 2 + 1) * HD)
        k = acc[g // 2][:, sl]
        v = acc[2 + g // 2][:, sl]
        k3 = k.reshape(16, 8, HD)
        r3 = pltpu.roll(k, 64, 1).reshape(16, 8, HD)
        rot = k3 * near_cos[None] + r3 * near_sin[None]
        kv_s[:, g * 16 : (g + 1) * 16, :] = jnp.concatenate([rot, v.reshape(16, 8, HD)], 1).astype(BF)
    kv_first = [remote(kv_s.at[dp_of[k]], kv1.at[d], ss.at[0, k], rs.at[0, k], on_dp(k)) for k in range(1, 16)]
    for copy in kv_first:
        copy.start()

    loads[6].wait()
    for i in range(8):
        parts = [
            jnp.dot(pick, q[:, h * HD : (h + 1) * HD], preferred_element_type=F32).reshape(16, 8, HD)
            for h in (2 * i, 2 * i + 1)
        ]
        q_s[:, i * 16 : (i + 1) * 16, :] = jnp.concatenate(parts, 1).astype(BF)
    q_first = [remote(q_s.at[dp_of[k]], q1.at[d], ss.at[1, k], rs.at[1, k], on_dp(k)) for k in range(1, 16)]
    for copy in q_first:
        copy.start()
    hidden = [remote(h_s.at[y_of[k]], h_rx.at[y], ys.at[3, k], yr.at[3, k], on_y(k)) for k in (1, 3, 2)]
    hidden[0].start()
    hidden[1].start()
    kv1[d] = kv_s[d]
    q1[d] = q_s[d]
    g_rx[y] = g_s[y]
    h_rx[y] = h_s[y]

    for copy in kv_first:
        copy.wait_recv()
    group = lambda k: pl.ds(pl.multiple_of(y_of[k] * 16, 16), 16)
    kv_second = [
        remote(kv1.at[:, group(k), :], kv_all.at[z, y], ys.at[1, k], yr.at[1, k], on_y(k)) for k in range(1, 4)
    ]
    for copy in kv_second:
        copy.start()
    kv_all[z, y] = kv1[:, group(0), :]

    chunk = [(y + 4 - t) % 4 for t in range(4)]
    own_up, own_down = [], []
    for t in range(4):
        if t:
            kv_second[t - 1].wait_recv()
        place = kv_all.at[z, chunk[t]]
        own_up.append(remote(place, place, zs.at[0, t], zr.at[0, t], up))
        own_down.append(remote(place, place, zs.at[1, t], zr.at[1, t], down))
        own_up[t].start()
        own_down[t].start()

    for copy in q_first:
        copy.wait_recv()
    heads = lambda k: pl.ds(pl.multiple_of(y_of[k] * 32, 32), 32)
    q_second = [remote(q1.at[:, heads(k), :], q_rx.at[y], ys.at[2, k], yr.at[2, k], on_y(k)) for k in range(1, 4)]
    for copy in q_second:
        copy.start()
    hidden[2].start()
    q_rx[y] = q1[:, heads(0), :]

    passed = []
    for t in range(4):
        if t % 2 == 0:
            own_up[t].wait_recv()
            place = kv_all.at[z_down, chunk[t]]
            passed.append(remote(place, place, zs.at[2, t], zr.at[2, t], up))
        else:
            own_down[t].wait_recv()
            place = kv_all.at[z_up, chunk[t]]
            passed.append(remote(place, place, zs.at[2, t], zr.at[2, t], down))
        passed[t].start()
    for t in range(4):
        (own_down if t % 2 == 0 else own_up)[t].wait_recv()
    lane = lax.broadcasted_iota(jnp.int32, (128, 512), 1)
    take = (lax.broadcasted_iota(jnp.int32, (128, 512), 0) == (lane // 32) * 8 + lane % 8).astype(F32).astype(BF)
    ids = plan_ids[:, 128:].astype(F32)
    counts = [jnp.sum((ids < k).astype(F32), axis=1, keepdims=True) for k in range(1, 8)]
    for i in range(4):
        mine = plan_ids[:, pl.ds(pl.multiple_of(z * 512 + (i + 1) * 128, 128), 128)].astype(F32)
        mine = jnp.dot(jnp.broadcast_to(mine, (16, 128)).astype(BF), take, preferred_element_type=F32)[:1]
        begin = jnp.zeros((1, 512), F32)
        for k in range(1, 8):
            begin = jnp.where(mine == k, counts[k - 1], begin)
        lowest[i] = begin.astype(jnp.int32)

    for copy in passed + q_second + grads + hidden:
        copy.wait_recv()
    for copy in kv_first + grads + q_first + kv_second + own_up + own_down + q_second + hidden + passed:
        copy.wait_send()


def front(plan_ids, cos, sin, x, q, og, w):
    hbm = pl.BlockSpec(memory_space=pltpu.HBM)
    return pl.pallas_call(
        front_kernel,
        in_specs=[vm()] * 3 + [hbm] * 4,
        out_specs=[vm()] * 5,
        out_shape=[
            jax.ShapeDtypeStruct((4, 4, 16, 16, HD), BF),
            jax.ShapeDtypeStruct((4, 16, 32, HD), BF),
            jax.ShapeDtypeStruct((4, 16, 32, HD), BF),
            jax.ShapeDtypeStruct((4, 128, 1024), BF),
            jax.ShapeDtypeStruct((4, 1, 512), jnp.int32),
        ],
        scratch_shapes=[
            pltpu.VMEM((128, 4096), BF),
            pltpu.VMEM((128, 2048), BF),
            pltpu.VMEM((128, 2048), BF),
            pltpu.VMEM((4, 256, 4096), BF),
            pltpu.VMEM((128, 4096), BF),
            pltpu.VMEM((4, 128, 256), F32),
            pltpu.VMEM((16, 64, HD), BF),
            pltpu.VMEM((16, 128, HD), BF),
            pltpu.VMEM((4, 16, 32, HD), BF),
            pltpu.VMEM((4, 128, 1024), BF),
            pltpu.VMEM((16, 64, HD), BF),
            pltpu.VMEM((16, 128, HD), BF),
            pltpu.SemaphoreType.DMA((7,)),
            pltpu.SemaphoreType.DMA((2, 16)),
            pltpu.SemaphoreType.DMA((2, 16)),
            pltpu.SemaphoreType.DMA((4, 4)),
            pltpu.SemaphoreType.DMA((4, 4)),
            pltpu.SemaphoreType.DMA((3, 4)),
            pltpu.SemaphoreType.DMA((3, 4)),
        ],
        compiler_params=pltpu.CompilerParams(collective_id=0, has_side_effects=True, vmem_limit_bytes=49 * MIB),
        name="front",
    )(plan_ids, cos, sin, x, q, og, w)


def attend_kernel(q, og, kv, first, att, qg, dkv, keys, vals, keys_t, vals_t, dk, dv, sc, gp, q_t, og_t, out_t, grad_t, tops):
    base = (lax.axis_index("ctx") // 4) * 512
    for i in range(4):
        block = kv[pl.ds(i * 64, 64)].astype(F32)
        rows = slice(i * 512, (i + 1) * 512)
        k = block[:, :8, :].reshape(512, HD)
        v = block[:, 8:, :].reshape(512, HD)
        keys[rows, :] = k.astype(BF)
        vals[rows, :] = v.astype(BF)
        keys_t[:, rows] = k.T.astype(BF)
        vals_t[:, rows] = v.T.astype(BF)
    keys[2048:, :] = jnp.zeros((128, HD), BF)
    vals[2048:, :] = jnp.zeros((128, HD), BF)
    keys_t[:, 2048:] = jnp.zeros((HD, 128), BF)
    vals_t[:, 2048:] = jnp.zeros((HD, 128), BF)
    dk[...] = jnp.zeros_like(dk)
    dv[...] = jnp.zeros_like(dv)
    fold = SCALE * math.log2(math.e)

    def query_block(qb, carry):
        here = pl.ds(pl.multiple_of(qb * 512, 512), 512)
        q_t[...] = q[here, :].astype(F32).T.astype(BF)
        og_t[...] = og[here, :].astype(F32).T.astype(BF)
        lowest = first[qb]
        start = (jnp.min(lowest) // 128) * 128
        span = base + (qb + 1) * 128 - start
        blocks = []
        for size in (1024, 512, 256, 128):
            count = (span + 128) // size if size == 512 else span // size
            blocks.append((size, count))
            span = jnp.maximum(span - size * count, 0)

        def sweep(part, carry):
            first_row = start
            for size, count in blocks:
                carry = lax.fori_loop(0, count, functools.partial(part, size, first_row), carry)
                first_row = first_row + size * count
            return carry

        lane = lax.broadcasted_iota(jnp.int32, (1, 512), 1)
        position = base + qb * 128 + (lane // 32) * 8 + lane % 8
        out_t[...] = jnp.zeros_like(out_t)
        grad_t[...] = jnp.zeros_like(grad_t)

        def eights(t):
            return t.reshape(t.shape[0] // 8, 8, 512)

        def scores(size, at, i, sums):
            at = pl.multiple_of(at + i * size, 128)
            rows = pl.ds(at, size)
            s = jnp.dot(keys[rows, :], q_t[...], preferred_element_type=F32)
            grad = jnp.dot(vals[rows, :], og_t[...], preferred_element_type=F32)
            gp[rows, :] = grad
            index = at + lax.broadcasted_iota(jnp.int32, (size, 512), 0)
            s = jnp.where((index <= position) & (index >= lowest), s, MASK_VALUE)
            top, total, product = sums
            high = jnp.maximum(top, jnp.max(jnp.max(eights(s), axis=0), axis=0, keepdims=True) * fold)
            e = jnp.exp2(s * fold - high)
            sc[rows, :] = e
            tops[at // 128] = high
            shrink = jnp.exp2(top - high)
            return (
                high,
                total * shrink + jnp.sum(eights(e), axis=0),
                product * shrink + jnp.sum(eights(e * grad), axis=0),
            )

        zero = jnp.zeros((8, 512), F32)
        top, total, product = sweep(scores, (jnp.full((1, 512), MASK_VALUE, F32), zero, zero))
        inverse = 1.0 / jnp.sum(total, axis=0, keepdims=True)
        delta = jnp.sum(product, axis=0, keepdims=True) * inverse

        def both(size, at, i, c):
            at = pl.multiple_of(at + i * size, 128)
            rows = pl.ds(at, size)
            p = sc[rows, :] * (jnp.exp2(tops[at // 128] - top) * inverse)
            rounded = p.astype(BF)
            ds = (p * (gp[rows, :] - delta)).astype(BF)
            dv[rows, :] += jnp.dot(rounded, og[here, :], preferred_element_type=F32)
            dk[rows, :] += jnp.dot(ds, q[here, :], preferred_element_type=F32)
            out_t[...] += jnp.dot(vals_t[:, rows], rounded, preferred_element_type=F32)
            grad_t[...] += jnp.dot(keys_t[:, rows], ds, preferred_element_type=F32)
            return c

        sweep(both, 0)
        att[here, :] = out_t[...].T.astype(BF)
        qg[here, :] = (grad_t[...] * SCALE).T.astype(BF)
        return carry

    lax.fori_loop(0, 4, query_block, 0)
    for i in range(4):
        rows = slice(i * 512, (i + 1) * 512)
        dkv[i, 0] = (dk[rows, :] * SCALE).astype(BF)
        dkv[i, 1] = dv[rows, :].astype(BF)


def attend(q, og, kv, first):
    return pl.pallas_call(
        attend_kernel,
        in_specs=[vm()] * 4,
        out_specs=[vm()] * 3,
        scratch_shapes=[
            pltpu.VMEM((2176, HD), BF),
            pltpu.VMEM((2176, HD), BF),
            pltpu.VMEM((HD, 2176), BF),
            pltpu.VMEM((HD, 2176), BF),
            pltpu.VMEM((2176, HD), F32),
            pltpu.VMEM((2176, HD), F32),
            pltpu.VMEM((2176, 512), F32),
            pltpu.VMEM((2176, 512), F32),
            pltpu.VMEM((HD, 512), BF),
            pltpu.VMEM((HD, 512), BF),
            pltpu.VMEM((HD, 512), F32),
            pltpu.VMEM((HD, 512), F32),
            pltpu.VMEM((17, 1, 512), F32),
        ],
        out_shape=[
            jax.ShapeDtypeStruct((2048, HD), BF),
            jax.ShapeDtypeStruct((2048, HD), BF),
            jax.ShapeDtypeStruct((4, 2, 512, HD), BF),
        ],
        compiler_params=pltpu.CompilerParams(vmem_limit_bytes=48 * MIB),
        name="attend",
    )(q, og, kv, first)


def back_kernel(
    att, qg, dkv, cos, sin, hs, w_h, att_o, qg_o, hg_o, grad,
    att_rx, qg_rx, hop, mid, fin, own_a, own_b, src, pg_rx, hsr, pgh, w, tile, pair, mine, ring, part, last,
    ws, ys, yr, zs, zr, ss, rs, cs, cr, xs, xr, es, er,
):
    d, c = lax.axis_index("dp"), lax.axis_index("ctx")
    z, y = c // 4, c % 4
    zl, x, core = d // 8, (d // 2) % 4, d % 2
    dp_of = [(d + k) % 16 for k in range(16)]
    y_of = [(y + k) % 4 for k in range(4)]
    x_of = [(x + k) % 4 for k in range(4)]
    z_of = [(z + k) % 4 for k in range(4)]
    on_dp = lambda k: {"dp": dp_of[k]}
    on_y = lambda k: {"ctx": z * 4 + y_of[k]}
    on_x = lambda k: {"dp": zl * 8 + x_of[k] * 2 + core}
    on_z = lambda lo, k: {"dp": lo * 8 + x * 2 + core, "ctx": z_of[k] * 4 + y}
    sibling = {"dp": d + 1 - 2 * core}
    up, down = {"ctx": (c + 4) % 16}, {"ctx": (c + 12) % 16}
    z_up, z_far, z_down = z_of[1], z_of[2], z_of[3]
    low, high = pl.ds(0, 256), pl.ds(256, 256)

    weights = pltpu.make_async_copy(w_h, w, ws)
    weights.start()
    greet(
        [on_dp(k) for k in range(1, 16)]
        + [on_y(k) for k in range(1, 4)]
        + [on_z(zl, k) for k in range(1, 4)]
        + [on_z(1 - zl, k) for k in range(1, 4)]
    )

    far, near = {}, {}
    for s in (1, 0):
        far[s] = [
            remote(dkv.at[z_far, s, low], hop.at[s, 0], zs.at[s, 0], zr.at[s, 0], down),
            remote(dkv.at[z_far, s, high], hop.at[s, 1], zs.at[s, 1], zr.at[s, 1], up),
        ]
        near[s] = [
            remote(dkv.at[z_down, s, high], fin.at[s, 0, high], zs.at[s, 2], zr.at[s, 2], down),
            remote(dkv.at[z_up, s, low], fin.at[s, 0, low], zs.at[s, 3], zr.at[s, 3], up),
        ]
    for copy in far[1] + near[1]:
        copy.start()
    outs = []
    for i, (a, b) in enumerate(((att, att_rx), (qg, qg_rx))):
        for k in range(1, 4):
            outs.append(remote(a.at[y_of[k]], b.at[y], ys.at[i, k], yr.at[i, k], on_y(k)))
            outs[-1].start()
        b[y] = a[y]

    sums = {}

    def pass_on(s):
        far[s][0].wait_recv()
        mid[s, 0] = (hop[s, 0].astype(F32) + dkv[z_down, s, 0:256, :].astype(F32)).astype(BF)
        first = remote(mid.at[s, 0], fin.at[s, 1, low], zs.at[s, 4], zr.at[s, 4], down)
        first.start()
        far[s][1].wait_recv()
        mid[s, 1] = (hop[s, 1].astype(F32) + dkv[z_up, s, 256:512, :].astype(F32)).astype(BF)
        second = remote(mid.at[s, 1], fin.at[s, 1, high], zs.at[s, 5], zr.at[s, 5], up)
        second.start()
        sums[s] = [first, second]

    exchanged, packed = {}, {}

    def complete(s):
        for copy in near[s] + sums[s]:
            copy.wait_recv()
        for i in range(2):
            pieces = []
            for j in (2 * i, 2 * i + 1):
                sl = slice(j * 128, (j + 1) * 128)
                t = dkv[z, s, sl, :].astype(F32) + fin[s, 0, sl, :].astype(F32) + fin[s, 1, sl, :].astype(F32)
                t = t.astype(BF).astype(F32)
                if s == 0:
                    swapped = pltpu.roll(t, 64, 1)
                    turned = []
                    for a in range(16):
                        rows = slice(a * 8, (a + 1) * 8)
                        c8, s8 = turn(cos, sin, slice(j * 16 + a, j * 16 + a + 1))
                        turned.append(t[rows, :] * c8 - swapped[rows, :] * s8)
                    t = jnp.concatenate(turned, 0)
                own_b[s, j] = t.astype(BF)
                pieces.append(t.reshape(16, 8, HD))
            own_a[s, :, i * 16 : (i + 1) * 16, :] = jnp.concatenate(pieces, 1).astype(BF)
        exchanged[s] = [
            remote(own_a.at[s, dp_of[k]], src.at[s, y, d], ss.at[s, k], rs.at[s, k], on_dp(k)) for k in range(1, 16)
        ]
        for copy in exchanged[s]:
            copy.start()
        packed[s] = [
            remote(own_b.at[s, y_of[k]], pg_rx.at[s, y], ys.at[2 + s, k], yr.at[2 + s, k], on_y(k))
            for k in range(1, 4)
        ]
        for copy in packed[s]:
            copy.start()
        src[s, y, d] = own_a[s, d]
        pg_rx[s, y] = own_b[s, y]

    gathered = {}

    def gather(s):
        for copy in exchanged[s]:
            copy.wait_recv()
        gathered[s] = [
            remote(src.at[s, y], src.at[s, y], ys.at[4 + s, k], yr.at[4 + s, k], on_y(k)) for k in range(1, 4)
        ]
        for copy in gathered[s]:
            copy.start()

    swaps = {0: [], 1: []}
    order = [2, 1, 3, 0]

    swap = lambda s, g: remote(tile.at[s, g, 1 - core], pair.at[s, g], cs.at[s, g], cr.at[s, g], sibling)

    def multiply(s):
        for k in (0, 1, 3, 2):
            if k:
                gathered[s][k - 1].wait_recv()
            g = y_of[(4 - k) % 4]
            rows = src[s, g].reshape(512, HD)
            tile[s, g] = cols_dot(rows, hsr[...]).reshape(2, 64, 1024).astype(BF)
            copy = swap(s, g)
            copy.start()
            swaps[s].append(copy)

    rings = {0: [], 1: []}

    def add_pair(s):
        for k in order:
            g = x_of[k]
            swap(s, g).wait_recv()
            for j in range(4):
                sl = slice(j * 256, (j + 1) * 256)
                mine[s, k, :, sl] = (
                    tile[s, g, core, :, sl].astype(F32) + pair[s, g, :, sl].astype(F32)
                ).astype(BF)
            if k:
                copy = remote(mine.at[s, k], ring.at[s, k], xs.at[s, k], xr.at[s, k], on_x(k))
                copy.start()
                rings[s].append(copy)

    same = lambda s, k: remote(part.at[s, z_of[k]], last.at[k], es.at[k], er.at[k], on_z(s, k))
    other = lambda s, k: remote(part.at[s, z_of[k]], last.at[4 + k], es.at[4 + k], er.at[4 + k], on_z(s, k))

    def add_ring(s):
        for copy in rings[s]:
            copy.wait_recv()
        for j in range(4):
            sl = slice(j * 256, (j + 1) * 256)
            t = mine[s, 0, :, sl].astype(F32)
            for k in range(1, 4):
                t = t + ring[s, k, :, sl].astype(F32)
            part[s, j] = t.astype(BF)

        @pl.when(zl == s)
        def _():
            for k in range(1, 4):
                same(s, k).start()

        @pl.when(zl != s)
        def _():
            for k in range(4):
                other(s, k).start()

    for j in range(4):
        sl = slice(j * 256, (j + 1) * 256)
        pieces = [hs[i, :, sl].astype(F32).reshape(16, 8, 256) for i in range(4)]
        hsr[:, sl] = jnp.concatenate(pieces, 1).reshape(512, 256).astype(BF)
    pass_on(1)
    for copy in far[0] + near[0]:
        copy.start()
    complete(1)
    pass_on(0)
    gather(1)
    for copy in outs:
        copy.wait_recv()
    for g in range(4):
        for source, target in ((att_rx, att_o), (qg_rx, qg_o)):
            block = source[g].reshape(16, 32, HD).astype(F32)
            for h in range(4):
                cols = slice((g * 4 + h) * HD, (g * 4 + h + 1) * HD)
                target[:, cols] = block[:, h * 8 : h * 8 + 8, :].reshape(128, HD).astype(BF)
    complete(0)
    multiply(1)
    gather(0)
    add_pair(1)
    multiply(0)
    add_ring(1)
    for s in (1, 0):
        for copy in packed[s]:
            copy.wait_recv()
        for g in range(4):
            cols = slice(s * 512 + g * HD, s * 512 + (g + 1) * HD)
            pgh[:, cols] = pg_rx[s, g]
    add_pair(0)
    weights.wait()
    for j in range(8):
        sl = slice(j * 512, (j + 1) * 512)
        hg_o[:, sl] = jnp.dot(pgh[...], w[:, sl], preferred_element_type=F32).astype(BF)
    add_ring(0)
    ends = [same(zl, k) for k in range(1, 4)] + [other(1 - zl, k) for k in range(4)]
    for copy in ends:
        copy.wait_recv()
    t = part[zl, z].astype(F32)
    for k in range(1, 8):
        t = t + last[k].astype(F32)
    grad[...] = t * (1.0 / 16.0)
    for s in (0, 1):
        for copy in far[s] + near[s] + sums[s] + exchanged[s] + packed[s] + gathered[s] + swaps[s] + rings[s]:
            copy.wait_send()
    for copy in outs + ends:
        copy.wait_send()


def back(att, qg, dkv, cos, sin, hs, w):
    dma = pltpu.SemaphoreType.DMA
    return pl.pallas_call(
        back_kernel,
        in_specs=[vm()] * 6 + [pl.BlockSpec(memory_space=pltpu.HBM)],
        out_specs=[vm()] * 4,
        out_shape=[
            jax.ShapeDtypeStruct((128, 2048), BF),
            jax.ShapeDtypeStruct((128, 2048), BF),
            jax.ShapeDtypeStruct((128, 4096), BF),
            jax.ShapeDtypeStruct((64, 256), F32),
        ],
        scratch_shapes=[
            pltpu.VMEM((4, 512, HD), BF),
            pltpu.VMEM((4, 512, HD), BF),
            pltpu.VMEM((2, 2, 256, HD), BF),
            pltpu.VMEM((2, 2, 256, HD), BF),
            pltpu.VMEM((2, 2, 512, HD), BF),
            pltpu.VMEM((2, 16, 32, HD), BF),
            pltpu.VMEM((2, 4, 128, HD), BF),
            pltpu.VMEM((2, 4, 16, 32, HD), BF),
            pltpu.VMEM((2, 4, 128, HD), BF),
            pltpu.VMEM((512, 1024), BF),
            pltpu.VMEM((128, 1024), BF),
            pltpu.VMEM((1024, 4096), BF),
            pltpu.VMEM((2, 4, 2, 64, 1024), BF),
            pltpu.VMEM((2, 4, 64, 1024), BF),
            pltpu.VMEM((2, 4, 64, 1024), BF),
            pltpu.VMEM((2, 4, 64, 1024), BF),
            pltpu.VMEM((2, 4, 64, 256), BF),
            pltpu.VMEM((8, 64, 256), BF),
            dma, dma((6, 4)), dma((6, 4)), dma((2, 6)), dma((2, 6)), dma((2, 16)), dma((2, 16)),
            dma((2, 4)), dma((2, 4)), dma((2, 4)), dma((2, 4)), dma((8,)), dma((8,)),
        ],
        compiler_params=pltpu.CompilerParams(collective_id=1, has_side_effects=True, vmem_limit_bytes=48 * MIB),
        name="back",
    )(att, qg, dkv, cos, sin, hs, w)


def store_kernel(a, b, c, e, a_o, b_o, c_o, e_o, sems):
    copies = [pltpu.make_async_copy(p, o, sems.at[i]) for i, (p, o) in enumerate(((a, a_o), (b, b_o), (c, c_o), (e, e_o)))]
    for copy in copies:
        copy.start()
    for copy in copies:
        copy.wait()


def store(*arrays):
    hbm = pl.BlockSpec(memory_space=pltpu.HBM)
    return pl.pallas_call(
        store_kernel,
        in_specs=[vm()] * 4,
        out_specs=[hbm] * 4,
        out_shape=[jax.ShapeDtypeStruct(a.shape, a.dtype) for a in arrays],
        scratch_shapes=[pltpu.SemaphoreType.DMA((4,))],
        compiler_params=pltpu.CompilerParams(vmem_limit_bytes=16 * MIB),
        name="store",
    )(*arrays)


def body(hidden_rows, query_rows, out_grad, projection, packing_plan, document_ids):
    z = lax.axis_index("ctx") // 4
    small = jnp.arange(8, dtype=jnp.int32)
    cos, sin = angle_tables(jnp.concatenate([z * 512 + jnp.arange(64, dtype=jnp.int32) * 8, small]))
    plan_ids = jnp.concatenate([packing_plan, document_ids], axis=1)
    kv_all, q_rx, g_rx, h_rx, first = front(plan_ids, cos, sin, hidden_rows, query_rows, out_grad, projection)
    att, qg, dkv = attend(
        q_rx.reshape(2048, HD), g_rx.reshape(2048, HD), kv_all.reshape(256, 16, HD), first
    )
    return store(*back(att.reshape(4, 512, HD), qg.reshape(4, 512, HD), dkv, cos, sin, h_rx, projection))


def solution(mesh):
    rows = P(("dp", "ctx"), None)
    return jax.shard_map(
        body,
        mesh=mesh,
        in_specs=(rows, rows, rows, P(), rows, P("dp", None)),
        out_specs=(rows, rows, rows, P("dp", "ctx")),
        check_vma=False,
    )
```

```python
import functools
import math

import jax
import jax.numpy as jnp
from jax import lax
from jax.experimental import pallas as pl
from jax.experimental.pallas import tpu as pltpu
from jax.sharding import PartitionSpec as P

ROPE_BASE = 500000.0
MASK_VALUE = -1e30
HD = 128
SCALE = HD ** (-0.5)
BF = jnp.bfloat16
F32 = jnp.float32
MESH = pl.DeviceIdType.MESH
MIB = 1024 * 1024


def vm():
    return pl.BlockSpec(memory_space=pltpu.VMEM)


def rows_dot(a, b):
    return lax.dot_general(a, b, (((1,), (1,)), ((), ())), preferred_element_type=F32)


def cols_dot(a, b):
    return lax.dot_general(a, b, (((0,), (0,)), ((), ())), preferred_element_type=F32)


def angle_tables(positions):
    half = HD // 2
    exponent = jnp.arange(half, dtype=F32) * (-2.0 * math.log(ROPE_BASE) / HD)
    angles = positions.astype(F32)[:, None] * jnp.exp(exponent)[None, :]
    cosine, sine = jnp.cos(angles), jnp.sin(angles)
    return jnp.concatenate([cosine, cosine], 1), jnp.concatenate([-sine, sine], 1)


def turn(cos, sin, rows):
    c, s, c8, s8 = cos[rows, :], sin[rows, :], cos[64:, :], sin[64:, :]
    return c * c8 - s * s8, s * c8 + c * s8


def remote(src, dst, send, recv, device):
    return pltpu.make_async_remote_copy(
        src_ref=src, dst_ref=dst, send_sem=send, recv_sem=recv, device_id=device, device_id_type=MESH
    )


def greet(devices):
    barrier = pltpu.get_barrier_semaphore()
    for device in devices:
        pl.semaphore_signal(barrier, inc=1, device_id=device, device_id_type=MESH)
    pl.semaphore_wait(barrier, len(devices))


def front_kernel(
    plan_ids, cos, sin, x_h, q_h, og_h, w_h, kv_all, q_rx, g_rx, h_rx, lowest,
    x, q, og, w, xp, acc, kv_s, q_s, g_s, h_s, kv1, q1, ls, ss, rs, ys, yr, zs, zr,
):
    d, c = lax.axis_index("dp"), lax.axis_index("ctx")
    z, y = c // 4, c % 4
    dp_of = [(d + k) % 16 for k in range(16)]
    y_of = [(y + k) % 4 for k in range(4)]
    on_dp = lambda k: {"dp": dp_of[k]}
    on_y = lambda k: {"ctx": z * 4 + y_of[k]}
    up, down = {"ctx": (c + 4) % 16}, {"ctx": (c + 12) % 16}
    z_up, z_down = (z + 1) % 4, (z + 3) % 4

    loads = [pltpu.make_async_copy(x_h, x, ls.at[2])]
    loads += [pltpu.make_async_copy(w_h.at[pl.ds(i * 256, 256)], w.at[i], ls.at[3 + i]) for i in range(4)]
    loads += [pltpu.make_async_copy(og_h, og, ls.at[0]), pltpu.make_async_copy(q_h, q, ls.at[1])]
    for copy in loads:
        copy.start()
    partners = [on_dp(k) for k in range(1, 16)] + [on_y(k) for k in range(1, 4)] + [up, down]
    barrier = pltpu.get_barrier_semaphore()
    for device in partners:
        pl.semaphore_signal(barrier, inc=1, device_id=device, device_id_type=MESH)

    pick = (lax.broadcasted_iota(jnp.int32, (128, 128), 0) == plan_ids[:, :128]).astype(F32).astype(BF)
    loads[0].wait()
    for j in range(16):
        sl = slice(j * 256, (j + 1) * 256)
        t = jnp.dot(pick, x[:, sl], preferred_element_type=F32).astype(BF)
        xp[:, sl] = t
        h_s[j % 4, :, (j // 4) * 256 : (j // 4 + 1) * 256] = t
    loads[5].wait()
    for i in range(8):
        grads = [og[:, h * HD : (h + 1) * HD].astype(F32).reshape(16, 8, HD) for h in (2 * i, 2 * i + 1)]
        g_s[i // 2, :, (i % 2) * 16 : (i % 2 + 1) * 16, :] = jnp.concatenate(grads, 1).astype(BF)
    pl.semaphore_wait(barrier, len(partners))
    grads = [remote(g_s.at[y_of[k]], g_rx.at[y], ys.at[0, k], yr.at[0, k], on_y(k)) for k in range(1, 4)]
    for copy in grads:
        copy.start()

    for i in range(4):
        loads[1 + i].wait()
        acc[i] = rows_dot(xp[...], w[i])
    near_cos, near_sin = turn(cos, sin, pl.ds(y * 16 + d, 1))
    for g in range(4):
        sl = slice((g % 2) * HD, (g % 2 + 1) * HD)
        k = acc[g // 2][:, sl]
        v = acc[2 + g // 2][:, sl]
        k3 = k.reshape(16, 8, HD)
        r3 = pltpu.roll(k, 64, 1).reshape(16, 8, HD)
        rot = k3 * near_cos[None] + r3 * near_sin[None]
        kv_s[:, g * 16 : (g + 1) * 16, :] = jnp.concatenate([rot, v.reshape(16, 8, HD)], 1).astype(BF)
    kv_first = [remote(kv_s.at[dp_of[k]], kv1.at[d], ss.at[0, k], rs.at[0, k], on_dp(k)) for k in range(1, 16)]
    for copy in kv_first:
        copy.start()

    loads[6].wait()
    for i in range(8):
        parts = [
            jnp.dot(pick, q[:, h * HD : (h + 1) * HD], preferred_element_type=F32).reshape(16, 8, HD)
            for h in (2 * i, 2 * i + 1)
        ]
        q_s[:, i * 16 : (i + 1) * 16, :] = jnp.concatenate(parts, 1).astype(BF)
    q_first = [remote(q_s.at[dp_of[k]], q1.at[d], ss.at[1, k], rs.at[1, k], on_dp(k)) for k in range(1, 16)]
    for copy in q_first:
        copy.start()
    hidden = [remote(h_s.at[y_of[k]], h_rx.at[y], ys.at[3, k], yr.at[3, k], on_y(k)) for k in (1, 3, 2)]
    hidden[0].start()
    hidden[1].start()
    kv1[d] = kv_s[d]
    q1[d] = q_s[d]
    g_rx[y] = g_s[y]
    h_rx[y] = h_s[y]

    for copy in kv_first:
        copy.wait_recv()
    group = lambda k: pl.ds(pl.multiple_of(y_of[k] * 16, 16), 16)
    kv_second = [
        remote(kv1.at[:, group(k), :], kv_all.at[z, y], ys.at[1, k], yr.at[1, k], on_y(k)) for k in range(1, 4)
    ]
    for copy in kv_second:
        copy.start()
    kv_all[z, y] = kv1[:, group(0), :]

    chunk = [(y + 4 - t) % 4 for t in range(4)]
    own_up, own_down = [], []
    for t in range(4):
        if t:
            kv_second[t - 1].wait_recv()
        place = kv_all.at[z, chunk[t]]
        own_up.append(remote(place, place, zs.at[0, t], zr.at[0, t], up))
        own_down.append(remote(place, place, zs.at[1, t], zr.at[1, t], down))
        own_up[t].start()
        own_down[t].start()

    for copy in q_first:
        copy.wait_recv()
    heads = lambda k: pl.ds(pl.multiple_of(y_of[k] * 32, 32), 32)
    q_second = [remote(q1.at[:, heads(k), :], q_rx.at[y], ys.at[2, k], yr.at[2, k], on_y(k)) for k in range(1, 4)]
    for copy in q_second:
        copy.start()
    hidden[2].start()
    q_rx[y] = q1[:, heads(0), :]

    passed = []
    for t in range(4):
        if t % 2 == 0:
            own_up[t].wait_recv()
            place = kv_all.at[z_down, chunk[t]]
            passed.append(remote(place, place, zs.at[2, t], zr.at[2, t], up))
        else:
            own_down[t].wait_recv()
            place = kv_all.at[z_up, chunk[t]]
            passed.append(remote(place, place, zs.at[2, t], zr.at[2, t], down))
        passed[t].start()
    for t in range(4):
        (own_down if t % 2 == 0 else own_up)[t].wait_recv()
    lane = lax.broadcasted_iota(jnp.int32, (128, 512), 1)
    take = (lax.broadcasted_iota(jnp.int32, (128, 512), 0) == (lane // 32) * 8 + lane % 8).astype(F32).astype(BF)
    ids = plan_ids[:, 128:].astype(F32)
    counts = [jnp.sum((ids < k).astype(F32), axis=1, keepdims=True) for k in range(1, 8)]
    for i in range(4):
        mine = plan_ids[:, pl.ds(pl.multiple_of(z * 512 + (i + 1) * 128, 128), 128)].astype(F32)
        mine = jnp.dot(jnp.broadcast_to(mine, (16, 128)).astype(BF), take, preferred_element_type=F32)[:1]
        begin = jnp.zeros((1, 512), F32)
        for k in range(1, 8):
            begin = jnp.where(mine == k, counts[k - 1], begin)
        lowest[i] = begin.astype(jnp.int32)

    for copy in passed + q_second + grads + hidden:
        copy.wait_recv()
    for copy in kv_first + grads + q_first + kv_second + own_up + own_down + q_second + hidden + passed:
        copy.wait_send()


def front(plan_ids, cos, sin, x, q, og, w):
    hbm = pl.BlockSpec(memory_space=pltpu.HBM)
    return pl.pallas_call(
        front_kernel,
        in_specs=[vm()] * 3 + [hbm] * 4,
        out_specs=[vm()] * 5,
        out_shape=[
            jax.ShapeDtypeStruct((4, 4, 16, 16, HD), BF),
            jax.ShapeDtypeStruct((4, 16, 32, HD), BF),
            jax.ShapeDtypeStruct((4, 16, 32, HD), BF),
            jax.ShapeDtypeStruct((4, 128, 1024), BF),
            jax.ShapeDtypeStruct((4, 1, 512), jnp.int32),
        ],
        scratch_shapes=[
            pltpu.VMEM((128, 4096), BF),
            pltpu.VMEM((128, 2048), BF),
            pltpu.VMEM((128, 2048), BF),
            pltpu.VMEM((4, 256, 4096), BF),
            pltpu.VMEM((128, 4096), BF),
            pltpu.VMEM((4, 128, 256), F32),
            pltpu.VMEM((16, 64, HD), BF),
            pltpu.VMEM((16, 128, HD), BF),
            pltpu.VMEM((4, 16, 32, HD), BF),
            pltpu.VMEM((4, 128, 1024), BF),
            pltpu.VMEM((16, 64, HD), BF),
            pltpu.VMEM((16, 128, HD), BF),
            pltpu.SemaphoreType.DMA((7,)),
            pltpu.SemaphoreType.DMA((2, 16)),
            pltpu.SemaphoreType.DMA((2, 16)),
            pltpu.SemaphoreType.DMA((4, 4)),
            pltpu.SemaphoreType.DMA((4, 4)),
            pltpu.SemaphoreType.DMA((3, 4)),
            pltpu.SemaphoreType.DMA((3, 4)),
        ],
        compiler_params=pltpu.CompilerParams(collective_id=0, has_side_effects=True, vmem_limit_bytes=49 * MIB),
        name="front",
    )(plan_ids, cos, sin, x, q, og, w)


def attend_kernel(q, og, kv, first, att, qg, dkv, keys, vals, keys_t, vals_t, dk, dv, sc, gp, q_t, og_t, out_t, grad_t, tops):
    base = (lax.axis_index("ctx") // 4) * 512
    for i in range(4):
        block = kv[pl.ds(i * 64, 64)].astype(F32)
        rows = slice(i * 512, (i + 1) * 512)
        k = block[:, :8, :].reshape(512, HD)
        v = block[:, 8:, :].reshape(512, HD)
        keys[rows, :] = k.astype(BF)
        vals[rows, :] = v.astype(BF)
        keys_t[:, rows] = k.T.astype(BF)
        vals_t[:, rows] = v.T.astype(BF)
    keys[2048:, :] = jnp.zeros((128, HD), BF)
    vals[2048:, :] = jnp.zeros((128, HD), BF)
    keys_t[:, 2048:] = jnp.zeros((HD, 128), BF)
    vals_t[:, 2048:] = jnp.zeros((HD, 128), BF)
    dk[...] = jnp.zeros_like(dk)
    dv[...] = jnp.zeros_like(dv)
    fold = SCALE * math.log2(math.e)

    def query_block(qb, carry):
        here = pl.ds(pl.multiple_of(qb * 512, 512), 512)
        q_t[...] = q[here, :].astype(F32).T.astype(BF)
        og_t[...] = og[here, :].astype(F32).T.astype(BF)
        lowest = first[qb]
        start = (jnp.min(lowest) // 128) * 128
        span = base + (qb + 1) * 128 - start
        blocks = []
        for size in (1024, 512, 256, 128):
            count = (span + 128) // size if size == 512 else span // size
            blocks.append((size, count))
            span = jnp.maximum(span - size * count, 0)

        def sweep(part, carry):
            first_row = start
            for size, count in blocks:
                carry = lax.fori_loop(0, count, functools.partial(part, size, first_row), carry)
                first_row = first_row + size * count
            return carry

        lane = lax.broadcasted_iota(jnp.int32, (1, 512), 1)
        position = base + qb * 128 + (lane // 32) * 8 + lane % 8
        out_t[...] = jnp.zeros_like(out_t)
        grad_t[...] = jnp.zeros_like(grad_t)

        def eights(t):
            return t.reshape(t.shape[0] // 8, 8, 512)

        def scores(size, at, i, sums):
            at = pl.multiple_of(at + i * size, 128)
            rows = pl.ds(at, size)
            s = jnp.dot(keys[rows, :], q_t[...], preferred_element_type=F32)
            grad = jnp.dot(vals[rows, :], og_t[...], preferred_element_type=F32)
            gp[rows, :] = grad
            index = at + lax.broadcasted_iota(jnp.int32, (size, 512), 0)
            s = jnp.where((index <= position) & (index >= lowest), s, MASK_VALUE)
            top, total, product = sums
            high = jnp.maximum(top, jnp.max(jnp.max(eights(s), axis=0), axis=0, keepdims=True) * fold)
            e = jnp.exp2(s * fold - high)
            sc[rows, :] = e
            tops[at // 128] = high
            shrink = jnp.exp2(top - high)
            return (
                high,
                total * shrink + jnp.sum(eights(e), axis=0),
                product * shrink + jnp.sum(eights(e * grad), axis=0),
            )

        zero = jnp.zeros((8, 512), F32)
        top, total, product = sweep(scores, (jnp.full((1, 512), MASK_VALUE, F32), zero, zero))
        inverse = 1.0 / jnp.sum(total, axis=0, keepdims=True)
        delta = jnp.sum(product, axis=0, keepdims=True) * inverse

        def both(size, at, i, c):
            at = pl.multiple_of(at + i * size, 128)
            rows = pl.ds(at, size)
            p = sc[rows, :] * (jnp.exp2(tops[at // 128] - top) * inverse)
            rounded = p.astype(BF)
            ds = (p * (gp[rows, :] - delta)).astype(BF)
            dv[rows, :] += jnp.dot(rounded, og[here, :], preferred_element_type=F32)
            dk[rows, :] += jnp.dot(ds, q[here, :], preferred_element_type=F32)
            out_t[...] += jnp.dot(vals_t[:, rows], rounded, preferred_element_type=F32)
            grad_t[...] += jnp.dot(keys_t[:, rows], ds, preferred_element_type=F32)
            return c

        sweep(both, 0)
        att[here, :] = out_t[...].T.astype(BF)
        qg[here, :] = (grad_t[...] * SCALE).T.astype(BF)
        return carry

    lax.fori_loop(0, 4, query_block, 0)
    for i in range(4):
        rows = slice(i * 512, (i + 1) * 512)
        dkv[i, 0] = (dk[rows, :] * SCALE).astype(BF)
        dkv[i, 1] = dv[rows, :].astype(BF)


def attend(q, og, kv, first):
    return pl.pallas_call(
        attend_kernel,
        in_specs=[vm()] * 4,
        out_specs=[vm()] * 3,
        scratch_shapes=[
            pltpu.VMEM((2176, HD), BF),
            pltpu.VMEM((2176, HD), BF),
            pltpu.VMEM((HD, 2176), BF),
            pltpu.VMEM((HD, 2176), BF),
            pltpu.VMEM((2176, HD), F32),
            pltpu.VMEM((2176, HD), F32),
            pltpu.VMEM((2176, 512), F32),
            pltpu.VMEM((2176, 512), F32),
            pltpu.VMEM((HD, 512), BF),
            pltpu.VMEM((HD, 512), BF),
            pltpu.VMEM((HD, 512), F32),
            pltpu.VMEM((HD, 512), F32),
            pltpu.VMEM((17, 1, 512), F32),
        ],
        out_shape=[
            jax.ShapeDtypeStruct((2048, HD), BF),
            jax.ShapeDtypeStruct((2048, HD), BF),
            jax.ShapeDtypeStruct((4, 2, 512, HD), BF),
        ],
        compiler_params=pltpu.CompilerParams(vmem_limit_bytes=48 * MIB),
        name="attend",
    )(q, og, kv, first)


def back_kernel(
    att, qg, dkv, cos, sin, hs, w_h, att_o, qg_o, hg_o, grad,
    att_rx, qg_rx, hop, mid, fin, own_a, own_b, src, pg_rx, hsr, pgh, w, tile, pair, mine, ring, part, last,
    ws, ys, yr, zs, zr, ss, rs, cs, cr, xs, xr, es, er,
):
    d, c = lax.axis_index("dp"), lax.axis_index("ctx")
    z, y = c // 4, c % 4
    zl, x, core = d // 8, (d // 2) % 4, d % 2
    dp_of = [(d + k) % 16 for k in range(16)]
    y_of = [(y + k) % 4 for k in range(4)]
    x_of = [(x + k) % 4 for k in range(4)]
    z_of = [(z + k) % 4 for k in range(4)]
    on_dp = lambda k: {"dp": dp_of[k]}
    on_y = lambda k: {"ctx": z * 4 + y_of[k]}
    on_x = lambda k: {"dp": zl * 8 + x_of[k] * 2 + core}
    on_z = lambda lo, k: {"dp": lo * 8 + x * 2 + core, "ctx": z_of[k] * 4 + y}
    sibling = {"dp": d + 1 - 2 * core}
    up, down = {"ctx": (c + 4) % 16}, {"ctx": (c + 12) % 16}
    z_up, z_far, z_down = z_of[1], z_of[2], z_of[3]
    low, high = pl.ds(0, 256), pl.ds(256, 256)

    weights = pltpu.make_async_copy(w_h, w, ws)
    weights.start()
    greet(
        [on_dp(k) for k in range(1, 16)]
        + [on_y(k) for k in range(1, 4)]
        + [on_z(zl, k) for k in range(1, 4)]
        + [on_z(1 - zl, k) for k in range(1, 4)]
    )

    far, near = {}, {}
    for s in (1, 0):
        far[s] = [
            remote(dkv.at[z_far, s, low], hop.at[s, 0], zs.at[s, 0], zr.at[s, 0], down),
            remote(dkv.at[z_far, s, high], hop.at[s, 1], zs.at[s, 1], zr.at[s, 1], up),
        ]
        near[s] = [
            remote(dkv.at[z_down, s, high], fin.at[s, 0, high], zs.at[s, 2], zr.at[s, 2], down),
            remote(dkv.at[z_up, s, low], fin.at[s, 0, low], zs.at[s, 3], zr.at[s, 3], up),
        ]
    for copy in far[1] + near[1]:
        copy.start()
    outs = []
    for i, (a, b) in enumerate(((att, att_rx), (qg, qg_rx))):
        for k in range(1, 4):
            outs.append(remote(a.at[y_of[k]], b.at[y], ys.at[i, k], yr.at[i, k], on_y(k)))
            outs[-1].start()
        b[y] = a[y]

    sums = {}

    def pass_on(s):
        far[s][0].wait_recv()
        mid[s, 0] = (hop[s, 0].astype(F32) + dkv[z_down, s, 0:256, :].astype(F32)).astype(BF)
        first = remote(mid.at[s, 0], fin.at[s, 1, low], zs.at[s, 4], zr.at[s, 4], down)
        first.start()
        far[s][1].wait_recv()
        mid[s, 1] = (hop[s, 1].astype(F32) + dkv[z_up, s, 256:512, :].astype(F32)).astype(BF)
        second = remote(mid.at[s, 1], fin.at[s, 1, high], zs.at[s, 5], zr.at[s, 5], up)
        second.start()
        sums[s] = [first, second]

    exchanged, packed = {}, {}

    def complete(s):
        for copy in near[s] + sums[s]:
            copy.wait_recv()
        for i in range(2):
            pieces = []
            for j in (2 * i, 2 * i + 1):
                sl = slice(j * 128, (j + 1) * 128)
                t = dkv[z, s, sl, :].astype(F32) + fin[s, 0, sl, :].astype(F32) + fin[s, 1, sl, :].astype(F32)
                t = t.astype(BF).astype(F32)
                if s == 0:
                    swapped = pltpu.roll(t, 64, 1)
                    turned = []
                    for a in range(16):
                        rows = slice(a * 8, (a + 1) * 8)
                        c8, s8 = turn(cos, sin, slice(j * 16 + a, j * 16 + a + 1))
                        turned.append(t[rows, :] * c8 - swapped[rows, :] * s8)
                    t = jnp.concatenate(turned, 0)
                own_b[s, j] = t.astype(BF)
                pieces.append(t.reshape(16, 8, HD))
            own_a[s, :, i * 16 : (i + 1) * 16, :] = jnp.concatenate(pieces, 1).astype(BF)
        exchanged[s] = [
            remote(own_a.at[s, dp_of[k]], src.at[s, y, d], ss.at[s, k], rs.at[s, k], on_dp(k)) for k in range(1, 16)
        ]
        for copy in exchanged[s]:
            copy.start()
        packed[s] = [
            remote(own_b.at[s, y_of[k]], pg_rx.at[s, y], ys.at[2 + s, k], yr.at[2 + s, k], on_y(k))
            for k in range(1, 4)
        ]
        for copy in packed[s]:
            copy.start()
        src[s, y, d] = own_a[s, d]
        pg_rx[s, y] = own_b[s, y]

    gathered = {}

    def gather(s):
        for copy in exchanged[s]:
            copy.wait_recv()
        gathered[s] = [
            remote(src.at[s, y], src.at[s, y], ys.at[4 + s, k], yr.at[4 + s, k], on_y(k)) for k in range(1, 4)
        ]
        for copy in gathered[s]:
            copy.start()

    swaps = {0: [], 1: []}
    order = [2, 1, 3, 0]

    swap = lambda s, g: remote(tile.at[s, g, 1 - core], pair.at[s, g], cs.at[s, g], cr.at[s, g], sibling)

    def multiply(s):
        for k in (0, 1, 3, 2):
            if k:
                gathered[s][k - 1].wait_recv()
            g = y_of[(4 - k) % 4]
            rows = src[s, g].reshape(512, HD)
            tile[s, g] = cols_dot(rows, hsr[...]).reshape(2, 64, 1024).astype(BF)
            copy = swap(s, g)
            copy.start()
            swaps[s].append(copy)

    rings = {0: [], 1: []}

    def add_pair(s):
        for k in order:
            g = x_of[k]
            swap(s, g).wait_recv()
            for j in range(4):
                sl = slice(j * 256, (j + 1) * 256)
                mine[s, k, :, sl] = (
                    tile[s, g, core, :, sl].astype(F32) + pair[s, g, :, sl].astype(F32)
                ).astype(BF)
            if k:
                copy = remote(mine.at[s, k], ring.at[s, k], xs.at[s, k], xr.at[s, k], on_x(k))
                copy.start()
                rings[s].append(copy)

    same = lambda s, k: remote(part.at[s, z_of[k]], last.at[k], es.at[k], er.at[k], on_z(s, k))
    other = lambda s, k: remote(part.at[s, z_of[k]], last.at[4 + k], es.at[4 + k], er.at[4 + k], on_z(s, k))

    def add_ring(s):
        for copy in rings[s]:
            copy.wait_recv()
        for j in range(4):
            sl = slice(j * 256, (j + 1) * 256)
            t = mine[s, 0, :, sl].astype(F32)
            for k in range(1, 4):
                t = t + ring[s, k, :, sl].astype(F32)
            part[s, j] = t.astype(BF)

        @pl.when(zl == s)
        def _():
            for k in range(1, 4):
                same(s, k).start()

        @pl.when(zl != s)
        def _():
            for k in range(4):
                other(s, k).start()

    for j in range(4):
        sl = slice(j * 256, (j + 1) * 256)
        pieces = [hs[i, :, sl].astype(F32).reshape(16, 8, 256) for i in range(4)]
        hsr[:, sl] = jnp.concatenate(pieces, 1).reshape(512, 256).astype(BF)
    pass_on(1)
    for copy in far[0] + near[0]:
        copy.start()
    complete(1)
    pass_on(0)
    gather(1)
    for copy in outs:
        copy.wait_recv()
    for g in range(4):
        for source, target in ((att_rx, att_o), (qg_rx, qg_o)):
            block = source[g].reshape(16, 32, HD).astype(F32)
            for h in range(4):
                cols = slice((g * 4 + h) * HD, (g * 4 + h + 1) * HD)
                target[:, cols] = block[:, h * 8 : h * 8 + 8, :].reshape(128, HD).astype(BF)
    complete(0)
    multiply(1)
    gather(0)
    add_pair(1)
    multiply(0)
    add_ring(1)
    for s in (1, 0):
        for copy in packed[s]:
            copy.wait_recv()
        for g in range(4):
            cols = slice(s * 512 + g * HD, s * 512 + (g + 1) * HD)
            pgh[:, cols] = pg_rx[s, g]
    add_pair(0)
    weights.wait()
    for j in range(8):
        sl = slice(j * 512, (j + 1) * 512)
        hg_o[:, sl] = jnp.dot(pgh[...], w[:, sl], preferred_element_type=F32).astype(BF)
    add_ring(0)
    ends = [same(zl, k) for k in range(1, 4)] + [other(1 - zl, k) for k in range(4)]
    for copy in ends:
        copy.wait_recv()
    t = part[zl, z].astype(F32)
    for k in range(1, 8):
        t = t + last[k].astype(F32)
    grad[...] = t * (1.0 / 16.0)
    for s in (0, 1):
        for copy in far[s] + near[s] + sums[s] + exchanged[s] + packed[s] + gathered[s] + swaps[s] + rings[s]:
            copy.wait_send()
    for copy in outs + ends:
        copy.wait_send()


def back(att, qg, dkv, cos, sin, hs, w):
    dma = pltpu.SemaphoreType.DMA
    return pl.pallas_call(
        back_kernel,
        in_specs=[vm()] * 6 + [pl.BlockSpec(memory_space=pltpu.HBM)],
        out_specs=[vm()] * 4,
        out_shape=[
            jax.ShapeDtypeStruct((128, 2048), BF),
            jax.ShapeDtypeStruct((128, 2048), BF),
            jax.ShapeDtypeStruct((128, 4096), BF),
            jax.ShapeDtypeStruct((64, 256), F32),
        ],
        scratch_shapes=[
            pltpu.VMEM((4, 512, HD), BF),
            pltpu.VMEM((4, 512, HD), BF),
            pltpu.VMEM((2, 2, 256, HD), BF),
            pltpu.VMEM((2, 2, 256, HD), BF),
            pltpu.VMEM((2, 2, 512, HD), BF),
            pltpu.VMEM((2, 16, 32, HD), BF),
            pltpu.VMEM((2, 4, 128, HD), BF),
            pltpu.VMEM((2, 4, 16, 32, HD), BF),
            pltpu.VMEM((2, 4, 128, HD), BF),
            pltpu.VMEM((512, 1024), BF),
            pltpu.VMEM((128, 1024), BF),
            pltpu.VMEM((1024, 4096), BF),
            pltpu.VMEM((2, 4, 2, 64, 1024), BF),
            pltpu.VMEM((2, 4, 64, 1024), BF),
            pltpu.VMEM((2, 4, 64, 1024), BF),
            pltpu.VMEM((2, 4, 64, 1024), BF),
            pltpu.VMEM((2, 4, 64, 256), BF),
            pltpu.VMEM((8, 64, 256), BF),
            dma, dma((6, 4)), dma((6, 4)), dma((2, 6)), dma((2, 6)), dma((2, 16)), dma((2, 16)),
            dma((2, 4)), dma((2, 4)), dma((2, 4)), dma((2, 4)), dma((8,)), dma((8,)),
        ],
        compiler_params=pltpu.CompilerParams(collective_id=1, has_side_effects=True, vmem_limit_bytes=48 * MIB),
        name="back",
    )(att, qg, dkv, cos, sin, hs, w)


def store_kernel(a, b, c, e, a_o, b_o, c_o, e_o, sems):
    copies = [pltpu.make_async_copy(p, o, sems.at[i]) for i, (p, o) in enumerate(((a, a_o), (b, b_o), (c, c_o), (e, e_o)))]
    for copy in copies:
        copy.start()
    for copy in copies:
        copy.wait()


def store(*arrays):
    hbm = pl.BlockSpec(memory_space=pltpu.HBM)
    return pl.pallas_call(
        store_kernel,
        in_specs=[vm()] * 4,
        out_specs=[hbm] * 4,
        out_shape=[jax.ShapeDtypeStruct(a.shape, a.dtype) for a in arrays],
        scratch_shapes=[pltpu.SemaphoreType.DMA((4,))],
        compiler_params=pltpu.CompilerParams(vmem_limit_bytes=16 * MIB),
        name="store",
    )(*arrays)


def body(hidden_rows, query_rows, out_grad, projection, packing_plan, document_ids):
    z = lax.axis_index("ctx") // 4
    small = jnp.arange(8, dtype=jnp.int32)
    cos, sin = angle_tables(jnp.concatenate([z * 512 + jnp.arange(64, dtype=jnp.int32) * 8, small]))
    hidden_rows, query_rows, out_grad = [
        pltpu.with_memory_space_constraint(a, pltpu.HBM) for a in (hidden_rows, query_rows, out_grad)
    ]
    plan_ids = jnp.concatenate([packing_plan, document_ids], axis=1)
    kv_all, q_rx, g_rx, h_rx, first = front(plan_ids, cos, sin, hidden_rows, query_rows, out_grad, projection)
    att, qg, dkv = attend(
        q_rx.reshape(2048, HD), g_rx.reshape(2048, HD), kv_all.reshape(256, 16, HD), first
    )
    return store(*back(att.reshape(4, 512, HD), qg.reshape(4, 512, HD), dkv, cos, sin, h_rx, projection))


def solution(mesh):
    rows = P(("dp", "ctx"), None)
    return jax.shard_map(
        body,
        mesh=mesh,
        in_specs=(rows, rows, rows, P(), rows, P("dp", None)),
        out_specs=(rows, rows, rows, P("dp", "ctx")),
        check_vma=False,
    )
```
